32 devices in a mesh: dom: 8 (over z, x), face: 4 (over y, core).
Axes of the slice: x: 2, y: 2, z: 4, core: 2. Of those that a mesh axis runs over, the one named last changes fastest.
Arguments:
- start: float32 [64, 4096], P(None, ('dom', 'face')), may hold values from -6 to 6
- rhs: float32 [64, 4096], P(None, ('dom', 'face')), may hold values from -6 to 6
- diag_block: bfloat16 [64, 64, 4096], P(None, None, ('dom', 'face'))
- precond: bfloat16 [64, 64, 4096], P(None, None, ('dom', 'face'))
- lift: float32 [6, 16, 64], replicated, may hold values from -0.625 to 0.625
- neighbour: int32 [6, 4096], P(None, ('dom', 'face')), may hold values from 0 to 831, as said below
- orient: int32 [6, 4096], P(None, ('dom', 'face')), may hold values from 0 to 7
- owner: int32 [4096], P(('dom', 'face')), may hold values from 0 to 7, as said below
- slot: int32 [4096], P(('dom', 'face')), may hold values from 0 to 63
Outputs:
- solution: float32 [64, 4096], P(None, ('dom', 'face'))
- coarse_op: float32 [729, 2048], P(None, ('dom', 'face'))
- coarse_rhs: float32 [27, 2048], P(None, ('dom', 'face'))
The draws below stay inside these ranges and needn't reach their ends.
Inputs may be any that keep to these rules, and one draw needn't show every extreme that they name: neighbour of face 2 of local element e < 32 is 768 + e; of face 3 of local element 128 - 32 + j it is 800 + j; every other face f points to a face-(f xor 1) trace of a local element, below 768. Local elements 0 .. 31 of a device are owned by its own dom index, all others by another dom index; from the elements of one device at most 28 go to one owner, and some owner receives exactly 28 from each device.
All inputs are finite; a program needn't handle non-finite values.
Results may differ from the reference program's by a relative error of at most 0.0029.
Values may be sent and summed in bfloat16 or wider, within the bound.
No kernel may reach another device: no remote copies, remote signals or barrier semaphores. Data moves between devices by JAX's collectives and lax.ppermute only.
A program may use at most 64 MiB of HBM per device.

```python
import jax
import jax.numpy as jnp
import numpy as np
from jax import lax

NODES = 64
FACE_NODES = 16
SWEEPS = 2
E_DEV = 128
STAYING = 32
BOUNDARY = 32
AGG_DEV = 64
OWNER_RANKS = 8
SLABS = 4
CAPACITY = 28
ELEMENTS = 4096
AGGREGATES = 2048


def block_draw(key, diag_lo, diag_hi, spread):
    first, second = jax.random.split(key)
    offdiag = spread * jax.random.normal(first, (64, 64, ELEMENTS), jnp.float32)
    diagonal = jax.random.uniform(second, (64, ELEMENTS), jnp.float32, diag_lo, diag_hi)
    identity = jnp.eye(64, dtype=jnp.float32)[:, :, None]
    return offdiag * (1.0 - identity) + identity * diagonal[:, None, :]


def draw_diag_block(key, part):
    return block_draw(key, 3.0, 5.0, 0.15).astype(jnp.bfloat16)


def draw_precond(key, part):
    return block_draw(key, 0.15, 0.3, 0.02).astype(jnp.bfloat16)


def draw_neighbour(key, part):
    element = jnp.arange(ELEMENTS, dtype=jnp.int32)
    local_pos = element % E_DEV
    rows_out = []
    for direction in range(6):
        random_elem = jax.random.randint(jax.random.fold_in(key, direction), (ELEMENTS,), 0, E_DEV)
        chosen = (direction ^ 1) * E_DEV + random_elem
        if direction == 2:
            chosen = jnp.where(local_pos < BOUNDARY, 6 * E_DEV + local_pos, chosen)
        if direction == 3:
            chosen = jnp.where(local_pos >= E_DEV - BOUNDARY, 6 * E_DEV + BOUNDARY + local_pos - (E_DEV - BOUNDARY), chosen)
        rows_out.append(chosen)
    return jnp.stack(rows_out).astype(jnp.int32)


def routing(key):
    root_key = jax.random.fold_in(key, 77)
    jitter_key, extra_key, pinned_key, placement_key = jax.random.split(root_key, 4)
    devices = OWNER_RANKS * SLABS
    dom_of = jnp.arange(devices, dtype=jnp.int32) // SLABS
    cells = (OWNER_RANKS - 1) * CAPACITY
    movers = E_DEV - STAYING
    jitter_values = jax.random.randint(jitter_key, (devices, cells), 0, 65536)
    favoured_owners = jax.random.randint(extra_key, (OWNER_RANKS,), 0, 4)
    pinned_owner = jax.random.randint(pinned_key, (devices,), 1, OWNER_RANKS)
    cell_numbers = jnp.arange(cells, dtype=jnp.int32)
    shift_amount = cell_numbers // CAPACITY + 1
    destination = (dom_of[:, None] + shift_amount[None, :]) % OWNER_RANKS
    extra_score = favoured_owners[destination] + 8 * (shift_amount[None, :] == pinned_owner[:, None]).astype(jnp.int32)
    ranking_score = (extra_score * 65536 + jitter_values) * 1024 + cell_numbers[None, :]
    unused, picked = lax.top_k(ranking_score, movers)
    moving_dest = (dom_of[:, None] + picked // CAPACITY + 1) % OWNER_RANKS
    staying_dest = jnp.broadcast_to(dom_of[:, None], (devices, STAYING))
    owners_all = jnp.concatenate([staying_dest, moving_dest], 1).reshape(-1).astype(jnp.int32)
    slots_all = jax.random.randint(placement_key, (devices, E_DEV), 0, AGG_DEV)
    position = jnp.arange(E_DEV, dtype=jnp.int32)[None, :]
    slots_all = jnp.where(position == 0, 0, slots_all)
    slots_all = jnp.where(position == E_DEV - 1, AGG_DEV - 1, slots_all)
    return (owners_all, slots_all.reshape(-1).astype(jnp.int32))


def draw_owner(key, part):
    return routing(key)[0]


def draw_slot(key, part):
    return routing(key)[1]


def plant(result, own_key, smallest, top_value):
    shape = result.shape
    place = [jax.random.randint(jax.random.fold_in(own_key, axis), (), 0, shape[axis]) for axis in range(len(shape))]
    result = result.at[tuple(place)].set(smallest)
    longest = shape.index(max(shape))
    place[longest] = (place[longest] + 1) % shape[longest]
    return result.at[tuple(place)].set(top_value)


def level_of(own_key, shape, shards, smallest, high):
    def one(dim, shards_of):
        steps = jax.random.uniform(jax.random.fold_in(jax.random.fold_in(own_key, 6), dim), (shards_of,), jnp.float32, smallest / len(shards), high / len(shards))
        return jnp.repeat(jnp.exp(steps), shape[dim] // shards_of).reshape((-1,) + (1,) * (len(shape) - dim - 1))

    loudness = one(*shards[0])
    for cut in shards[1:]:
        loudness = loudness * one(*cut)
    return loudness


def noise(stream_key, shape, scale, reach, cuts=(), kind=jnp.bfloat16):
    values = jax.random.normal(stream_key, shape, jnp.float32) * scale
    if len(cuts) > 0:
        values = level_of(stream_key, shape, cuts, -0.22, 0.18) * values
    return jnp.clip(values, min=-reach, max=reach).astype(kind)


def setup_inputs(seed: int = 0) -> dict:
    splits = jax.random.split(jax.random.key(seed), 10)
    start = noise(splits[0], (NODES, ELEMENTS), 1.0, 6.0, ((1, 32),), jnp.float32)
    rhs = noise(splits[1], (NODES, ELEMENTS), 1.0, 6.0, ((1, 32),), jnp.float32)
    diag_block = draw_diag_block(jax.random.fold_in(splits[9], 71), 0)
    precond = draw_precond(jax.random.fold_in(splits[9], 71), 0)
    lift = noise(splits[4], (6, FACE_NODES, NODES), 96 ** -0.5, 0.625, (), jnp.float32)
    neighbour = draw_neighbour(jax.random.fold_in(splits[9], 71), 0)
    orient = plant(jax.random.randint(splits[6], (6, ELEMENTS), 0, 8), jax.random.fold_in(splits[6], 1), 0, 7).astype(jnp.int32)
    owner = draw_owner(jax.random.fold_in(splits[9], 71), 0)
    slot = draw_slot(jax.random.fold_in(splits[9], 71), 0)
    return dict(start=start, rhs=rhs, diag_block=diag_block, precond=precond, lift=lift, neighbour=neighbour, orient=orient, owner=owner, slot=slot)


def turn_table():
    square = np.arange(16).reshape(4, 4)
    tables = []
    for turn in range(8):
        layout = square.T if turn & 4 else square
        if turn & 1:
            layout = layout[::-1, :]
        if turn & 2:
            layout = layout[:, ::-1]
        tables.append(layout.reshape(16))
    return np.stack(tables)

def restrict_table():
    fine_nodes = np.array([-1.0, -1.0 / np.sqrt(5.0), 1.0 / np.sqrt(5.0), 1.0])
    coarse_nodes = np.array([-1.0, 0.0, 1.0])
    basis = np.ones((4, 3))
    for column in range(3):
        for other in range(3):
            if other != column:
                basis[:, column] *= (fine_nodes - coarse_nodes[other]) / (coarse_nodes[column] - coarse_nodes[other])
    prolong = (basis[:, None, None, :, None, None] * basis[None, :, None, None, :, None] * basis[None, None, :, None, None, :]).reshape(64, 27)
    return prolong.T.astype(np.float32)

def face_traces(values):
    cube = values.reshape(4, 4, 4, -1)
    planes = [cube[0], cube[3], cube[:, 0], cube[:, 3], cube[:, :, 0], cube[:, :, 3]]
    return jnp.stack([plane.reshape(16, -1) for plane in planes])

def couple(face_vals, low_in, high_in, neighbour, orient, lift):
    local_count = face_vals.shape[2]
    pool = jnp.concatenate([face_vals.transpose(1, 0, 2).reshape(16, 6 * local_count), low_in, high_in], 1)
    picked = jnp.take(pool, neighbour.reshape(-1), axis=1).reshape(16, 6, local_count)
    tables = turn_table()
    turned = jnp.zeros_like(picked)
    for turn in range(8):
        turned = turned + jnp.where(orient[None, :, :] == turn, picked[tables[turn]], 0.0)
    return jnp.einsum('kfn,fke->ne', lift, turned, precision=lax.Precision.HIGHEST)

def galerkin(blocks, rtab):
    half = jnp.einsum('cn,nms->cms', rtab, blocks, precision=lax.Precision.HIGHEST)
    return jnp.einsum('cms,dm->cds', half, rtab, precision=lax.Precision.HIGHEST)

def reference(start, rhs, diag_block, precond, lift, neighbour, orient, owner, slot):
    devices = OWNER_RANKS * SLABS
    indices = jnp.arange(devices, dtype=jnp.int32)

    def cut(array, index):
        return lax.dynamic_slice_in_dim(array, index * E_DEV, E_DEV, axis=array.ndim - 1)

    def to_global(stacked):
        return stacked.transpose(1, 0, 2).reshape(stacked.shape[1], ELEMENTS)

    def all_residuals(values):

        def rim_of(index):
            face_vals = face_traces(cut(values, index))
            return jnp.concatenate([face_vals[2][:, :BOUNDARY], face_vals[3][:, E_DEV - BOUNDARY:]], 1)
        rims = lax.map(rim_of, indices).reshape(OWNER_RANKS, SLABS, 16, 2 * BOUNDARY)
        blank = jnp.zeros((OWNER_RANKS, 1, 16, BOUNDARY), jnp.float32)
        from_below = jnp.concatenate([blank, rims[:, :-1, :, BOUNDARY:]], 1).reshape(devices, 16, BOUNDARY)
        from_above = jnp.concatenate([rims[:, 1:, :, :BOUNDARY], blank], 1).reshape(devices, 16, BOUNDARY)

        def one_device(inputs):
            index, low_in, high_in = inputs
            local_vals = cut(values, index)
            face_vals = face_traces(local_vals)
            product = jnp.einsum('nme,me->ne', cut(diag_block, index).astype(jnp.float32), local_vals, precision=lax.Precision.HIGHEST)
            coupled = couple(face_vals, low_in, high_in, cut(neighbour, index), cut(orient, index), lift)
            return cut(rhs, index) - (product - coupled)
        return to_global(lax.map(one_device, (indices, from_below, from_above)))
    solution = start
    for sweep_idx in range(SWEEPS):
        resid = all_residuals(solution)

        def smooth(index):
            return jnp.einsum('nme,me->ne', cut(precond, index).astype(jnp.float32), cut(resid, index), precision=lax.Precision.HIGHEST)
        solution = solution + to_global(lax.map(smooth, indices))
    resid = all_residuals(solution)
    resid_low = lax.optimization_barrier(resid.astype(jnp.bfloat16))
    rtab = jnp.asarray(restrict_table(), dtype=jnp.float32)

    def coarse_of(index):
        return galerkin(cut(diag_block, index).astype(jnp.float32), rtab).reshape(729, E_DEV)
    element_coarse = to_global(lax.map(coarse_of, indices))
    element_rhs = jnp.einsum('cn,ne->ce', rtab, resid_low.astype(jnp.float32), precision=lax.Precision.HIGHEST)
    element = jnp.arange(ELEMENTS, dtype=jnp.int32)
    slab_index = element // E_DEV % SLABS
    target = (owner * SLABS + slab_index) * AGG_DEV + slot
    coarse_op = jnp.zeros((729, AGGREGATES), jnp.float32).at[:, target].add(element_coarse)
    coarse_rhs = jnp.zeros((27, AGGREGATES), jnp.float32).at[:, target].add(element_rhs)
    return (solution, coarse_op, coarse_rhs)
```

```python
import jax
import jax.numpy as jnp
import numpy as np
from jax import lax
from jax.experimental import pallas as pl
from jax.experimental.pallas import tpu as pltpu
from jax.sharding import PartitionSpec as P

SWEEPS = 2
NODES = 64
COARSE = 27
FACES = 6
GROUP = 4
F32 = jnp.float32
BF16 = jnp.bfloat16
VMEM_LIMIT = 24 * 1024 * 1024

NN = (((1,), (0,)), ((), ()))
NT = (((1,), (1,)), ((), ()))
TN = (((0,), (0,)), ((), ()))


def restrict_line():
    fine = np.array([-1.0, -1.0 / np.sqrt(5.0), 1.0 / np.sqrt(5.0), 1.0])
    coarse = np.array([-1.0, 0.0, 1.0])
    basis = np.ones((4, 3))
    for column in range(3):
        for other in range(3):
            if other != column:
                basis[:, column] *= (fine - coarse[other]) / (coarse[column] - coarse[other])
    return basis.T


def restrict_table():
    line = restrict_line()
    return np.kron(np.kron(line, line), line)


def split_table(table):
    table = table.astype(np.float32)
    high = table.astype(BF16)
    low = (table - high.astype(np.float32)).astype(BF16)
    return high, low


def ceil_to(value, step):
    return -(-value // step) * step


def halves(values):
    high = values.astype(BF16)
    low = (values - high.astype(F32)).astype(BF16)
    return high, low


def dot(left, right, dims):
    return lax.dot_general(left, right, dims, preferred_element_type=F32)


def dot_split(left, right, dims):
    left_high, left_low = left
    right_high, right_low = right
    return (
        dot(left_high, right_high, dims)
        + dot(left_low, right_high, dims)
        + dot(left_high, right_low, dims)
    )


def lanes(shape):
    return lax.broadcasted_iota(jnp.int32, shape, 1)


def rows(shape):
    return lax.broadcasted_iota(jnp.int32, shape, 0)


def face_traces(ref):
    return [
        ref[0:16],
        ref[48:64],
        jnp.concatenate([ref[16 * i : 16 * i + 4] for i in range(4)], 0),
        jnp.concatenate([ref[16 * i + 12 : 16 * i + 16] for i in range(4)], 0),
        ref[pl.ds(0, 16, stride=4)],
        ref[pl.ds(3, 16, stride=4)],
    ]


def take(values, index, axis):
    return jnp.take_along_axis(values, index, axis=axis, mode="promise_in_bounds")


def turn(values, orient_row):
    shape = values.shape
    orient = jnp.broadcast_to(orient_row, shape)
    place = rows(shape)
    first = (place >> 2) ^ ((orient & 1) * 3)
    second = (place & 3) ^ (((orient >> 1) & 1) * 3)
    flip = (orient & 4) > 0
    source = jnp.where(flip, 4 * second + first, 4 * first + second)
    out = []
    for half in (source[:8], source[8:]):
        within = half & 7
        out.append(jnp.where(half >= 8, take(values[8:], within, 0), take(values[:8], within, 0)))
    return jnp.concatenate(out, 0)


def pick(traces, neighbour_ref, face):
    values = traces[face ^ 1]
    count = values.shape[1]
    index = jnp.clip(neighbour_ref[face : face + 1] - (face ^ 1) * count, 0, count - 1)
    return take(values, jnp.broadcast_to(index, values.shape), 1)


def apply_blocks(ref, values):
    out = []
    for group in range(NODES // 8):
        block = ref[8 * group : 8 * group + 8].astype(F32) * values[None]
        out.append(jnp.sum(block, axis=1))
    return jnp.concatenate(out, 0)


def pack_rim(traces):
    shape = traces[2].shape
    return jnp.where(lanes(shape) < shape[1] // 2, traces[2], traces[3])


def halo_of(pos_ref, gathered_ref):
    slabs, _, count = gathered_ref.shape
    pos = pos_ref[0]
    below = gathered_ref[jnp.maximum(pos - 1, 0)]
    above = gathered_ref[jnp.minimum(pos + 1, slabs - 1)]
    below = jnp.where(pos > 0, pltpu.roll(below, count // 4, 1), 0.0)
    above = jnp.where(pos < slabs - 1, pltpu.roll(above, count - count // 4, 1), 0.0)
    return below, above


def coupling(traces, below, above, neighbour_ref, orient_ref, lift_ref):
    count = below.shape[1]
    edge = count // 4
    turned = []
    for face in range(FACES):
        values = pick(traces, neighbour_ref, face)
        if face == 2:
            values = jnp.where(lanes(values.shape) < edge, below, values)
        if face == 3:
            values = jnp.where(lanes(values.shape) >= count - edge, above, values)
        turned.append(turn(values, orient_ref[face : face + 1]))
    turned = jnp.concatenate(turned, 0)
    lift = lift_ref[...].reshape(FACES * 16, NODES)
    return dot_split(halves(lift), halves(turned), TN)


def rim_kernel(start_ref, rim_ref):
    rim_ref[...] = pack_rim(face_traces(start_ref))


def residual(pos_ref, gathered_ref, sol_ref, rhs_ref, diag_ref, lift_ref, neighbour_ref, orient_ref):
    traces = face_traces(sol_ref)
    below, above = halo_of(pos_ref, gathered_ref)
    coupled = coupling(traces, below, above, neighbour_ref, orient_ref, lift_ref)
    return rhs_ref[...] - (apply_blocks(diag_ref, sol_ref[...]) - coupled)


def sweep_kernel(
    pos_ref, gathered_ref, sol_ref, rhs_ref, diag_ref, precond_ref, lift_ref, neighbour_ref, orient_ref,
    out_ref, rim_ref,
):
    resid = residual(pos_ref, gathered_ref, sol_ref, rhs_ref, diag_ref, lift_ref, neighbour_ref, orient_ref)
    out_ref[...] = sol_ref[...] + apply_blocks(precond_ref, resid)
    rim_ref[...] = pack_rim(face_traces(out_ref))


def targets(owner_row, staying, owner_count, capacity):
    count = owner_row.shape[1]
    shape = (owner_count, count)
    hits = (rows(shape) == owner_row) & (lanes(shape) >= staying)
    hits = jnp.where(hits, 1.0, 0.0)
    before = jnp.where(rows((count, count)) < lanes((count, count)), 1.0, 0.0)
    earlier = dot(hits.astype(BF16), before.astype(BF16), NN)
    rank = jnp.sum(hits * earlier, axis=0, keepdims=True).astype(jnp.int32)
    return jnp.where(lanes(owner_row.shape) >= staying, owner_row * capacity + rank, -1)


def one_hot(condition):
    return jnp.where(condition, 1.0, 0.0).astype(BF16)


def contract(four, line):
    first, second = float(line[0, 1]), float(line[0, 2])
    middle = float(line[1, 1])
    return [
        four[0] + first * four[1] + second * four[2],
        middle * (four[1] + four[2]),
        four[3] + second * four[1] + first * four[2],
    ]


def galerkin_kernel(
    staying, owner_count, capacity,
    diag_ref, owner_ref, slot_ref, table_ref,
    send_ref, local_ref, target_ref, high_ref, low_ref, full_ref,
):
    line = restrict_line()
    count = diag_ref.shape[2]
    chunk = 16

    def step(part, carry):
        at = pl.ds(pl.multiple_of(part * chunk, chunk), chunk)
        planes = []
        for i in range(4):
            bars = []
            for j in range(4):
                four = [diag_ref[16 * i + 4 * j + k, at].astype(F32) for k in range(4)]
                bars.append(contract(four, line))
            sheet = [contract([bars[j][k] for j in range(4)], line) for k in range(3)]
            planes.append([sheet[k][j] for j in range(3) for k in range(3)])
        for rest in range(9):
            made = contract([planes[i][rest] for i in range(4)], line)
            for i in range(3):
                high, low = halves(made[i])
                high_ref[9 * i + rest, at] = high
                low_ref[9 * i + rest, at] = low
        return carry

    lax.fori_loop(0, NODES // chunk, step, 0)
    high_ref[COARSE] = jnp.zeros((NODES, count), BF16)
    low_ref[COARSE] = jnp.zeros((NODES, count), BF16)
    full_ref[...] = jnp.zeros(full_ref.shape, F32)
    padded = table_ref.shape[0] // 2
    table = table_ref[...]
    for part in range(high_ref.shape[0] // GROUP):
        high = high_ref[GROUP * part : GROUP * part + GROUP].reshape(GROUP * NODES, count)
        low = low_ref[GROUP * part : GROUP * part + GROUP].reshape(GROUP * NODES, count)
        both = dot(table, high, NN)
        made = both[:padded] + both[padded:] + dot(table[:padded], low, NN)
        full_ref[GROUP * COARSE * part : GROUP * COARSE * part + padded] = made
    full_ref[COARSE * COARSE : COARSE * COARSE + 1] = (slot_ref[...] + 1).astype(F32)
    local = full_ref[...].astype(BF16)
    local_ref[...] = local
    target = targets(owner_ref[...], staying, owner_count, capacity)
    target_ref[...] = target
    shape = (owner_count * capacity, count)
    send_ref[...] = dot(one_hot(rows(shape) == target), local, NT).astype(BF16)


def slot_hits(got_ref, aggregates):
    ids = got_ref[:, COARSE * COARSE : COARSE * COARSE + 1].astype(F32)
    shape = (ids.shape[0], aggregates)
    return one_hot(ids == (lanes(shape) + 1).astype(F32))


def stay_hits(slot_ref, staying, aggregates):
    shape = (aggregates, slot_ref.shape[1])
    return one_hot((rows(shape) == slot_ref[...]) & (lanes(shape) < staying))


def gather_op_kernel(staying, got_ref, local_ref, slot_ref, out_ref):
    aggregates = out_ref.shape[1]
    total = dot(slot_hits(got_ref, aggregates), got_ref[...], TN)
    total = total + dot(stay_hits(slot_ref, staying, aggregates), local_ref[...], NT)
    out_ref[...] = total.T[: COARSE * COARSE]


def last_kernel(
    pos_ref, gathered_ref, sol_ref, rhs_ref, diag_ref, lift_ref, neighbour_ref, orient_ref, target_ref,
    low_ref, send_ref,
):
    resid = residual(pos_ref, gathered_ref, sol_ref, rhs_ref, diag_ref, lift_ref, neighbour_ref, orient_ref)
    low = resid.astype(BF16)
    low_ref[...] = low
    shape = (send_ref.shape[0], low.shape[1])
    send_ref[...] = dot(one_hot(rows(shape) == target_ref[...]), low, NT).astype(BF16)


def gather_rhs_kernel(staying, got_ref, ids_ref, low_ref, slot_ref, table_ref, out_ref):
    aggregates = out_ref.shape[1]
    total = dot(got_ref[...], slot_hits(ids_ref, aggregates), TN)
    total = total + dot(low_ref[...], stay_hits(slot_ref, staying, aggregates), NT)
    padded = table_ref.shape[0] // 2
    high, low = halves(total)
    both = dot(table_ref[...], high, NN)
    made = both[:padded] + both[padded:] + dot(table_ref[:padded], low, NN)
    out_ref[...] = made[:COARSE]


def call(kernel, outs, args, scratch=(), flops=0, scalars=0):
    bytes_in = sum(a.size * a.dtype.itemsize for a in args)
    bytes_out = sum(o.size * o.dtype.itemsize for o in outs)
    specs = [
        pl.BlockSpec(memory_space=pltpu.SMEM if i < scalars else pltpu.VMEM) for i in range(len(args))
    ]
    return pl.pallas_call(
        kernel,
        out_shape=tuple(outs),
        in_specs=specs,
        out_specs=tuple(pl.BlockSpec(memory_space=pltpu.VMEM) for _ in outs),
        scratch_shapes=list(scratch),
        compiler_params=pltpu.CompilerParams(vmem_limit_bytes=VMEM_LIMIT),
        cost_estimate=pl.CostEstimate(
            flops=flops, bytes_accessed=bytes_in + bytes_out, transcendentals=0
        ),
    )(*args)


def struct(shape, dtype):
    return jax.ShapeDtypeStruct(shape, dtype)


def block_table(table, copies, row_step):
    out = []
    for part in split_table(table):
        full = np.zeros((ceil_to(copies * table.shape[0], row_step), copies * table.shape[1]), BF16)
        for copy in range(copies):
            full[
                copy * table.shape[0] : (copy + 1) * table.shape[0],
                copy * table.shape[1] : (copy + 1) * table.shape[1],
            ] = part
        out.append(full)
    return np.concatenate(out, 0)


def per_device(start, rhs, diag_block, precond, lift, neighbour, orient, owner, slot):
    count = start.shape[1]
    staying = count // 4
    aggregates = count // 2
    owner_count = lax.axis_size("dom")
    movers = count - staying
    capacity = ceil_to(2 * ((movers + owner_count - 2) // (owner_count - 1)), 16)
    total = owner_count * capacity
    entries = ceil_to(COARSE * COARSE + 1, 128)
    groups = -(-COARSE // GROUP)
    pos = jnp.reshape(lax.axis_index("face"), (1,)).astype(jnp.int32)
    owner = owner.reshape(1, count)
    slot = slot.reshape(1, count)
    table = jnp.asarray(block_table(restrict_table(), GROUP, 16))
    small = jnp.asarray(block_table(restrict_table(), 1, 16))

    (rim,) = call(rim_kernel, [struct((16, count), F32)], [start])
    op_send, local_op, target = call(
        lambda *refs: galerkin_kernel(staying, owner_count, capacity, *refs),
        [
            struct((total, entries), BF16),
            struct((entries, count), BF16),
            struct((1, count), jnp.int32),
        ],
        [diag_block, owner, slot, table],
        scratch=[
            pltpu.VMEM((groups * GROUP, NODES, count), BF16),
            pltpu.VMEM((groups * GROUP, NODES, count), BF16),
            pltpu.VMEM((entries, count), F32),
        ],
        flops=200_000_000,
    )
    op_got = lax.all_to_all(op_send, "dom", split_axis=0, concat_axis=0, tiled=True)

    sol = start
    for _ in range(SWEEPS):
        gathered = lax.all_gather(rim, "face")
        sol, rim = call(
            sweep_kernel,
            [struct((NODES, count), F32), struct((16, count), F32)],
            [pos, gathered, sol, rhs, diag_block, precond, lift, neighbour, orient],
            flops=100_000_000,
            scalars=1,
        )
    gathered = lax.all_gather(rim, "face")
    low, rhs_send = call(
        last_kernel,
        [struct((NODES, count), BF16), struct((total, NODES), BF16)],
        [pos, gathered, sol, rhs, diag_block, lift, neighbour, orient, target],
        flops=100_000_000,
        scalars=1,
    )
    rhs_got = lax.all_to_all(rhs_send, "dom", split_axis=0, concat_axis=0, tiled=True)
    (coarse_op,) = call(
        lambda *refs: gather_op_kernel(staying, *refs),
        [struct((COARSE * COARSE, aggregates), F32)],
        [op_got, local_op, slot],
        flops=100_000_000,
    )
    (coarse_rhs,) = call(
        lambda *refs: gather_rhs_kernel(staying, *refs),
        [struct((COARSE, aggregates), F32)],
        [rhs_got, op_got, low, slot, small],
        flops=10_000_000,
    )
    return (sol, coarse_op, coarse_rhs)


def solution(mesh):
    return jax.shard_map(
        per_device,
        mesh=mesh,
        in_specs=(
            P(None, ("dom", "face")),
            P(None, ("dom", "face")),
            P(None, None, ("dom", "face")),
            P(None, None, ("dom", "face")),
            P(),
            P(None, ("dom", "face")),
            P(None, ("dom", "face")),
            P(("dom", "face")),
            P(("dom", "face")),
        ),
        out_specs=(P(None, ("dom", "face")), P(None, ("dom", "face")), P(None, ("dom", "face"))),
        check_vma=False,
    )
```

```python
import jax
import jax.numpy as jnp
import numpy as np
from jax import lax
from jax.experimental import pallas as pl
from jax.experimental.pallas import tpu as pltpu
from jax.sharding import PartitionSpec as P

SWEEPS = 2
NODES = 64
COARSE = 27
FACES = 6
GROUP = 4
F32 = jnp.float32
BF16 = jnp.bfloat16
VMEM_LIMIT = 24 * 1024 * 1024

NN = (((1,), (0,)), ((), ()))
NT = (((1,), (1,)), ((), ()))
TN = (((0,), (0,)), ((), ()))


def restrict_line():
    fine = np.array([-1.0, -1.0 / np.sqrt(5.0), 1.0 / np.sqrt(5.0), 1.0])
    coarse = np.array([-1.0, 0.0, 1.0])
    basis = np.ones((4, 3))
    for column in range(3):
        for other in range(3):
            if other != column:
                basis[:, column] *= (fine - coarse[other]) / (coarse[column] - coarse[other])
    return basis.T


def restrict_table():
    line = restrict_line()
    return np.kron(np.kron(line, line), line)


def split_table(table):
    table = table.astype(np.float32)
    high = table.astype(BF16)
    low = (table - high.astype(np.float32)).astype(BF16)
    return high, low


def ceil_to(value, step):
    return -(-value // step) * step


def halves(values):
    high = values.astype(BF16)
    low = (values - high.astype(F32)).astype(BF16)
    return high, low


def dot(left, right, dims):
    return lax.dot_general(left, right, dims, preferred_element_type=F32)


def dot_split(left, right, dims):
    left_high, left_low = left
    right_high, right_low = right
    return (
        dot(left_high, right_high, dims)
        + dot(left_low, right_high, dims)
        + dot(left_high, right_low, dims)
    )


def lanes(shape):
    return lax.broadcasted_iota(jnp.int32, shape, 1)


def rows(shape):
    return lax.broadcasted_iota(jnp.int32, shape, 0)


def face_traces(ref):
    return [
        ref[0:16],
        ref[48:64],
        jnp.concatenate([ref[16 * i : 16 * i + 4] for i in range(4)], 0),
        jnp.concatenate([ref[16 * i + 12 : 16 * i + 16] for i in range(4)], 0),
        ref[pl.ds(0, 16, stride=4)],
        ref[pl.ds(3, 16, stride=4)],
    ]


def take(values, index, axis):
    return jnp.take_along_axis(values, index, axis=axis, mode="promise_in_bounds")


def turn(values, orient_row):
    shape = values.shape
    orient = jnp.broadcast_to(orient_row, shape)
    place = rows(shape)
    first = (place >> 2) ^ ((orient & 1) * 3)
    second = (place & 3) ^ (((orient >> 1) & 1) * 3)
    flip = (orient & 4) > 0
    source = jnp.where(flip, 4 * second + first, 4 * first + second)
    out = []
    for half in (source[:8], source[8:]):
        within = half & 7
        out.append(jnp.where(half >= 8, take(values[8:], within, 0), take(values[:8], within, 0)))
    return jnp.concatenate(out, 0)


def pick(traces, neighbour_ref, face):
    values = traces[face ^ 1]
    count = values.shape[1]
    index = jnp.clip(neighbour_ref[face : face + 1] - (face ^ 1) * count, 0, count - 1)
    return take(values, jnp.broadcast_to(index, values.shape), 1)


def apply_blocks(ref, values):
    out = []
    for group in range(NODES // 8):
        block = ref[8 * group : 8 * group + 8].astype(F32) * values[None]
        out.append(jnp.sum(block, axis=1))
    return jnp.concatenate(out, 0)


def pack_rim(traces):
    shape = traces[2].shape
    return jnp.where(lanes(shape) < shape[1] // 2, traces[2], traces[3])


def coupling(traces, below, above, neighbour_ref, orient_ref, lift_ref):
    count = below.shape[1]
    edge = count // 4
    turned = []
    for face in range(FACES):
        values = pick(traces, neighbour_ref, face)
        if face == 2:
            values = jnp.where(lanes(values.shape) < edge, below, values)
        if face == 3:
            values = jnp.where(lanes(values.shape) >= count - edge, above, values)
        turned.append(turn(values, orient_ref[face : face + 1]))
    turned = jnp.concatenate(turned, 0)
    lift = lift_ref[...].reshape(FACES * 16, NODES)
    return dot_split(halves(lift), halves(turned), TN)


def edge_mask(shape):
    return (lanes(shape) < shape[1] // 4) | (lanes(shape) >= shape[1] - shape[1] // 4)


def low_mask(shape):
    return ((lanes(shape) // (shape[1] // 4)) & 1) == 0


def both_halves(shape, low, high):
    return jnp.where(lanes(shape) < shape[1] // 2, low, high)


def response(precond_ref, lift_ref):
    count = precond_ref.shape[2]
    parts = []
    for face in (2, 3):
        parts.extend(halves(lift_ref[face]))
    stack = jnp.concatenate(parts, 0)
    shape = (NODES, count)
    out = []
    for spot in range(16):
        node = 16 * (spot // 4) + spot % 4
        block = both_halves(shape, precond_ref[node].astype(F32), precond_ref[node + 12].astype(F32))
        made = dot(stack, block.astype(BF16), NN)
        out.append(
            both_halves((16, count), made[0:16] + made[16:32], made[32:48] + made[48:64])
        )
    return out


def halo_lift(below, above, orient_ref, lift_ref):
    shape = below.shape
    edge = shape[1] // 4
    low = jnp.where(lanes(shape) < edge, turn(below, orient_ref[2:3]), 0.0)
    high = jnp.where(lanes(shape) >= shape[1] - edge, turn(above, orient_ref[3:4]), 0.0)
    lift = lift_ref[2:4].reshape(32, NODES)
    return dot_split(halves(lift), halves(jnp.concatenate([low, high], 0)), TN)


def first_kernel(
    start_ref, rhs_ref, diag_ref, precond_ref, lift_ref, neighbour_ref, orient_ref,
    partial_ref, message_ref,
):
    traces = face_traces(start_ref)
    shape = traces[2].shape
    count = shape[1]
    none = jnp.zeros(shape, F32)
    coupled = coupling(traces, none, none, neighbour_ref, orient_ref, lift_ref)
    resid = rhs_ref[...] - (apply_blocks(diag_ref, start_ref[...]) - coupled)
    partial_ref[...] = start_ref[...] + apply_blocks(precond_ref, resid)
    direct = edge_mask(shape)
    later = pack_rim(face_traces(partial_ref))
    message_ref[0:16] = jnp.where(direct, pack_rim(traces), pltpu.roll(later, count // 2, 1))
    reply = response(precond_ref, lift_ref)
    for spot in range(8):
        message_ref[16 + 16 * spot : 32 + 16 * spot] = jnp.where(
            direct, reply[spot], pltpu.roll(reply[spot + 8], count // 2, 1)
        )
    orient = both_halves((1, count), orient_ref[2:3], orient_ref[3:4])
    message_ref[144:152] = jnp.broadcast_to(orient.astype(F32), (8, count))


def merged(pos_ref, gathered_ref, at):
    slabs = gathered_ref.shape[0]
    pos = pos_ref[0]
    above = gathered_ref[jnp.minimum(pos + 1, slabs - 1), at]
    below = gathered_ref[jnp.maximum(pos - 1, 0), at]
    above = jnp.where(pos < slabs - 1, above, 0.0)
    below = jnp.where(pos > 0, below, 0.0)
    return jnp.where(low_mask(above.shape), above, below)


def aside(values):
    count = values.shape[1]
    return pltpu.roll(values, count // 4, 1), pltpu.roll(values, count - count // 4, 1)


def middle_kernel(
    pos_ref, gathered_ref, start_ref, partial_ref, rhs_ref, diag_ref, precond_ref, lift_ref,
    neighbour_ref, orient_ref,
    out_ref, rest_ref, rim_ref, sol_ref,
):
    own = face_traces(start_ref)
    shape = own[2].shape
    count = shape[1]
    head = merged(pos_ref, gathered_ref, pl.ds(0, 16))
    orient = merged(pos_ref, gathered_ref, pl.ds(144, 8))[0:1].astype(jnp.int32)
    sent = both_halves(shape, aside(own[3])[0], aside(own[2])[1])
    sent = turn(sent, orient)
    below, above = aside(head)
    delta = halo_lift(below, above, orient_ref, lift_ref)
    sol_ref[...] = partial_ref[...] + apply_blocks(precond_ref, delta)
    later = pltpu.roll(head, count // 2, 1)
    reply = []
    for spot in range(8):
        block = merged(pos_ref, gathered_ref, pl.ds(16 + 16 * spot, 16))
        reply.append((block, pltpu.roll(block, count // 2, 1)))
    reply = [pair[0] for pair in reply] + [pair[1] for pair in reply]
    change = [jnp.sum(block * sent, axis=0, keepdims=True) for block in reply]
    below, above = aside(later + jnp.concatenate(change, 0))
    traces = face_traces(sol_ref)
    coupled = coupling(traces, below, above, neighbour_ref, orient_ref, lift_ref)
    resid = rhs_ref[...] - (apply_blocks(diag_ref, sol_ref[...]) - coupled)
    out_ref[...] = sol_ref[...] + apply_blocks(precond_ref, resid)
    traces = face_traces(out_ref)
    none = jnp.zeros(shape, F32)
    coupled = coupling(traces, none, none, neighbour_ref, orient_ref, lift_ref)
    rest_ref[...] = rhs_ref[...] - (apply_blocks(diag_ref, out_ref[...]) - coupled)
    rim_ref[...] = pack_rim(traces)


def targets(owner_row, staying, owner_count, capacity):
    count = owner_row.shape[1]
    shape = (owner_count, count)
    hits = (rows(shape) == owner_row) & (lanes(shape) >= staying)
    hits = jnp.where(hits, 1.0, 0.0)
    before = jnp.where(rows((count, count)) < lanes((count, count)), 1.0, 0.0)
    earlier = dot(hits.astype(BF16), before.astype(BF16), NN)
    rank = jnp.sum(hits * earlier, axis=0, keepdims=True).astype(jnp.int32)
    return jnp.where(lanes(owner_row.shape) >= staying, owner_row * capacity + rank, -1)


def one_hot(condition):
    return jnp.where(condition, 1.0, 0.0).astype(BF16)


def contract(four, line):
    first, second = float(line[0, 1]), float(line[0, 2])
    middle = float(line[1, 1])
    return [
        four[0] + first * four[1] + second * four[2],
        middle * (four[1] + four[2]),
        four[3] + second * four[1] + first * four[2],
    ]


def galerkin_kernel(
    staying, owner_count, capacity,
    diag_ref, owner_ref, slot_ref, table_ref,
    send_ref, local_ref, target_ref, high_ref, low_ref, full_ref,
):
    line = restrict_line()
    count = diag_ref.shape[2]
    chunk = 16

    def step(part, carry):
        at = pl.ds(pl.multiple_of(part * chunk, chunk), chunk)
        planes = []
        for i in range(4):
            bars = []
            for j in range(4):
                four = [diag_ref[16 * i + 4 * j + k, at].astype(F32) for k in range(4)]
                bars.append(contract(four, line))
            sheet = [contract([bars[j][k] for j in range(4)], line) for k in range(3)]
            planes.append([sheet[k][j] for j in range(3) for k in range(3)])
        for rest in range(9):
            made = contract([planes[i][rest] for i in range(4)], line)
            for i in range(3):
                high, low = halves(made[i])
                high_ref[9 * i + rest, at] = high
                low_ref[9 * i + rest, at] = low
        return carry

    lax.fori_loop(0, NODES // chunk, step, 0)
    high_ref[COARSE] = jnp.zeros((NODES, count), BF16)
    low_ref[COARSE] = jnp.zeros((NODES, count), BF16)
    full_ref[...] = jnp.zeros(full_ref.shape, F32)
    padded = table_ref.shape[0] // 2
    table = table_ref[...]
    for part in range(high_ref.shape[0] // GROUP):
        high = high_ref[GROUP * part : GROUP * part + GROUP].reshape(GROUP * NODES, count)
        low = low_ref[GROUP * part : GROUP * part + GROUP].reshape(GROUP * NODES, count)
        both = dot(table, high, NN)
        made = both[:padded] + both[padded:] + dot(table[:padded], low, NN)
        full_ref[GROUP * COARSE * part : GROUP * COARSE * part + padded] = made
    full_ref[COARSE * COARSE : COARSE * COARSE + 1] = (slot_ref[...] + 1).astype(F32)
    local = full_ref[...].astype(BF16)
    local_ref[...] = local
    target = targets(owner_ref[...], staying, owner_count, capacity)
    target_ref[...] = target
    shape = (owner_count * capacity, count)
    send_ref[...] = dot(one_hot(rows(shape) == target), local, NT).astype(BF16)


def slot_hits(got_ref, aggregates):
    ids = got_ref[:, COARSE * COARSE : COARSE * COARSE + 1].astype(F32)
    shape = (ids.shape[0], aggregates)
    return one_hot(ids == (lanes(shape) + 1).astype(F32))


def stay_hits(slot_ref, staying, aggregates):
    shape = (aggregates, slot_ref.shape[1])
    return one_hot((rows(shape) == slot_ref[...]) & (lanes(shape) < staying))


def gather_op_kernel(staying, got_ref, local_ref, slot_ref, out_ref):
    aggregates = out_ref.shape[1]
    total = dot(slot_hits(got_ref, aggregates), got_ref[...], TN)
    total = total + dot(stay_hits(slot_ref, staying, aggregates), local_ref[...], NT)
    out_ref[...] = total.T[: COARSE * COARSE]


def last_kernel(
    pos_ref, gathered_ref, rest_ref, lift_ref, orient_ref, target_ref, after_ref,
    low_ref, send_ref,
):
    below, above = aside(merged(pos_ref, gathered_ref, pl.ds(0, 16)))
    resid = rest_ref[...] + halo_lift(below, above, orient_ref, lift_ref)
    low = resid.astype(BF16)
    low_ref[...] = low
    shape = (send_ref.shape[0], low.shape[1])
    send_ref[...] = dot(one_hot(rows(shape) == target_ref[...]), low, NT).astype(BF16)


def gather_rhs_kernel(staying, got_ref, ids_ref, low_ref, slot_ref, table_ref, out_ref):
    aggregates = out_ref.shape[1]
    total = dot(got_ref[...], slot_hits(ids_ref, aggregates), TN)
    total = total + dot(low_ref[...], stay_hits(slot_ref, staying, aggregates), NT)
    padded = table_ref.shape[0] // 2
    high, low = halves(total)
    both = dot(table_ref[...], high, NN)
    made = both[:padded] + both[padded:] + dot(table_ref[:padded], low, NN)
    out_ref[...] = made[:COARSE]


def call(kernel, outs, args, scratch=(), flops=0, scalars=0, anywhere=0):
    bytes_in = sum(a.size * a.dtype.itemsize for a in args)
    bytes_out = sum(o.size * o.dtype.itemsize for o in outs)
    spaces = [pltpu.SMEM] * scalars + [pltpu.VMEM] * (len(args) - scalars - anywhere) + [pl.ANY] * anywhere
    specs = [pl.BlockSpec(memory_space=space) for space in spaces]
    return pl.pallas_call(
        kernel,
        out_shape=tuple(outs),
        in_specs=specs,
        out_specs=tuple(pl.BlockSpec(memory_space=pltpu.VMEM) for _ in outs),
        scratch_shapes=list(scratch),
        compiler_params=pltpu.CompilerParams(vmem_limit_bytes=VMEM_LIMIT),
        cost_estimate=pl.CostEstimate(
            flops=flops, bytes_accessed=bytes_in + bytes_out, transcendentals=0
        ),
    )(*args)


def struct(shape, dtype):
    return jax.ShapeDtypeStruct(shape, dtype)


def block_table(table, copies, row_step):
    out = []
    for part in split_table(table):
        full = np.zeros((ceil_to(copies * table.shape[0], row_step), copies * table.shape[1]), BF16)
        for copy in range(copies):
            full[
                copy * table.shape[0] : (copy + 1) * table.shape[0],
                copy * table.shape[1] : (copy + 1) * table.shape[1],
            ] = part
        out.append(full)
    return np.concatenate(out, 0)


def per_device(start, rhs, diag_block, precond, lift, neighbour, orient, owner, slot):
    count = start.shape[1]
    staying = count // 4
    aggregates = count // 2
    owner_count = lax.axis_size("dom")
    movers = count - staying
    capacity = ceil_to(2 * ((movers + owner_count - 2) // (owner_count - 1)), 16)
    total = owner_count * capacity
    entries = ceil_to(COARSE * COARSE + 1, 128)
    groups = -(-COARSE // GROUP)
    pos = jnp.reshape(lax.axis_index("face"), (1,)).astype(jnp.int32)
    owner = owner.reshape(1, count)
    slot = slot.reshape(1, count)
    table = jnp.asarray(block_table(restrict_table(), GROUP, 16))
    small = jnp.asarray(block_table(restrict_table(), 1, 16))

    op_send, local_op, target = call(
        lambda *refs: galerkin_kernel(staying, owner_count, capacity, *refs),
        [
            struct((total, entries), BF16),
            struct((entries, count), BF16),
            struct((1, count), jnp.int32),
        ],
        [diag_block, owner, slot, table],
        scratch=[
            pltpu.VMEM((groups * GROUP, NODES, count), BF16),
            pltpu.VMEM((groups * GROUP, NODES, count), BF16),
            pltpu.VMEM((entries, count), F32),
        ],
        flops=200_000_000,
    )
    op_got = lax.all_to_all(op_send, "dom", split_axis=0, concat_axis=0, tiled=True)

    partial, message = call(
        first_kernel,
        [struct((NODES, count), F32), struct((152, count), F32)],
        [start, rhs, diag_block, precond, lift, neighbour, orient],
        flops=100_000_000,
    )
    gathered = lax.all_gather(message, "face")
    sol, rest, rim = call(
        middle_kernel,
        [struct((NODES, count), F32), struct((NODES, count), F32), struct((16, count), F32)],
        [pos, gathered, start, partial, rhs, diag_block, precond, lift, neighbour, orient],
        scratch=[pltpu.VMEM((NODES, count), F32)],
        flops=200_000_000,
        scalars=1,
    )
    gathered = lax.all_gather(rim, "face")
    low, rhs_send = call(
        last_kernel,
        [struct((NODES, count), BF16), struct((total, NODES), BF16)],
        [pos, gathered, rest, lift, orient, target, op_got],
        flops=100_000_000,
        scalars=1,
        anywhere=1,
    )
    rhs_got = lax.all_to_all(rhs_send, "dom", split_axis=0, concat_axis=0, tiled=True)
    (coarse_op,) = call(
        lambda *refs: gather_op_kernel(staying, *refs),
        [struct((COARSE * COARSE, aggregates), F32)],
        [op_got, local_op, slot],
        flops=100_000_000,
    )
    (coarse_rhs,) = call(
        lambda *refs: gather_rhs_kernel(staying, *refs),
        [struct((COARSE, aggregates), F32)],
        [rhs_got, op_got, low, slot, small],
        flops=10_000_000,
    )
    return (sol, coarse_op, coarse_rhs)


def solution(mesh):
    return jax.shard_map(
        per_device,
        mesh=mesh,
        in_specs=(
            P(None, ("dom", "face")),
            P(None, ("dom", "face")),
            P(None, None, ("dom", "face")),
            P(None, None, ("dom", "face")),
            P(),
            P(None, ("dom", "face")),
            P(None, ("dom", "face")),
            P(("dom", "face")),
            P(("dom", "face")),
        ),
        out_specs=(P(None, ("dom", "face")), P(None, ("dom", "face")), P(None, ("dom", "face"))),
        check_vma=False,
    )
```

```python
import jax
import jax.numpy as jnp
import numpy as np
from jax import lax
from jax.experimental import pallas as pl
from jax.experimental.pallas import tpu as pltpu
from jax.sharding import PartitionSpec as P

SWEEPS = 2
NODES = 64
COARSE = 27
FACES = 6
GROUP = 4
F32 = jnp.float32
BF16 = jnp.bfloat16
VMEM_LIMIT = 24 * 1024 * 1024
FIRST_LIMIT = None

NN = (((1,), (0,)), ((), ()))
NT = (((1,), (1,)), ((), ()))
TN = (((0,), (0,)), ((), ()))


def restrict_line():
    fine = np.array([-1.0, -1.0 / np.sqrt(5.0), 1.0 / np.sqrt(5.0), 1.0])
    coarse = np.array([-1.0, 0.0, 1.0])
    basis = np.ones((4, 3))
    for column in range(3):
        for other in range(3):
            if other != column:
                basis[:, column] *= (fine - coarse[other]) / (coarse[column] - coarse[other])
    return basis.T


def restrict_table():
    line = restrict_line()
    return np.kron(np.kron(line, line), line)


def split_table(table):
    table = table.astype(np.float32)
    high = table.astype(BF16)
    low = (table - high.astype(np.float32)).astype(BF16)
    return high, low


def ceil_to(value, step):
    return -(-value // step) * step


def halves(values):
    high = values.astype(BF16)
    low = (values - high.astype(F32)).astype(BF16)
    return high, low


def dot(left, right, dims):
    return lax.dot_general(left, right, dims, preferred_element_type=F32)


def dot_split(left, right, dims):
    left_high, left_low = left
    right_high, right_low = right
    return (
        dot(left_high, right_high, dims)
        + dot(left_low, right_high, dims)
        + dot(left_high, right_low, dims)
    )


def small_table():
    shape = (32, NODES)
    line = restrict_line()
    row, col = rows(shape), lanes(shape)
    step = 9
    table = jnp.ones(shape, F32)
    left = row
    for digit in range(3):
        mine = (left >= step).astype(jnp.int32) + (left >= 2 * step).astype(jnp.int32)
        left = left - step * mine
        fine = (col >> (4 - 2 * digit)) & 3
        value = jnp.zeros(shape, F32)
        for i in range(3):
            for j in range(4):
                value = jnp.where((mine == i) & (fine == j), float(line[i, j]), value)
        table = table * value
        step //= 3
    return jnp.where(row < COARSE, table, 0.0)


def lanes(shape):
    return lax.broadcasted_iota(jnp.int32, shape, 1)


def rows(shape):
    return lax.broadcasted_iota(jnp.int32, shape, 0)


def face_traces(ref):
    return [
        ref[0:16],
        ref[48:64],
        jnp.concatenate([ref[16 * i : 16 * i + 4] for i in range(4)], 0),
        jnp.concatenate([ref[16 * i + 12 : 16 * i + 16] for i in range(4)], 0),
        ref[pl.ds(0, 16, stride=4)],
        ref[pl.ds(3, 16, stride=4)],
    ]


def take(values, index, axis):
    return jnp.take_along_axis(values, index, axis=axis, mode="promise_in_bounds")


def turn(values, orient_row):
    shape = values.shape
    orient = jnp.broadcast_to(orient_row, shape)
    place = rows(shape)
    first = (place >> 2) ^ ((orient & 1) * 3)
    second = (place & 3) ^ (((orient >> 1) & 1) * 3)
    flip = (orient & 4) > 0
    source = jnp.where(flip, 4 * second + first, 4 * first + second)
    out = []
    for half in (source[:8], source[8:]):
        within = half & 7
        out.append(jnp.where(half >= 8, take(values[8:], within, 0), take(values[:8], within, 0)))
    return jnp.concatenate(out, 0)


def pick(traces, neighbour_ref, face):
    values = traces[face ^ 1]
    count = values.shape[1]
    index = jnp.clip(neighbour_ref[face : face + 1] - (face ^ 1) * count, 0, count - 1)
    return take(values, jnp.broadcast_to(index, values.shape), 1)


def fold(parts):
    place = rows(parts[0].shape)
    step = 1
    while len(parts) > 1:
        even = (place & step) == 0
        parts = [
            jnp.where(even, x, y) + pltpu.roll(jnp.where(even, y, x), step, 0)
            for x, y in zip(parts[::2], parts[1::2])
        ]
        step *= 2
    return parts[0]


def apply_blocks(ref, values):
    count = values.shape[1]
    tiles = values.reshape(NODES // 8, 8, count)
    out = []
    for group in range(NODES // 8):
        parts = []
        for node in range(8 * group, 8 * group + 8):
            parts.append(jnp.sum(ref[node].astype(F32).reshape(NODES // 8, 8, count) * tiles, axis=0))
        out.append(fold(parts))
    return jnp.concatenate(out, 0)


def pack_rim(traces):
    shape = traces[2].shape
    return jnp.where(lanes(shape) < shape[1] // 2, traces[2], traces[3])


def coupling(traces, below, above, neighbour_ref, orient_ref, lift_ref):
    count = below.shape[1]
    edge = count // 4
    turned = []
    for face in range(FACES):
        values = pick(traces, neighbour_ref, face)
        if face == 2:
            values = jnp.where(lanes(values.shape) < edge, below, values)
        if face == 3:
            values = jnp.where(lanes(values.shape) >= count - edge, above, values)
        turned.append(turn(values, orient_ref[face : face + 1]))
    turned = jnp.concatenate(turned, 0)
    lift = lift_ref[...].reshape(FACES * 16, NODES)
    return dot_split(halves(lift), halves(turned), TN)


def edge_mask(shape):
    return (lanes(shape) < shape[1] // 4) | (lanes(shape) >= shape[1] - shape[1] // 4)


def low_mask(shape):
    return ((lanes(shape) // (shape[1] // 4)) & 1) == 0


def both_halves(shape, low, high):
    return jnp.where(lanes(shape) < shape[1] // 2, low, high)


def response(precond_ref, lift_ref):
    count = precond_ref.shape[2]
    parts = []
    for face in (2, 3):
        parts.extend(halves(lift_ref[face]))
    stack = jnp.concatenate(parts, 0)
    shape = (NODES, count)
    out = []
    for spot in range(16):
        node = 16 * (spot // 4) + spot % 4
        block = both_halves(shape, precond_ref[node].astype(F32), precond_ref[node + 12].astype(F32))
        made = dot(stack, block.astype(BF16), NN)
        out.append(
            both_halves((16, count), made[0:16] + made[16:32], made[32:48] + made[48:64])
        )
    return out


def halo_lift(below, above, orient_ref, lift_ref):
    shape = below.shape
    edge = shape[1] // 4
    low = jnp.where(lanes(shape) < edge, turn(below, orient_ref[2:3]), 0.0)
    high = jnp.where(lanes(shape) >= shape[1] - edge, turn(above, orient_ref[3:4]), 0.0)
    lift = lift_ref[2:4].reshape(32, NODES)
    return dot_split(halves(lift), halves(jnp.concatenate([low, high], 0)), TN)


def first_half(
    start_ref, rhs_ref, diag_ref, precond_ref, lift_ref, neighbour_ref, orient_ref, owner_rank,
    partial_ref, message_ref, wait_precond,
):
    traces = face_traces(start_ref)
    shape = traces[2].shape
    count = shape[1]
    none = jnp.zeros(shape, F32)
    coupled = coupling(traces, none, none, neighbour_ref, orient_ref, lift_ref)
    resid = rhs_ref[...] - (apply_blocks(diag_ref, start_ref[...]) - coupled)
    wait_precond()
    partial_ref[...] = start_ref[...] + apply_blocks(precond_ref, resid)
    direct = edge_mask(shape)
    reply = response(precond_ref, lift_ref)
    for spot in range(8):
        message_ref[48 + 16 * spot : 64 + 16 * spot] = jnp.where(
            direct, reply[spot], pltpu.roll(reply[spot + 8], count // 2, 1)
        ).astype(BF16)
    later = pack_rim(face_traces(partial_ref))
    high, low = halves(jnp.where(direct, pack_rim(traces), pltpu.roll(later, count // 2, 1)))
    message_ref[0:16] = high
    message_ref[16:32] = low
    orient = both_halves((1, count), orient_ref[2:3], orient_ref[3:4])
    owner, rank = owner_rank
    place = rows(shape)
    facts = jnp.where(place < 4, orient, jnp.where(place < 8, owner, rank))
    message_ref[32:48] = facts.astype(F32).astype(BF16)


def merged(pos_ref, gathered_ref, at):
    slabs = gathered_ref.shape[0]
    pos = pos_ref[0]
    above = gathered_ref[jnp.minimum(pos + 1, slabs - 1), at].astype(F32)
    below = gathered_ref[jnp.maximum(pos - 1, 0), at].astype(F32)
    above = jnp.where(pos < slabs - 1, above, 0.0)
    below = jnp.where(pos > 0, below, 0.0)
    return jnp.where(low_mask(above.shape), above, below)


def aside(values):
    count = values.shape[1]
    return pltpu.roll(values, count // 4, 1), pltpu.roll(values, count - count // 4, 1)


def target_of(facts, staying, capacity):
    owner = facts[4:5].astype(jnp.int32)
    rank = facts[8:9].astype(jnp.int32)
    return jnp.where(lanes(owner.shape) >= staying, owner * capacity + rank, -1)


def middle_kernel(
    staying, capacity,
    pos_ref, gathered_ref, start_ref, partial_ref, rhs_ref, diag_ref, precond_ref, lift_ref,
    neighbour_ref, orient_ref, slot_ref,
    out_ref, rest_ref, rim_ref, facts_ref, edge_ref, sol_ref, new_ref, sem,
):
    own = face_traces(start_ref)
    shape = own[2].shape
    count = shape[1]
    head = merged(pos_ref, gathered_ref, pl.ds(0, 16)) + merged(pos_ref, gathered_ref, pl.ds(16, 16))
    known = merged(pos_ref, gathered_ref, pl.ds(32, 16))
    orient = known[0:1].astype(jnp.int32)
    sent = both_halves(shape, aside(own[3])[0], aside(own[2])[1])
    sent = turn(sent, orient)
    below, above = aside(head)
    delta = halo_lift(below, above, orient_ref, lift_ref)
    sol_ref[...] = partial_ref[...] + apply_blocks(precond_ref, delta)
    later = pltpu.roll(head, count // 2, 1)
    reply = []
    for spot in range(8):
        block = merged(pos_ref, gathered_ref, pl.ds(48 + 16 * spot, 16))
        reply.append((block, pltpu.roll(block, count // 2, 1)))
    reply = [pair[0] for pair in reply] + [pair[1] for pair in reply]
    change = [block * sent for block in reply]
    change = [block[:8] + block[8:] for block in change]
    change = jnp.concatenate([fold(change[:8]), fold(change[8:])], 0)
    below, above = aside(later + change)
    traces = face_traces(sol_ref)
    coupled = coupling(traces, below, above, neighbour_ref, orient_ref, lift_ref)
    resid = rhs_ref[...] - (apply_blocks(diag_ref, sol_ref[...]) - coupled)
    new_ref[...] = sol_ref[...] + apply_blocks(precond_ref, resid)
    copy = pltpu.make_async_copy(new_ref, out_ref, sem)
    copy.start()
    traces = face_traces(new_ref)
    none = jnp.zeros(shape, F32)
    coupled = coupling(traces, none, none, neighbour_ref, orient_ref, lift_ref)
    rest_ref[...] = rhs_ref[...] - (apply_blocks(diag_ref, new_ref[...]) - coupled)
    rim_ref[...] = pack_rim(traces)
    mine = gathered_ref[pos_ref[0], pl.ds(32, 16)].astype(F32)
    target = jnp.where(
        lanes((1, count)) >= count - count // 4, target_of(known, staying, capacity), -1
    )
    place = rows((8, count))
    facts = jnp.where(place == 0, orient, target)
    facts = jnp.where(place == 2, target_of(mine, staying, capacity), facts)
    facts = jnp.where(place == 3, orient_ref[2:3], facts)
    facts_ref[...] = jnp.where(place == 4, slot_ref[...], facts)
    edge_ref[...] = lift_ref[2:4].reshape(32, NODES)
    copy.wait()


def spread(values, copies):
    none = jnp.zeros(values.shape, values.dtype)
    return jnp.concatenate(
        [
            jnp.concatenate([values if i == j else none for j in range(copies)], 1)
            for i in range(copies)
        ],
        0,
    )


def packed_by_target(values, target, owners, depth):
    count = values.shape[1]
    shape = (owners * depth, count)
    place = rows(shape)
    base = (place // depth) * (GROUP * depth) + place % depth
    hits = jnp.concatenate([one_hot(base + depth * g == target) for g in range(GROUP)], 1)
    made = dot(hits, spread(values, GROUP), NT)
    return made.reshape(owners, depth, GROUP * values.shape[0])


def send_kernel(pos_ref, rest_ref, rim_ref, facts_ref, after_ref, send_ref):
    pos = pos_ref[0]
    count = rest_ref.shape[1]
    edge = count // 4
    owners, slabs, depth, _ = send_ref.shape
    high, low = halves(rest_ref[...])
    keep = lanes(low.shape) >= count - edge
    low = jnp.where(keep, low.astype(F32), 0.0).astype(BF16)
    made = dot_split(halves(small_table()), (high, low), NN)
    send_ref[...] = jnp.zeros(send_ref.shape, BF16)
    ours = packed_by_target(made.astype(BF16), facts_ref[2:3], owners, depth)
    send_ref[:, pl.ds(pos, 1)] = ours.astype(BF16)[:, None]
    moved_up, moved_down = aside(rim_ref[...])

    @pl.when(pos > 0)
    def _():
        turned = turn(moved_down, facts_ref[0:1])
        turned = jnp.concatenate([turned, jnp.zeros(turned.shape, F32)], 0).astype(BF16)
        theirs = packed_by_target(turned, facts_ref[1:2], owners, depth)
        send_ref[:, pl.ds(pos - 1, 1)] = theirs.astype(BF16)[:, None]

    @pl.when(pos < slabs - 1)
    def _():
        group = lanes((8, count)) // edge
        rim = jnp.where(group == 0, moved_up[0:8], pltpu.roll(moved_up[8:16], edge, 1))
        send_ref[pl.ds(pos_ref[1], 1), pl.ds(pos + 1, 1), 0:8] = rim.astype(BF16)[None, None]


def rank_row(owner_row, staying, owner_count):
    count = owner_row.shape[1]
    shape = (owner_count, count)
    hits = (rows(shape) == owner_row) & (lanes(shape) >= staying)
    hits = jnp.where(hits, 1.0, 0.0)
    before = jnp.where(rows((count, count)) < lanes((count, count)), 1.0, 0.0)
    earlier = dot(hits.astype(BF16), before.astype(BF16), NN)
    return jnp.sum(hits * earlier, axis=0, keepdims=True).astype(jnp.int32)


def one_hot(condition):
    return jnp.where(condition, 1.0, 0.0).astype(BF16)


def contract(four, line):
    first, second = float(line[0, 1]), float(line[0, 2])
    middle = float(line[1, 1])
    return [
        four[0] + first * four[1] + second * four[2],
        middle * (four[1] + four[2]),
        four[3] + second * four[1] + first * four[2],
    ]


def first_kernel(staying, owner_count, capacity, *refs):
    (diag_in, slot_in, owner_in, table_in, start_in, rhs_in, lift_in, neighbour_in, orient_in, precond_in) = refs[:10]
    (send_out, local_out, partial_out, message_out) = refs[10:14]
    (diag_ref, slot_ref, owner_ref, table_ref, start_ref, rhs_ref, lift_ref, neighbour_ref) = refs[14:22]
    (orient_ref, precond_ref, send_ref, local_ref, partial_ref, message_ref) = refs[22:28]
    (high_ref, low_ref, full_ref, part_sem, sem, out_sem) = refs[28:]
    line = restrict_line()
    count = diag_ref.shape[2]
    chunk = 16

    def part_copy(part):
        at = pl.ds(pl.multiple_of(part * chunk, chunk), chunk)
        return pltpu.make_async_copy(diag_in.at[:, at], diag_ref.at[:, at], part_sem.at[part])

    pairs = [
        (slot_in, slot_ref), (owner_in, owner_ref), (table_in, table_ref), (start_in, start_ref),
        (rhs_in, rhs_ref), (lift_in, lift_ref), (neighbour_in, neighbour_ref), (orient_in, orient_ref),
        (precond_in, precond_ref),
    ]
    copies = [pltpu.make_async_copy(src, dst, sem.at[i]) for i, (src, dst) in enumerate(pairs)]
    for part in range(NODES // chunk):
        part_copy(part).start()
    for copy in copies:
        copy.start()

    def step(part, carry):
        part_copy(part).wait()
        at = pl.ds(pl.multiple_of(part * chunk, chunk), chunk)
        planes = []
        for i in range(4):
            bars = []
            for j in range(4):
                four = [diag_ref[16 * i + 4 * j + k, at].astype(F32) for k in range(4)]
                bars.append(contract(four, line))
            sheet = [contract([bars[j][k] for j in range(4)], line) for k in range(3)]
            planes.append([sheet[k][j] for j in range(3) for k in range(3)])
        for rest in range(9):
            made = contract([planes[i][rest] for i in range(4)], line)
            for i in range(3):
                high, low = halves(made[i])
                high_ref[9 * i + rest, at] = high
                low_ref[9 * i + rest, at] = low
        return carry

    lax.fori_loop(0, NODES // chunk, step, 0)
    high_ref[COARSE] = jnp.zeros((NODES, count), BF16)
    low_ref[COARSE] = jnp.zeros((NODES, count), BF16)
    full_ref[...] = jnp.zeros(full_ref.shape, F32)
    for copy in copies[:3]:
        copy.wait()
    padded = table_ref.shape[0] // 2
    table = table_ref[...]
    for part in range(high_ref.shape[0] // GROUP):
        high = high_ref[GROUP * part : GROUP * part + GROUP].reshape(GROUP * NODES, count)
        low = low_ref[GROUP * part : GROUP * part + GROUP].reshape(GROUP * NODES, count)
        both = dot(table, high, NN)
        made = both[:padded] + both[padded:] + dot(table[:padded], low, NN)
        full_ref[GROUP * COARSE * part : GROUP * COARSE * part + padded] = made
    full_ref[COARSE * COARSE : COARSE * COARSE + 1] = (slot_ref[...] + 1).astype(F32)
    local = full_ref[...].astype(BF16)
    local_ref[...] = local
    owner = owner_ref[...]
    rank = rank_row(owner, staying, owner_count)
    target = jnp.where(lanes(owner.shape) >= staying, owner * capacity + rank, -1)
    shape = (owner_count * capacity, count)
    send_ref[...] = dot(one_hot(rows(shape) == target), local, NT).astype(BF16)
    pairs = [(send_ref, send_out), (local_ref, local_out), (partial_ref, partial_out), (message_ref, message_out)]
    out = [pltpu.make_async_copy(src, dst, out_sem.at[i]) for i, (src, dst) in enumerate(pairs)]
    out[0].start()
    out[1].start()
    for copy in copies[3:8]:
        copy.wait()
    first_half(
        start_ref, rhs_ref, diag_ref, precond_ref, lift_ref, neighbour_ref, orient_ref, (owner, rank),
        partial_ref, message_ref, copies[8].wait,
    )
    out[2].start()
    out[3].start()
    for copy in out:
        copy.wait()


def block_sum(made, height, width):
    total = made[0:height, 0:width]
    for g in range(1, GROUP):
        total = total + made[height * g : height * g + height, width * g : width * g + width]
    return total


def operator_kernel(staying, got_ref, local_ref, facts_ref, op_ref, hits_ref):
    aggregates = op_ref.shape[0]
    count = local_ref.shape[1]
    owners, capacity, _ = got_ref.shape
    got = got_ref[...].reshape(owners * capacity, got_ref.shape[2])
    ids = got[:, COARSE * COARSE : COARSE * COARSE + 1].astype(F32)
    shape = (ids.shape[0], aggregates)
    hits = jnp.where(ids == (lanes(shape) + 1).astype(F32), 1.0, 0.0)
    stay = stay_hits(facts_ref, staying, aggregates)
    total = dot(hits.astype(BF16), got, TN) + dot(stay, local_ref[...], NT)
    op_ref[...] = total[:, : COARSE * COARSE]
    depth = capacity // GROUP
    hits = hits.reshape(owners, GROUP, depth, aggregates)
    hits_ref[...] = jnp.concatenate(
        [hits[:, g].reshape(owners * depth, aggregates) for g in range(GROUP)], 1
    ).astype(BF16)


def stay_hits(facts_ref, staying, aggregates):
    slot = facts_ref[4:5]
    shape = (aggregates, slot.shape[1])
    return one_hot((rows(shape) == slot) & (lanes(shape) < staying))


def last_kernel(staying, pos_ref, got_ref, hits_ref, rest_ref, facts_ref, edge_ref, out_ref):
    pos = pos_ref[0]
    owners, slabs, depth, width = got_ref.shape
    aggregates = out_ref.shape[1]
    count = rest_ref.shape[1]
    edge = count // 4
    hits = hits_ref[...]
    main = got_ref[:, pl.ds(pos, 1)].astype(F32).reshape(owners * depth, width).astype(BF16)
    side = got_ref[:, pl.ds(jnp.minimum(pos + 1, slabs - 1), 1)]
    side = jnp.where(pos < slabs - 1, side.astype(F32).reshape(owners * depth, width), 0.0).astype(BF16)
    main = block_sum(dot(main, hits, TN), width // GROUP, aggregates)
    side = block_sum(dot(side, hits, TN), width // GROUP, aggregates)[0:16]

    rim = got_ref[pl.ds(pos_ref[1], 1), pl.ds(jnp.maximum(pos - 1, 0), 1), 0:8]
    rim = jnp.where(pos > 0, rim.astype(F32).reshape(8, width), 0.0)
    rim = jnp.concatenate([rim, pltpu.roll(rim, count - edge, 1)], 0)
    rim = jnp.where(lanes(rim.shape) < edge, turn(rim, facts_ref[3:4]), 0.0)
    rest = rest_ref[...] + dot_split(halves(edge_ref[0:16]), halves(rim), TN)
    nodes = dot(rest.astype(BF16), stay_hits(facts_ref, staying, aggregates), NT)
    nodes = nodes + dot_split(halves(edge_ref[16:32]), halves(side), TN)
    made = dot_split(halves(small_table()), halves(nodes), NN)
    out_ref[...] = (made + main)[:COARSE]


def call(kernel, outs, args, spaces, out_spaces=None, scratch=(), flops=0, limit=VMEM_LIMIT):
    bytes_in = sum(a.size * a.dtype.itemsize for a in args)
    bytes_out = sum(o.size * o.dtype.itemsize for o in outs)
    out_spaces = out_spaces or [pltpu.VMEM] * len(outs)
    return pl.pallas_call(
        kernel,
        out_shape=tuple(outs),
        in_specs=[pl.BlockSpec(memory_space=space) for space in spaces],
        out_specs=tuple(pl.BlockSpec(memory_space=space) for space in out_spaces),
        scratch_shapes=list(scratch),
        compiler_params=pltpu.CompilerParams(vmem_limit_bytes=limit),
        cost_estimate=pl.CostEstimate(
            flops=flops, bytes_accessed=bytes_in + bytes_out, transcendentals=0
        ),
    )(*args)


def struct(shape, dtype):
    return jax.ShapeDtypeStruct(shape, dtype)


def block_table(table, copies, row_step):
    out = []
    for part in split_table(table):
        full = np.zeros((ceil_to(copies * table.shape[0], row_step), copies * table.shape[1]), BF16)
        for copy in range(copies):
            full[
                copy * table.shape[0] : (copy + 1) * table.shape[0],
                copy * table.shape[1] : (copy + 1) * table.shape[1],
            ] = part
        out.append(full)
    return np.concatenate(out, 0)


def per_device(start, rhs, diag_block, precond, lift, neighbour, orient, owner, slot):
    count = start.shape[1]
    staying = count // 4
    aggregates = count // 2
    owner_count = lax.axis_size("dom")
    slabs = lax.axis_size("face")
    movers = count - staying
    capacity = 2 * ((movers + owner_count - 2) // (owner_count - 1))
    depth = ceil_to(-(-max(capacity, count // 4) // GROUP), 8)
    capacity = GROUP * depth
    total = owner_count * capacity
    entries = ceil_to(COARSE * COARSE + 1, 128)
    groups = -(-COARSE // GROUP)
    pos = jnp.stack([lax.axis_index("face"), lax.axis_index("dom")]).astype(jnp.int32)
    owner = owner.reshape(1, count)
    slot = slot.reshape(1, count)
    table = jnp.asarray(block_table(restrict_table(), GROUP, 16))

    args = [diag_block, slot, owner, table, start, rhs, lift, neighbour, orient, precond]
    outs = [
        struct((total, entries), BF16),
        struct((entries, count), BF16),
        struct((NODES, count), F32),
        struct((176, count), BF16),
    ]
    op_send, local_op, partial, message = call(
        lambda *refs: first_kernel(staying, owner_count, capacity, *refs),
        outs,
        args,
        [pl.ANY] * len(args),
        [pl.ANY] * len(outs),
        scratch=[pltpu.VMEM(each.shape, each.dtype) for each in args + outs]
        + [
            pltpu.VMEM((groups * GROUP, NODES, count), BF16),
            pltpu.VMEM((groups * GROUP, NODES, count), BF16),
            pltpu.VMEM((entries, count), F32),
            pltpu.SemaphoreType.DMA((NODES // 16,)),
            pltpu.SemaphoreType.DMA((9,)),
            pltpu.SemaphoreType.DMA((4,)),
        ],
        flops=200_000_000,
        limit=FIRST_LIMIT,
    )
    op_got = lax.all_to_all(
        op_send.reshape(owner_count, capacity, entries), "dom", split_axis=0, concat_axis=0, tiled=True
    )
    gathered = lax.all_gather(message, "face")
    sol, rest, rim, facts, edge = call(
        lambda *refs: middle_kernel(staying, capacity, *refs),
        [
            struct((NODES, count), F32),
            struct((NODES, count), F32),
            struct((16, count), F32),
            struct((8, count), jnp.int32),
            struct((32, NODES), F32),
        ],
        [pos, gathered, start, partial, rhs, diag_block, precond, lift, neighbour, orient, slot],
        [pltpu.SMEM] + [pltpu.VMEM] * 10,
        [pl.ANY] + [pltpu.VMEM] * 4,
        scratch=[
            pltpu.VMEM((NODES, count), F32),
            pltpu.VMEM((NODES, count), F32),
            pltpu.SemaphoreType.DMA(()),
        ],
        flops=200_000_000,
    )
    (send,) = call(
        send_kernel,
        [struct((owner_count, slabs, depth, 128), BF16)],
        [pos, rest, rim, facts, op_got],
        [pltpu.SMEM] + [pltpu.VMEM] * 3 + [pl.ANY],
        flops=100_000_000,
    )
    got = lax.all_to_all(
        send.reshape(owner_count * slabs, depth, 128), ("dom", "face"), split_axis=0, concat_axis=0, tiled=True
    ).reshape(owner_count, slabs, depth, 128)
    coarse_op, hits = call(
        lambda *refs: operator_kernel(staying, *refs),
        [
            struct((aggregates, COARSE * COARSE), F32),
            struct((owner_count * depth, GROUP * aggregates), BF16),
        ],
        [op_got, local_op, facts],
        [pltpu.VMEM] * 3,
        flops=100_000_000,
    )
    (coarse_rhs,) = call(
        lambda *refs: last_kernel(staying, *refs),
        [struct((COARSE, aggregates), F32)],
        [pos, got, hits, rest, facts, edge],
        [pltpu.SMEM] + [pltpu.VMEM] * 5,
        flops=100_000_000,
    )
    return (sol, coarse_op.T, coarse_rhs)


def solution(mesh):
    return jax.shard_map(
        per_device,
        mesh=mesh,
        in_specs=(
            P(None, ("dom", "face")),
            P(None, ("dom", "face")),
            P(None, None, ("dom", "face")),
            P(None, None, ("dom", "face")),
            P(),
            P(None, ("dom", "face")),
            P(None, ("dom", "face")),
            P(("dom", "face")),
            P(("dom", "face")),
        ),
        out_specs=(P(None, ("dom", "face")), P(None, ("dom", "face")), P(None, ("dom", "face"))),
        check_vma=False,
    )
```

```python
import jax
import jax.numpy as jnp
import numpy as np
from jax import lax
from jax.experimental import pallas as pl
from jax.experimental.pallas import tpu as pltpu
from jax.sharding import PartitionSpec as P

SWEEPS = 2
NODES = 64
COARSE = 27
FACES = 6
GROUP = 4
SPLIT = 23
F32 = jnp.float32
BF16 = jnp.bfloat16
VMEM_LIMIT = 24 * 1024 * 1024
FIRST_LIMIT = None

NN = (((1,), (0,)), ((), ()))
NT = (((1,), (1,)), ((), ()))
TN = (((0,), (0,)), ((), ()))


def restrict_line():
    fine = np.array([-1.0, -1.0 / np.sqrt(5.0), 1.0 / np.sqrt(5.0), 1.0])
    coarse = np.array([-1.0, 0.0, 1.0])
    basis = np.ones((4, 3))
    for column in range(3):
        for other in range(3):
            if other != column:
                basis[:, column] *= (fine - coarse[other]) / (coarse[column] - coarse[other])
    return basis.T


def restrict_table():
    line = restrict_line()
    return np.kron(np.kron(line, line), line)


def split_table(table):
    table = table.astype(np.float32)
    high = table.astype(BF16)
    low = (table - high.astype(np.float32)).astype(BF16)
    return high, low


def ceil_to(value, step):
    return -(-value // step) * step


def halves(values):
    high = values.astype(BF16)
    low = (values - high.astype(F32)).astype(BF16)
    return high, low


def dot(left, right, dims):
    return lax.dot_general(left, right, dims, preferred_element_type=F32)


def dot_split(left, right, dims):
    left_high, left_low = left
    right_high, right_low = right
    return (
        dot(left_high, right_high, dims)
        + dot(left_low, right_high, dims)
        + dot(left_high, right_low, dims)
    )


def small_table():
    shape = (32, NODES)
    line = restrict_line()
    row, col = rows(shape), lanes(shape)
    step = 9
    table = jnp.ones(shape, F32)
    left = row
    for digit in range(3):
        mine = (left >= step).astype(jnp.int32) + (left >= 2 * step).astype(jnp.int32)
        left = left - step * mine
        fine = (col >> (4 - 2 * digit)) & 3
        value = jnp.zeros(shape, F32)
        for i in range(3):
            for j in range(4):
                value = jnp.where((mine == i) & (fine == j), float(line[i, j]), value)
        table = table * value
        step //= 3
    return jnp.where(row < COARSE, table, 0.0)


def lanes(shape):
    return lax.broadcasted_iota(jnp.int32, shape, 1)


def rows(shape):
    return lax.broadcasted_iota(jnp.int32, shape, 0)


def face_traces(ref):
    return [
        ref[0:16],
        ref[48:64],
        jnp.concatenate([ref[16 * i : 16 * i + 4] for i in range(4)], 0),
        jnp.concatenate([ref[16 * i + 12 : 16 * i + 16] for i in range(4)], 0),
        ref[pl.ds(0, 16, stride=4)],
        ref[pl.ds(3, 16, stride=4)],
    ]


def take(values, index, axis):
    return jnp.take_along_axis(values, index, axis=axis, mode="promise_in_bounds")


def turn(values, orient_row):
    shape = values.shape
    orient = jnp.broadcast_to(orient_row, shape)
    place = rows(shape)
    first = (place >> 2) ^ ((orient & 1) * 3)
    second = (place & 3) ^ (((orient >> 1) & 1) * 3)
    flip = (orient & 4) > 0
    source = jnp.where(flip, 4 * second + first, 4 * first + second)
    out = []
    for half in (source[:8], source[8:]):
        within = half & 7
        out.append(jnp.where(half >= 8, take(values[8:], within, 0), take(values[:8], within, 0)))
    return jnp.concatenate(out, 0)


def pick(traces, neighbour_ref, face):
    values = traces[face ^ 1]
    count = values.shape[1]
    index = jnp.clip(neighbour_ref[face : face + 1] - (face ^ 1) * count, 0, count - 1)
    return take(values, jnp.broadcast_to(index, values.shape), 1)


def fold(parts):
    place = rows(parts[0].shape)
    step = 1
    while len(parts) > 1:
        even = (place & step) == 0
        parts = [
            jnp.where(even, x, y) + pltpu.roll(jnp.where(even, y, x), step, 0)
            for x, y in zip(parts[::2], parts[1::2])
        ]
        step *= 2
    return parts[0]


def apply_blocks(ref, values):
    count = values.shape[1]
    tiles = values.reshape(NODES // 8, 8, count)
    out = []
    for group in range(NODES // 8):
        parts = []
        for node in range(8 * group, 8 * group + 8):
            parts.append(jnp.sum(ref[node].astype(F32).reshape(NODES // 8, 8, count) * tiles, axis=0))
        out.append(fold(parts))
    return jnp.concatenate(out, 0)


def pack_rim(traces):
    shape = traces[2].shape
    return jnp.where(lanes(shape) < shape[1] // 2, traces[2], traces[3])


def coupling(traces, below, above, neighbour_ref, orient_ref, lift_ref):
    count = below.shape[1]
    edge = count // 4
    turned = []
    for face in range(FACES):
        values = pick(traces, neighbour_ref, face)
        if face == 2:
            values = jnp.where(lanes(values.shape) < edge, below, values)
        if face == 3:
            values = jnp.where(lanes(values.shape) >= count - edge, above, values)
        turned.append(turn(values, orient_ref[face : face + 1]))
    turned = jnp.concatenate(turned, 0)
    lift = lift_ref[...].reshape(FACES * 16, NODES)
    return dot_split(halves(lift), halves(turned), TN)


def edge_mask(shape):
    return (lanes(shape) < shape[1] // 4) | (lanes(shape) >= shape[1] - shape[1] // 4)


def low_mask(shape):
    return ((lanes(shape) // (shape[1] // 4)) & 1) == 0


def both_halves(shape, low, high):
    return jnp.where(lanes(shape) < shape[1] // 2, low, high)


def response(precond_ref, lift_ref):
    count = precond_ref.shape[2]
    parts = []
    for face in (2, 3):
        parts.extend(halves(lift_ref[face]))
    stack = jnp.concatenate(parts, 0)
    shape = (NODES, count)
    out = []
    for spot in range(16):
        node = 16 * (spot // 4) + spot % 4
        block = both_halves(shape, precond_ref[node].astype(F32), precond_ref[node + 12].astype(F32))
        made = dot(stack, block.astype(BF16), NN)
        out.append(
            both_halves((16, count), made[0:16] + made[16:32], made[32:48] + made[48:64])
        )
    return out


def halo_lift(below, above, orient_ref, lift_ref):
    shape = below.shape
    edge = shape[1] // 4
    low = jnp.where(lanes(shape) < edge, turn(below, orient_ref[2:3]), 0.0)
    high = jnp.where(lanes(shape) >= shape[1] - edge, turn(above, orient_ref[3:4]), 0.0)
    lift = lift_ref[2:4].reshape(32, NODES)
    return dot_split(halves(lift), halves(jnp.concatenate([low, high], 0)), TN)


START = 0
RHS = NODES
LIFT = 2 * NODES
NEIGHBOUR = LIFT + FACES * 16
ORIENT = NEIGHBOUR + 8
OWNER = ORIENT + 8
SLOT = OWNER + 1
PACKED = ORIENT + 16


class Packed:
    def __init__(self, ref):
        self.start = ref.at[START : START + NODES]
        self.rhs = ref.at[RHS : RHS + NODES]
        self.lift = ref[LIFT : LIFT + FACES * 16, 0:NODES].reshape(FACES, 16, NODES)
        self.neighbour = ref[NEIGHBOUR : NEIGHBOUR + FACES].astype(jnp.int32)
        self.orient = ref[ORIENT : ORIENT + FACES].astype(jnp.int32)
        self.owner = ref[OWNER : OWNER + 1].astype(jnp.int32)
        self.slot = ref[SLOT : SLOT + 1].astype(jnp.int32)


def smooth_kernel(
    staying, owner_count,
    diag_ref, precond_ref, pack_ref,
    message_ref, partial_ref,
):
    count = diag_ref.shape[2]
    packed = Packed(pack_ref)
    start_ref, rhs_ref = packed.start, packed.rhs
    lift_ref, neighbour_ref, orient_ref = packed.lift, packed.neighbour, packed.orient
    traces = face_traces(start_ref)
    shape = traces[2].shape
    none = jnp.zeros(shape, F32)
    coupled = coupling(traces, none, none, neighbour_ref, orient_ref, lift_ref)
    resid = rhs_ref[...] - (apply_blocks(diag_ref, start_ref[...]) - coupled)
    partial_ref[...] = start_ref[...] + apply_blocks(precond_ref, resid)
    direct = edge_mask(shape)
    reply = response(precond_ref, lift_ref)
    for spot in range(8):
        message_ref[48 + 16 * spot : 64 + 16 * spot] = jnp.where(
            direct, reply[spot], pltpu.roll(reply[spot + 8], count // 2, 1)
        ).astype(BF16)
    later = pack_rim(face_traces(partial_ref))
    high, low = halves(jnp.where(direct, pack_rim(traces), pltpu.roll(later, count // 2, 1)))
    message_ref[0:16] = high
    message_ref[16:32] = low
    orient = both_halves((1, count), orient_ref[2:3], orient_ref[3:4])
    owner = packed.owner
    rank = rank_row(owner, staying, owner_count)
    place = rows(shape)
    facts = jnp.where(place < 4, orient, jnp.where(place < 8, owner, rank))
    message_ref[32:48] = facts.astype(F32).astype(BF16)


def merged(gathered_ref, at):
    slabs = gathered_ref.shape[0]
    pos = lax.axis_index("face")
    above = gathered_ref[jnp.minimum(pos + 1, slabs - 1), at].astype(F32)
    below = gathered_ref[jnp.maximum(pos - 1, 0), at].astype(F32)
    above = jnp.where(pos < slabs - 1, above, 0.0)
    below = jnp.where(pos > 0, below, 0.0)
    return jnp.where(low_mask(above.shape), above, below)


def aside(values):
    count = values.shape[1]
    return pltpu.roll(values, count // 4, 1), pltpu.roll(values, count - count // 4, 1)


def target_of(facts, staying, capacity):
    owner = facts[4:5].astype(jnp.int32)
    rank = facts[8:9].astype(jnp.int32)
    return jnp.where(lanes(owner.shape) >= staying, owner * capacity + rank, -1)


def middle_kernel(
    staying, capacity,
    gathered_ref, diag_ref, precond_ref, pack_ref, partial_ref,
    out_ref, rest_ref, rim_ref, facts_ref, edge_ref, sol_ref, new_ref, sem,
):
    count = diag_ref.shape[2]
    shape = (16, count)
    pos = lax.axis_index("face")
    packed = Packed(pack_ref)
    rhs_ref, slot = packed.rhs, packed.slot
    lift_ref, neighbour_ref, orient_ref = packed.lift, packed.neighbour, packed.orient
    head = merged(gathered_ref, pl.ds(0, 16)) + merged(gathered_ref, pl.ds(16, 16))
    known = merged(gathered_ref, pl.ds(32, 16))
    orient = known[0:1].astype(jnp.int32)
    own = gathered_ref[pos, pl.ds(0, 16)].astype(F32) + gathered_ref[pos, pl.ds(16, 16)].astype(F32)
    from_high, from_low = aside(own)
    sent = turn(both_halves(shape, from_high, from_low), orient)
    below, above = aside(head)
    delta = halo_lift(below, above, orient_ref, lift_ref)
    sol_ref[...] = partial_ref[...] + apply_blocks(precond_ref, delta)
    later = pltpu.roll(head, count // 2, 1)
    reply = []
    for spot in range(8):
        block = merged(gathered_ref, pl.ds(48 + 16 * spot, 16))
        reply.append((block, pltpu.roll(block, count // 2, 1)))
    reply = [pair[0] for pair in reply] + [pair[1] for pair in reply]
    change = [block * sent for block in reply]
    change = [block[:8] + block[8:] for block in change]
    change = jnp.concatenate([fold(change[:8]), fold(change[8:])], 0)
    below, above = aside(later + change)
    traces = face_traces(sol_ref)
    coupled = coupling(traces, below, above, neighbour_ref, orient_ref, lift_ref)
    resid = rhs_ref[...] - (apply_blocks(diag_ref, sol_ref[...]) - coupled)
    new_ref[...] = sol_ref[...] + apply_blocks(precond_ref, resid)
    copy = pltpu.make_async_copy(new_ref, out_ref, sem)
    copy.start()
    traces = face_traces(new_ref)
    none = jnp.zeros(shape, F32)
    coupled = coupling(traces, none, none, neighbour_ref, orient_ref, lift_ref)
    rest_ref[...] = rhs_ref[...] - (apply_blocks(diag_ref, new_ref[...]) - coupled)
    rim_ref[...] = pack_rim(traces)
    mine = gathered_ref[pos, pl.ds(32, 16)].astype(F32)
    target = jnp.where(
        lanes((1, count)) >= count - count // 4, target_of(known, staying, capacity), -1
    )
    place = rows((8, count))
    facts = jnp.where(place == 0, orient, target)
    facts = jnp.where(place == 2, target_of(mine, staying, capacity), facts)
    facts = jnp.where(place == 3, orient_ref[2:3], facts)
    facts_ref[...] = jnp.where(place == 4, slot, facts)
    edge_ref[...] = lift_ref[2:4].reshape(32, NODES)
    copy.wait()


def spread(values, copies):
    none = jnp.zeros(values.shape, values.dtype)
    return jnp.concatenate(
        [
            jnp.concatenate([values if i == j else none for j in range(copies)], 1)
            for i in range(copies)
        ],
        0,
    )


def packed_by_target(values, target, owners, depth):
    count = values.shape[1]
    shape = (owners * depth, count)
    place = rows(shape)
    base = (place // depth) * (GROUP * depth) + place % depth
    hits = jnp.concatenate([one_hot(base + depth * g == target) for g in range(GROUP)], 1)
    made = dot(hits, spread(values, GROUP), NT)
    return made.reshape(owners, depth, GROUP * values.shape[0])


def send_kernel(rest_ref, rim_ref, facts_ref, after_ref, send_ref):
    pos = lax.axis_index("face")
    count = rest_ref.shape[1]
    edge = count // 4
    owners, slabs, depth, _ = send_ref.shape
    high, low = halves(rest_ref[...])
    keep = lanes(low.shape) >= count - edge
    low = jnp.where(keep, low.astype(F32), 0.0).astype(BF16)
    made = dot_split(halves(small_table()), (high, low), NN)
    send_ref[...] = jnp.zeros(send_ref.shape, BF16)
    ours = packed_by_target(made.astype(BF16), facts_ref[2:3], owners, depth)
    send_ref[:, pl.ds(pos, 1)] = ours.astype(BF16)[:, None]
    moved_up, moved_down = aside(rim_ref[...])

    @pl.when(pos > 0)
    def _():
        turned = turn(moved_down, facts_ref[0:1])
        turned = jnp.concatenate([turned, jnp.zeros(turned.shape, F32)], 0).astype(BF16)
        theirs = packed_by_target(turned, facts_ref[1:2], owners, depth)
        send_ref[:, pl.ds(pos - 1, 1)] = theirs.astype(BF16)[:, None]

    @pl.when(pos < slabs - 1)
    def _():
        group = lanes((8, count)) // edge
        rim = jnp.where(group == 0, moved_up[0:8], pltpu.roll(moved_up[8:16], edge, 1))
        send_ref[pl.ds(lax.axis_index("dom"), 1), pl.ds(pos + 1, 1), 0:8] = rim.astype(BF16)[None, None]


def rank_row(owner_row, staying, owner_count):
    count = owner_row.shape[1]
    shape = (owner_count, count)
    hits = (rows(shape) == owner_row) & (lanes(shape) >= staying)
    hits = jnp.where(hits, 1.0, 0.0)
    before = jnp.where(rows((count, count)) < lanes((count, count)), 1.0, 0.0)
    earlier = dot(hits.astype(BF16), before.astype(BF16), NN)
    return jnp.sum(hits * earlier, axis=0, keepdims=True).astype(jnp.int32)


def one_hot(condition):
    return jnp.where(condition, 1.0, 0.0).astype(BF16)


def contract(four, line):
    first, second = float(line[0, 1]), float(line[0, 2])
    middle = float(line[1, 1])
    return [
        four[0] + first * four[1] + second * four[2],
        middle * (four[1] + four[2]),
        four[3] + second * four[1] + first * four[2],
    ]


def galerkin_kernel(
    staying, owner_count, capacity,
    diag_in, slot_in, owner_in, table_in, start_in, rhs_in, lift_in, neighbour_in, orient_in,
    precond_in,
    send_out, local_out, pack_out,
    diag_ref, slot_ref, owner_ref, table_ref, lift_ref, neighbour_ref, orient_ref,
    send_ref, local_ref, pack_ref,
    high_ref, low_ref, full_ref, part_sem, sem, out_sem,
):
    line = restrict_line()
    count = diag_ref.shape[2]
    chunk = 16

    def part_copy(part):
        at = pl.ds(pl.multiple_of(part * chunk, chunk), chunk)
        return pltpu.make_async_copy(diag_in.at[:, at], diag_ref.at[:, at], part_sem.at[part])

    pairs = [
        (slot_in, slot_ref), (owner_in, owner_ref), (table_in, table_ref),
        (start_in, pack_ref.at[START : START + NODES]), (rhs_in, pack_ref.at[RHS : RHS + NODES]),
        (lift_in, lift_ref), (neighbour_in, neighbour_ref), (orient_in, orient_ref),
    ]
    copies = [pltpu.make_async_copy(src, dst, sem.at[i]) for i, (src, dst) in enumerate(pairs)]
    for part in range(NODES // chunk):
        part_copy(part).start()
    for copy in copies:
        copy.start()
    high_ref[COARSE] = jnp.zeros((NODES, count), BF16)
    low_ref[COARSE] = jnp.zeros((NODES, count), BF16)
    full_ref[...] = jnp.zeros(full_ref.shape, F32)

    def step(part, carry):
        part_copy(part).wait()
        at = pl.ds(pl.multiple_of(part * chunk, chunk), chunk)
        planes = []
        for i in range(4):
            bars = []
            for j in range(4):
                four = [diag_ref[16 * i + 4 * j + k, at].astype(F32) for k in range(4)]
                bars.append(contract(four, line))
            sheet = [contract([bars[j][k] for j in range(4)], line) for k in range(3)]
            planes.append([sheet[k][j] for j in range(3) for k in range(3)])
        for rest in range(9):
            made = contract([planes[i][rest] for i in range(4)], line)
            for i in range(3):
                high, low = halves(made[i])
                high_ref[9 * i + rest, at] = high
                low_ref[9 * i + rest, at] = low
        return carry

    lax.fori_loop(0, NODES // chunk, step, 0)
    for copy in copies:
        copy.wait()
    pack_ref[LIFT : LIFT + FACES * 16, 0:NODES] = lift_ref[...].reshape(FACES * 16, NODES)
    pack_ref[NEIGHBOUR : NEIGHBOUR + FACES] = neighbour_ref[...].astype(F32)
    pack_ref[ORIENT : ORIENT + FACES] = orient_ref[...].astype(F32)
    pack_ref[OWNER : OWNER + 1] = owner_ref[...].astype(F32)
    pack_ref[SLOT : SLOT + 1] = slot_ref[...].astype(F32)
    pack_copy = pltpu.make_async_copy(pack_ref, pack_out, out_sem.at[2])
    pack_copy.start()
    padded = table_ref.shape[0] // 2
    table = table_ref[...]
    step_rows = GROUP * COARSE
    cut = SPLIT * COARSE
    for part in range(high_ref.shape[0] // GROUP):
        high = high_ref[GROUP * part : GROUP * part + GROUP].reshape(GROUP * NODES, count)
        low = low_ref[GROUP * part : GROUP * part + GROUP].reshape(GROUP * NODES, count)
        both = dot(table, high, NN)
        made = both[:padded] + both[padded:] + dot(table[:padded], low, NN)
        first, last = step_rows * part, min(step_rows * part + step_rows, COARSE * COARSE)
        if first < cut:
            end = min(cut, last)
            full_ref[first:end] = made[: end - first]
        if last > cut:
            begin = max(cut, first)
            to = 5 * 128 + begin - cut
            full_ref[to : to + last - begin] = made[begin - first : last - first]
    slot = (slot_ref[...] + 1).astype(F32)
    full_ref[5 * 128 - 1 : 5 * 128] = slot
    full_ref[6 * 128 - 1 : 6 * 128] = slot
    local = full_ref[...].astype(BF16)
    local_ref[...] = local
    local_copy = pltpu.make_async_copy(local_ref, local_out, out_sem.at[0])
    local_copy.start()
    owner = owner_ref[...]
    rank = rank_row(owner, staying, owner_count)
    target = jnp.where(lanes(owner.shape) >= staying, owner * capacity + rank, -1)
    twice = jnp.concatenate([target, target], 1)
    shape = (2 * capacity, 2 * count)
    upper = (rows(shape) >= capacity).astype(jnp.int32)
    place = rows(shape) - capacity * upper
    place = jnp.where(upper == (lanes(shape) >= count).astype(jnp.int32), place, -2 * owner_count * capacity)
    hits = jnp.concatenate([one_hot(place + capacity * o == twice) for o in range(owner_count)], 0)
    for pair in range(3):
        wide = jnp.concatenate([local[256 * pair : 256 * pair + 128], local[256 * pair + 128 : 256 * pair + 256]], 1)
        made = dot(hits, wide, NT)
        made = made.reshape(owner_count, 2 * capacity, 128).astype(BF16)
        send_ref[:, 2 * capacity * pair : 2 * capacity * pair + 2 * capacity] = made
    send_copy = pltpu.make_async_copy(send_ref, send_out, out_sem.at[1])
    send_copy.start()
    pack_copy.wait()
    local_copy.wait()
    send_copy.wait()


def block_sum(made, height, width):
    total = made[0:height, 0:width]
    for g in range(1, GROUP):
        total = total + made[height * g : height * g + height, width * g : width * g + width]
    return total


def operator_kernel(staying, got_ref, local_ref, facts_ref, op_ref, hits_ref):
    aggregates = op_ref.shape[0]
    owners, size, count = got_ref.shape
    both = size // 3
    capacity = both // 2
    ids = got_ref[:, 2 * both : size].astype(F32).reshape(owners * both, count)[:, count - 1 : count]
    shape = (owners * both, 2 * aggregates)
    column = lanes(shape)
    column = jnp.where(column >= aggregates, column - aggregates, column)
    hits = jnp.where(ids == (column + 1).astype(F32), 1.0, 0.0).reshape(owners, both, 2 * aggregates)
    shape = (owners, both, 2 * aggregates)
    upper = lax.broadcasted_iota(jnp.int32, shape, 1) >= capacity
    right = lax.broadcasted_iota(jnp.int32, shape, 2) >= aggregates
    paired = jnp.where(upper == right, hits, 0.0).reshape(owners * both, 2 * aggregates).astype(BF16)
    stay = stay_hits(facts_ref, staying, aggregates)
    out = []
    for pair in range(3):
        block = got_ref[:, both * pair : both * pair + both].astype(F32).reshape(owners * both, count).astype(BF16)
        total = dot(paired, block, TN)
        for side in range(2):
            at = 128 * (2 * pair + side)
            out.append(
                total[aggregates * side : aggregates * side + aggregates] + dot(stay, local_ref[at : at + 128], NT)
            )
    cut = SPLIT * COARSE
    for block in range(4):
        op_ref[:, 128 * block : 128 * block + 128] = out[block]
    op_ref[:, 512:cut] = out[4][:, : cut - 512]
    op_ref[:, cut:] = out[5][:, : COARSE * COARSE - cut]
    depth = hits_ref.shape[0] // owners
    parts = []
    for g in range(GROUP):
        part = hits[:, depth * g : depth * g + depth] if depth * g + depth <= both else None
        if part is None:
            part = jnp.zeros((owners, depth, 2 * aggregates), F32)
        parts.append(part.reshape(owners * depth, 2 * aggregates)[:, :aggregates])
    hits_ref[...] = jnp.concatenate(parts, 1).astype(BF16)


def stay_hits(facts_ref, staying, aggregates):
    slot = facts_ref[4:5]
    shape = (aggregates, slot.shape[1])
    return one_hot((rows(shape) == slot) & (lanes(shape) < staying))


def last_kernel(staying, got_ref, hits_ref, rest_ref, facts_ref, edge_ref, out_ref):
    pos = lax.axis_index("face")
    owners, slabs, depth, width = got_ref.shape
    aggregates = out_ref.shape[1]
    count = rest_ref.shape[1]
    edge = count // 4
    hits = hits_ref[...]
    main = got_ref[:, pl.ds(pos, 1)].astype(F32).reshape(owners * depth, width).astype(BF16)
    side = got_ref[:, pl.ds(jnp.minimum(pos + 1, slabs - 1), 1)]
    side = jnp.where(pos < slabs - 1, side.astype(F32).reshape(owners * depth, width), 0.0).astype(BF16)
    main = block_sum(dot(main, hits, TN), width // GROUP, aggregates)
    side = block_sum(dot(side, hits, TN), width // GROUP, aggregates)[0:16]

    rim = got_ref[pl.ds(lax.axis_index("dom"), 1), pl.ds(jnp.maximum(pos - 1, 0), 1), 0:8]
    rim = jnp.where(pos > 0, rim.astype(F32).reshape(8, width), 0.0)
    rim = jnp.concatenate([rim, pltpu.roll(rim, count - edge, 1)], 0)
    rim = jnp.where(lanes(rim.shape) < edge, turn(rim, facts_ref[3:4]), 0.0)
    rest = rest_ref[...] + dot_split(halves(edge_ref[0:16]), halves(rim), TN)
    nodes = dot(rest.astype(BF16), stay_hits(facts_ref, staying, aggregates), NT)
    nodes = nodes + dot_split(halves(edge_ref[16:32]), halves(side), TN)
    made = dot_split(halves(small_table()), halves(nodes), NN)
    out_ref[...] = (made + main)[:COARSE]


def call(kernel, outs, args, spaces, out_spaces=None, scratch=(), flops=0, limit=VMEM_LIMIT):
    bytes_in = sum(a.size * a.dtype.itemsize for a in args)
    bytes_out = sum(o.size * o.dtype.itemsize for o in outs)
    out_spaces = out_spaces or [pltpu.VMEM] * len(outs)
    return pl.pallas_call(
        kernel,
        out_shape=tuple(outs),
        in_specs=[pl.BlockSpec(memory_space=space) for space in spaces],
        out_specs=tuple(pl.BlockSpec(memory_space=space) for space in out_spaces),
        scratch_shapes=list(scratch),
        compiler_params=pltpu.CompilerParams(vmem_limit_bytes=limit),
        cost_estimate=pl.CostEstimate(
            flops=flops, bytes_accessed=bytes_in + bytes_out, transcendentals=0
        ),
    )(*args)


def struct(shape, dtype):
    return jax.ShapeDtypeStruct(shape, dtype)


def block_table(table, copies, row_step):
    out = []
    for part in split_table(table):
        full = np.zeros((ceil_to(copies * table.shape[0], row_step), copies * table.shape[1]), BF16)
        for copy in range(copies):
            full[
                copy * table.shape[0] : (copy + 1) * table.shape[0],
                copy * table.shape[1] : (copy + 1) * table.shape[1],
            ] = part
        out.append(full)
    return np.concatenate(out, 0)


def per_device(start, rhs, diag_block, precond, lift, neighbour, orient, owner, slot):
    count = start.shape[1]
    staying = count // 4
    aggregates = count // 2
    owner_count = lax.axis_size("dom")
    slabs = lax.axis_size("face")
    movers = count - staying
    capacity = 2 * ((movers + owner_count - 2) // (owner_count - 1))
    depth = ceil_to(-(-max(capacity, count // 4) // GROUP), 8)
    places = GROUP * depth
    capacity = ceil_to(capacity, 4)
    chunk = 6 * capacity
    entries = 6 * 128
    groups = -(-COARSE // GROUP)
    owner = owner.reshape(1, count)
    slot = slot.reshape(1, count)
    table = jnp.asarray(block_table(restrict_table(), GROUP, 16))

    args = [diag_block, slot, owner, table, start, rhs, lift, neighbour, orient, precond]
    outs = [
        struct((owner_count, chunk, 128), BF16),
        struct((entries, count), BF16),
        struct((PACKED, count), F32),
    ]
    held = [each for each in args if each is not start and each is not rhs and each is not precond]
    op_send, local_op, pack = call(
        lambda *refs: galerkin_kernel(staying, owner_count, capacity, *refs),
        outs,
        args,
        [pl.ANY] * len(args),
        [pl.ANY] * len(outs),
        scratch=[pltpu.VMEM(each.shape, each.dtype) for each in held + outs]
        + [
            pltpu.VMEM((groups * GROUP, NODES, count), BF16),
            pltpu.VMEM((groups * GROUP, NODES, count), BF16),
            pltpu.VMEM((entries, count), F32),
            pltpu.SemaphoreType.DMA((NODES // 16,)),
            pltpu.SemaphoreType.DMA((8,)),
            pltpu.SemaphoreType.DMA((3,)),
        ],
        flops=200_000_000,
        limit=FIRST_LIMIT,
    )
    op_got = lax.all_to_all(op_send, "dom", split_axis=0, concat_axis=0, tiled=True)
    message, partial = call(
        lambda *refs: smooth_kernel(staying, owner_count, *refs),
        [struct((176, count), BF16), struct((NODES, count), F32)],
        [diag_block, precond, pack],
        [pltpu.VMEM] * 3,
        flops=100_000_000,
    )
    gathered = lax.all_gather(message, "face")
    sol, rest, rim, facts, edge = call(
        lambda *refs: middle_kernel(staying, places, *refs),
        [
            struct((NODES, count), F32),
            struct((NODES, count), F32),
            struct((16, count), F32),
            struct((8, count), jnp.int32),
            struct((32, NODES), F32),
        ],
        [gathered, diag_block, precond, pack, partial],
        [pltpu.VMEM] * 5,
        [pl.ANY] + [pltpu.VMEM] * 4,
        scratch=[
            pltpu.VMEM((NODES, count), F32),
            pltpu.VMEM((NODES, count), F32),
            pltpu.SemaphoreType.DMA(()),
        ],
        flops=200_000_000,
    )
    (send,) = call(
        send_kernel,
        [struct((owner_count, slabs, depth, 128), BF16)],
        [rest, rim, facts, op_got],
        [pltpu.VMEM] * 3 + [pl.ANY],
        flops=100_000_000,
    )
    got = lax.all_to_all(
        send.reshape(owner_count * slabs, depth, 128), ("dom", "face"), split_axis=0, concat_axis=0, tiled=True
    ).reshape(owner_count, slabs, depth, 128)
    coarse_op, hits = call(
        lambda *refs: operator_kernel(staying, *refs),
        [
            struct((aggregates, COARSE * COARSE), F32),
            struct((owner_count * depth, GROUP * aggregates), BF16),
        ],
        [op_got, local_op, facts],
        [pltpu.VMEM] * 3,
        flops=100_000_000,
    )
    (coarse_rhs,) = call(
        lambda *refs: last_kernel(staying, *refs),
        [struct((COARSE, aggregates), F32)],
        [got, hits, rest, facts, edge],
        [pltpu.VMEM] * 5,
        flops=100_000_000,
    )
    return (sol, coarse_op.T, coarse_rhs)


def solution(mesh):
    return jax.shard_map(
        per_device,
        mesh=mesh,
        in_specs=(
            P(None, ("dom", "face")),
            P(None, ("dom", "face")),
            P(None, None, ("dom", "face")),
            P(None, None, ("dom", "face")),
            P(),
            P(None, ("dom", "face")),
            P(None, ("dom", "face")),
            P(("dom", "face")),
            P(("dom", "face")),
        ),
        out_specs=(P(None, ("dom", "face")), P(None, ("dom", "face")), P(None, ("dom", "face"))),
        check_vma=False,
    )
```

```python
import jax
import jax.numpy as jnp
import numpy as np
from jax import lax
from jax.experimental import pallas as pl
from jax.experimental.pallas import tpu as pltpu
from jax.sharding import PartitionSpec as P

SWEEPS = 2
NODES = 64
COARSE = 27
FACES = 6
GROUP = 4
SPLIT = 23
F32 = jnp.float32
BF16 = jnp.bfloat16
VMEM_LIMIT = 24 * 1024 * 1024
FIRST_LIMIT = None

NN = (((1,), (0,)), ((), ()))
NT = (((1,), (1,)), ((), ()))
TN = (((0,), (0,)), ((), ()))


def restrict_line():
    fine = np.array([-1.0, -1.0 / np.sqrt(5.0), 1.0 / np.sqrt(5.0), 1.0])
    coarse = np.array([-1.0, 0.0, 1.0])
    basis = np.ones((4, 3))
    for column in range(3):
        for other in range(3):
            if other != column:
                basis[:, column] *= (fine - coarse[other]) / (coarse[column] - coarse[other])
    return basis.T


def restrict_table():
    line = restrict_line()
    return np.kron(np.kron(line, line), line)


def split_table(table):
    table = table.astype(np.float32)
    high = table.astype(BF16)
    low = (table - high.astype(np.float32)).astype(BF16)
    return high, low


def ceil_to(value, step):
    return -(-value // step) * step


def halves(values):
    high = values.astype(BF16)
    low = (values - high.astype(F32)).astype(BF16)
    return high, low


def dot(left, right, dims):
    return lax.dot_general(left, right, dims, preferred_element_type=F32)


def dot_split(left, right):
    left_high, left_low = halves(left)
    right_high, right_low = right
    size = left.shape[0]
    both = dot(jnp.concatenate([left_high, left_low], 0), right_high, NN)
    return both[:size] + both[size:] + dot(left_high, right_low, NN)


def small_table():
    shape = (32, NODES)
    line = restrict_line()
    row, col = rows(shape), lanes(shape)
    step = 9
    table = jnp.ones(shape, F32)
    left = row
    for digit in range(3):
        mine = (left >= step).astype(jnp.int32) + (left >= 2 * step).astype(jnp.int32)
        left = left - step * mine
        fine = (col >> (4 - 2 * digit)) & 3
        value = jnp.zeros(shape, F32)
        for i in range(3):
            for j in range(4):
                value = jnp.where((mine == i) & (fine == j), float(line[i, j]), value)
        table = table * value
        step //= 3
    return jnp.where(row < COARSE, table, 0.0)


def lanes(shape):
    return lax.broadcasted_iota(jnp.int32, shape, 1)


def rows(shape):
    return lax.broadcasted_iota(jnp.int32, shape, 0)


def face_traces(ref):
    return [
        ref[0:16],
        ref[48:64],
        jnp.concatenate([ref[16 * i : 16 * i + 4] for i in range(4)], 0),
        jnp.concatenate([ref[16 * i + 12 : 16 * i + 16] for i in range(4)], 0),
        ref[pl.ds(0, 16, stride=4)],
        ref[pl.ds(3, 16, stride=4)],
    ]


def take(values, index, axis):
    return jnp.take_along_axis(values, index, axis=axis, mode="promise_in_bounds")


def turn(values, orient_row):
    shape = values.shape
    orient = jnp.broadcast_to(orient_row, shape)
    place = rows(shape)
    first = (place >> 2) ^ ((orient & 1) * 3)
    second = (place & 3) ^ (((orient >> 1) & 1) * 3)
    flip = (orient & 4) > 0
    source = jnp.where(flip, 4 * second + first, 4 * first + second)
    out = []
    for half in (source[:8], source[8:]):
        within = half & 7
        out.append(jnp.where(half >= 8, take(values[8:], within, 0), take(values[:8], within, 0)))
    return jnp.concatenate(out, 0)


def pick(traces, neighbour_ref, face):
    values = traces[face ^ 1]
    count = values.shape[1]
    index = jnp.clip(neighbour_ref[face : face + 1] - (face ^ 1) * count, 0, count - 1)
    return take(values, jnp.broadcast_to(index, values.shape), 1)


def fold(parts):
    place = rows(parts[0].shape)
    step = 1
    while len(parts) > 1:
        even = (place & step) == 0
        parts = [
            jnp.where(even, x, y) + pltpu.roll(jnp.where(even, y, x), step, 0)
            for x, y in zip(parts[::2], parts[1::2])
        ]
        step *= 2
    return parts[0]


def apply_blocks(ref, values):
    count = values.shape[1]
    tiles = values.reshape(NODES // 8, 8, count)
    out = []
    for group in range(NODES // 8):
        parts = []
        for node in range(8 * group, 8 * group + 8):
            parts.append(jnp.sum(ref[node].astype(F32).reshape(NODES // 8, 8, count) * tiles, axis=0))
        out.append(fold(parts))
    return jnp.concatenate(out, 0)


def pack_rim(traces):
    shape = traces[2].shape
    return jnp.where(lanes(shape) < shape[1] // 2, traces[2], traces[3])


def coupling(traces, below, above, neighbour_ref, orient_ref, lift):
    count = below.shape[1]
    edge = count // 4
    turned = []
    for face in range(FACES):
        values = pick(traces, neighbour_ref, face)
        if face == 2:
            values = jnp.where(lanes(values.shape) < edge, below, values)
        if face == 3:
            values = jnp.where(lanes(values.shape) >= count - edge, above, values)
        turned.append(turn(values, orient_ref[face : face + 1]))
    turned = jnp.concatenate(turned + [jnp.zeros((count - FACES * 16, count), F32)], 0)
    return dot_split(lift, halves(turned))


def edge_mask(shape):
    return (lanes(shape) < shape[1] // 4) | (lanes(shape) >= shape[1] - shape[1] // 4)


def low_mask(shape):
    return ((lanes(shape) // (shape[1] // 4)) & 1) == 0


def both_halves(shape, low, high):
    return jnp.where(lanes(shape) < shape[1] // 2, low, high)


def response(precond_ref, edge):
    count = precond_ref.shape[2]
    parts = []
    for lift in (edge[0:16], edge[16:32]):
        parts.extend(halves(lift))
    stack = jnp.concatenate(parts, 0)
    shape = (NODES, count)
    out = []
    for spot in range(16):
        node = 16 * (spot // 4) + spot % 4
        block = both_halves(shape, precond_ref[node].astype(F32), precond_ref[node + 12].astype(F32))
        made = dot(stack, block.astype(BF16), NN)
        out.append(
            both_halves((16, count), made[0:16] + made[16:32], made[32:48] + made[48:64])
        )
    return out


def halo_lift(below, above, orient_ref, lift):
    shape = below.shape
    edge = shape[1] // 4
    low = jnp.where(lanes(shape) < edge, turn(below, orient_ref[2:3]), 0.0)
    high = jnp.where(lanes(shape) >= shape[1] - edge, turn(above, orient_ref[3:4]), 0.0)
    none = jnp.zeros((32, shape[1]), F32)
    rest = jnp.zeros((shape[1] - 64, shape[1]), F32)
    return dot_split(lift, halves(jnp.concatenate([none, low, high, rest], 0)))


START = 0
RHS = NODES
LIFT = 2 * NODES
EDGE = LIFT + NODES
NEIGHBOUR = EDGE + 32
ORIENT = NEIGHBOUR + 8
OWNER = ORIENT + 8
SLOT = OWNER + 1
PACKED = ORIENT + 16


class Packed:
    def __init__(self, ref):
        self.start = ref.at[START : START + NODES]
        self.rhs = ref.at[RHS : RHS + NODES]
        self.lift = ref[LIFT : LIFT + NODES]
        self.edge = ref[EDGE : EDGE + 32, 0:NODES]
        self.neighbour = ref[NEIGHBOUR : NEIGHBOUR + FACES].astype(jnp.int32)
        self.orient = ref[ORIENT : ORIENT + FACES].astype(jnp.int32)
        self.owner = ref[OWNER : OWNER + 1].astype(jnp.int32)
        self.slot = ref[SLOT : SLOT + 1].astype(jnp.int32)


def smooth_kernel(
    staying, owner_count,
    diag_ref, precond_ref, pack_ref,
    message_ref, partial_ref,
):
    count = diag_ref.shape[2]
    packed = Packed(pack_ref)
    start_ref, rhs_ref = packed.start, packed.rhs
    lift, neighbour_ref, orient_ref = packed.lift, packed.neighbour, packed.orient
    traces = face_traces(start_ref)
    shape = traces[2].shape
    none = jnp.zeros(shape, F32)
    coupled = coupling(traces, none, none, neighbour_ref, orient_ref, lift)
    resid = rhs_ref[...] - (apply_blocks(diag_ref, start_ref[...]) - coupled)
    partial_ref[...] = start_ref[...] + apply_blocks(precond_ref, resid)
    direct = edge_mask(shape)
    reply = response(precond_ref, packed.edge)
    for spot in range(8):
        message_ref[48 + 16 * spot : 64 + 16 * spot] = jnp.where(
            direct, reply[spot], pltpu.roll(reply[spot + 8], count // 2, 1)
        ).astype(BF16)
    later = pack_rim(face_traces(partial_ref))
    high, low = halves(jnp.where(direct, pack_rim(traces), pltpu.roll(later, count // 2, 1)))
    message_ref[0:16] = high
    message_ref[16:32] = low
    orient = both_halves((1, count), orient_ref[2:3], orient_ref[3:4])
    owner = packed.owner
    rank = rank_row(owner, staying, owner_count)
    place = rows(shape)
    facts = jnp.where(place < 4, orient, jnp.where(place < 8, owner, rank))
    message_ref[32:48] = facts.astype(F32).astype(BF16)


def merged(gathered_ref, at):
    slabs = gathered_ref.shape[0]
    pos = lax.axis_index("face")
    above = gathered_ref[jnp.minimum(pos + 1, slabs - 1), at].astype(F32)
    below = gathered_ref[jnp.maximum(pos - 1, 0), at].astype(F32)
    above = jnp.where(pos < slabs - 1, above, 0.0)
    below = jnp.where(pos > 0, below, 0.0)
    return jnp.where(low_mask(above.shape), above, below)


def aside(values):
    count = values.shape[1]
    return pltpu.roll(values, count // 4, 1), pltpu.roll(values, count - count // 4, 1)


def target_of(facts, staying, capacity):
    owner = facts[4:5].astype(jnp.int32)
    rank = facts[8:9].astype(jnp.int32)
    return jnp.where(lanes(owner.shape) >= staying, owner * capacity + rank, -1)


def middle_kernel(
    staying, capacity,
    gathered_ref, diag_ref, precond_ref, pack_ref, partial_ref,
    new_ref, rest_ref, rim_ref, facts_ref, edge_ref, sol_ref,
):
    count = diag_ref.shape[2]
    shape = (16, count)
    pos = lax.axis_index("face")
    packed = Packed(pack_ref)
    rhs_ref, slot = packed.rhs, packed.slot
    lift, neighbour_ref, orient_ref = packed.lift, packed.neighbour, packed.orient
    head = merged(gathered_ref, pl.ds(0, 16)) + merged(gathered_ref, pl.ds(16, 16))
    known = merged(gathered_ref, pl.ds(32, 16))
    orient = known[0:1].astype(jnp.int32)
    own = gathered_ref[pos, pl.ds(0, 16)].astype(F32) + gathered_ref[pos, pl.ds(16, 16)].astype(F32)
    from_high, from_low = aside(own)
    sent = turn(both_halves(shape, from_high, from_low), orient)
    below, above = aside(head)
    delta = halo_lift(below, above, orient_ref, lift)
    sol_ref[...] = partial_ref[...] + apply_blocks(precond_ref, delta)
    later = pltpu.roll(head, count // 2, 1)
    reply = []
    for spot in range(8):
        block = merged(gathered_ref, pl.ds(48 + 16 * spot, 16))
        reply.append((block, pltpu.roll(block, count // 2, 1)))
    reply = [pair[0] for pair in reply] + [pair[1] for pair in reply]
    change = [block * sent for block in reply]
    change = [block[:8] + block[8:] for block in change]
    change = jnp.concatenate([fold(change[:8]), fold(change[8:])], 0)
    below, above = aside(later + change)
    traces = face_traces(sol_ref)
    coupled = coupling(traces, below, above, neighbour_ref, orient_ref, lift)
    resid = rhs_ref[...] - (apply_blocks(diag_ref, sol_ref[...]) - coupled)
    new_ref[...] = sol_ref[...] + apply_blocks(precond_ref, resid)
    traces = face_traces(new_ref)
    none = jnp.zeros(shape, F32)
    coupled = coupling(traces, none, none, neighbour_ref, orient_ref, lift)
    rest_ref[...] = rhs_ref[...] - (apply_blocks(diag_ref, new_ref[...]) - coupled)
    rim_ref[...] = pack_rim(traces)
    mine = gathered_ref[pos, pl.ds(32, 16)].astype(F32)
    target = jnp.where(
        lanes((1, count)) >= count - count // 4, target_of(known, staying, capacity), -1
    )
    place = rows((8, count))
    facts = jnp.where(place == 0, orient, target)
    facts = jnp.where(place == 2, target_of(mine, staying, capacity), facts)
    facts = jnp.where(place == 3, orient_ref[2:3], facts)
    facts_ref[...] = jnp.where(place == 4, slot, facts)
    edge_ref[...] = lift


def spread(values, copies):
    none = jnp.zeros(values.shape, values.dtype)
    return jnp.concatenate(
        [
            jnp.concatenate([values if i == j else none for j in range(copies)], 1)
            for i in range(copies)
        ],
        0,
    )


def packed_by_target(values, target, owners, depth):
    count = values.shape[1]
    shape = (owners * depth, count)
    place = rows(shape)
    base = (place // depth) * (GROUP * depth) + place % depth
    hits = jnp.concatenate([one_hot(base + depth * g == target) for g in range(GROUP)], 1)
    made = dot(hits, spread(values, GROUP), NT)
    return made.reshape(owners, depth, GROUP * values.shape[0])


def send_kernel(rest_ref, rim_ref, facts_ref, after_ref, send_ref):
    pos = lax.axis_index("face")
    count = rest_ref.shape[1]
    edge = count // 4
    owners, slabs, depth, _ = send_ref.shape
    high, low = halves(rest_ref[...])
    keep = lanes(low.shape) >= count - edge
    low = jnp.where(keep, low.astype(F32), 0.0).astype(BF16)
    made = dot_split(small_table(), (high, low))
    send_ref[...] = jnp.zeros(send_ref.shape, BF16)
    ours = packed_by_target(made.astype(BF16), facts_ref[2:3], owners, depth)
    send_ref[:, pl.ds(pos, 1)] = ours.astype(BF16)[:, None]
    moved_up, moved_down = aside(rim_ref[...])

    @pl.when(pos > 0)
    def _():
        turned = turn(moved_down, facts_ref[0:1])
        turned = jnp.concatenate([turned, jnp.zeros(turned.shape, F32)], 0).astype(BF16)
        theirs = packed_by_target(turned, facts_ref[1:2], owners, depth)
        send_ref[:, pl.ds(pos - 1, 1)] = theirs.astype(BF16)[:, None]

    @pl.when(pos < slabs - 1)
    def _():
        group = lanes((8, count)) // edge
        rim = jnp.where(group == 0, moved_up[0:8], pltpu.roll(moved_up[8:16], edge, 1))
        send_ref[pl.ds(lax.axis_index("dom"), 1), pl.ds(pos + 1, 1), 0:8] = rim.astype(BF16)[None, None]


def rank_row(owner_row, staying, owner_count):
    count = owner_row.shape[1]
    shape = (owner_count, count)
    hits = (rows(shape) == owner_row) & (lanes(shape) >= staying)
    hits = jnp.where(hits, 1.0, 0.0)
    before = jnp.where(rows((count, count)) < lanes((count, count)), 1.0, 0.0)
    earlier = dot(hits.astype(BF16), before.astype(BF16), NN)
    return jnp.sum(hits * earlier, axis=0, keepdims=True).astype(jnp.int32)


def one_hot(condition):
    return jnp.where(condition, 1.0, 0.0).astype(BF16)


def contract(four, line):
    first, second = float(line[0, 1]), float(line[0, 2])
    middle = float(line[1, 1])
    return [
        four[0] + first * four[1] + second * four[2],
        middle * (four[1] + four[2]),
        four[3] + second * four[1] + first * four[2],
    ]


def galerkin_kernel(
    staying, owner_count, capacity,
    diag_in, slot_in, owner_in, table_in, start_in, rhs_in, lift_in, neighbour_in, orient_in,
    precond_in,
    send_out, local_out, pack_out,
    diag_ref, slot_ref, owner_ref, table_ref, lift_ref, neighbour_ref, orient_ref,
    send_ref, local_ref, pack_ref,
    full_ref, part_sem, sem, out_sem, send_sem,
):
    line = restrict_line()
    count = diag_ref.shape[2]
    chunk = 2 * GROUP
    wide_step = 4

    def part_copy(part):
        at = pl.ds(part * wide_step * chunk, wide_step * chunk)
        return pltpu.make_async_copy(diag_in.at[at], diag_ref.at[at], part_sem.at[part])

    pairs = [
        (slot_in, slot_ref), (owner_in, owner_ref), (table_in, table_ref),
        (start_in, pack_ref.at[START : START + NODES]), (rhs_in, pack_ref.at[RHS : RHS + NODES]),
        (lift_in, lift_ref), (neighbour_in, neighbour_ref), (orient_in, orient_ref),
    ]
    copies = [pltpu.make_async_copy(src, dst, sem.at[i]) for i, (src, dst) in enumerate(pairs)]
    for part in range(NODES // (wide_step * chunk)):
        part_copy(part).start()
    for copy in copies:
        copy.start()
    for copy in copies:
        copy.wait()
    stacked = lift_ref[...].reshape(FACES * 16, NODES)
    stacked = jnp.concatenate([stacked, jnp.zeros((count - FACES * 16, NODES), F32)], 0)
    pack_ref[LIFT : LIFT + NODES] = stacked.T
    pack_ref[EDGE : EDGE + 32, 0:NODES] = stacked[32:64]
    pack_ref[NEIGHBOUR : NEIGHBOUR + FACES] = neighbour_ref[...].astype(F32)
    pack_ref[ORIENT : ORIENT + FACES] = orient_ref[...].astype(F32)
    pack_ref[OWNER : OWNER + 1] = owner_ref[...].astype(F32)
    pack_ref[SLOT : SLOT + 1] = slot_ref[...].astype(F32)
    pack_copy = pltpu.make_async_copy(pack_ref, pack_out, out_sem.at[1])
    pack_copy.start()
    table = table_ref[...]
    padded = table.shape[0] // 2
    tall = padded // GROUP
    planes = []
    for i in range(4):
        bars = []
        for half in range(2):
            part = 2 * i + half
            if part % wide_step == 0:
                part_copy(part // wide_step).wait()
            wide = [
                diag_ref[chunk * part + GROUP * j : chunk * part + GROUP * j + GROUP].reshape(GROUP * NODES, count)
                for j in range(2)
            ]
            both = dot(table, jnp.concatenate(wide, 1), NN)
            made = both[:padded] + both[padded:]
            for j in range(2):
                four = [made[tall * k : tall * k + tall, count * j : count * j + count] for k in range(4)]
                bars.append(contract(four, line))
        sheet = [contract([bars[j][k] for j in range(4)], line) for k in range(3)]
        planes.append([sheet[k][j] for j in range(3) for k in range(3)])
    made = [contract([planes[i][rest] for i in range(4)], line) for rest in range(9)]
    for c in range(COARSE):
        at = COARSE * c if c < SPLIT else 5 * 128 + COARSE * (c - SPLIT)
        full_ref[at : at + tall] = made[c % 9][c // 9]
    full_ref[5 * 128 + COARSE * (COARSE - SPLIT) :] = jnp.zeros((128 - COARSE * (COARSE - SPLIT), count), F32)
    slot = (slot_ref[...] + 1).astype(F32)
    full_ref[5 * 128 - 1 : 5 * 128] = slot
    full_ref[6 * 128 - 1 : 6 * 128] = slot
    local = full_ref[...].astype(BF16)
    local_ref[...] = local
    local_copy = pltpu.make_async_copy(local_ref, local_out, out_sem.at[0])
    local_copy.start()
    owner = owner_ref[...]
    rank = rank_row(owner, staying, owner_count)
    target = jnp.where(lanes(owner.shape) >= staying, owner * capacity + rank, -1)
    twice = jnp.concatenate([target, target], 1)
    shape = (2 * capacity, 2 * count)
    upper = (rows(shape) >= capacity).astype(jnp.int32)
    place = rows(shape) - capacity * upper
    place = jnp.where(upper == (lanes(shape) >= count).astype(jnp.int32), place, -2 * owner_count * capacity)
    wide = [
        jnp.concatenate([local[256 * pair : 256 * pair + 128], local[256 * pair + 128 : 256 * pair + 256]], 1)
        for pair in range(3)
    ]
    send_copies = []
    share = max(owner_count // 2, 1)
    for first in range(0, owner_count, share):
        some = pl.ds(first, share)
        hits = [one_hot(place + capacity * o == twice) for o in range(first, first + share)]
        hits = jnp.concatenate(hits, 0)
        for pair in range(3):
            made = dot(hits, wide[pair], NT).reshape(share, 2 * capacity, 128).astype(BF16)
            send_ref[some, 2 * capacity * pair : 2 * capacity * pair + 2 * capacity] = made
        copy = pltpu.make_async_copy(send_ref.at[some], send_out.at[some], send_sem.at[first // share])
        copy.start()
        send_copies.append(copy)
    for copy in send_copies:
        copy.wait()
    pack_copy.wait()
    local_copy.wait()


def block_sum(made, height, width):
    total = made[0:height, 0:width]
    for g in range(1, GROUP):
        total = total + made[height * g : height * g + height, width * g : width * g + width]
    return total


def sum_operators(staying, got_ref, local_ref, facts_ref, op_ref, depth):
    aggregates = op_ref.shape[0]
    owners, size, count = got_ref.shape
    both = size // 3
    capacity = both // 2
    ids = got_ref[:, 2 * both : size].astype(F32).reshape(owners * both, count)[:, count - 1 : count]
    shape = (owners * both, 2 * aggregates)
    column = lanes(shape)
    column = jnp.where(column >= aggregates, column - aggregates, column)
    hits = jnp.where(ids == (column + 1).astype(F32), 1.0, 0.0).reshape(owners, both, 2 * aggregates)
    shape = (owners, both, 2 * aggregates)
    upper = lax.broadcasted_iota(jnp.int32, shape, 1) >= capacity
    right = lax.broadcasted_iota(jnp.int32, shape, 2) >= aggregates
    paired = jnp.where(upper == right, hits, 0.0).reshape(owners * both, 2 * aggregates).astype(BF16)
    stay = stay_hits(facts_ref, staying, aggregates)
    out = []
    for pair in range(3):
        block = got_ref[:, both * pair : both * pair + both].astype(F32).reshape(owners * both, count).astype(BF16)
        total = dot(paired, block, TN)
        for side in range(2):
            at = 128 * (2 * pair + side)
            out.append(
                total[aggregates * side : aggregates * side + aggregates] + dot(stay, local_ref[at : at + 128], NT)
            )
    cut = SPLIT * COARSE
    for block in range(4):
        op_ref[:, 128 * block : 128 * block + 128] = out[block]
    op_ref[:, 512:cut] = out[4][:, : cut - 512]
    op_ref[:, cut:] = out[5][:, : COARSE * COARSE - cut]
    parts = []
    for g in range(GROUP):
        part = hits[:, depth * g : depth * g + depth] if depth * g + depth <= both else None
        if part is None:
            part = jnp.zeros((owners, depth, 2 * aggregates), F32)
        parts.append(part.reshape(owners * depth, 2 * aggregates)[:, :aggregates])
    return jnp.concatenate(parts, 1).astype(BF16)


def stay_hits(facts_ref, staying, aggregates):
    slot = facts_ref[4:5]
    shape = (aggregates, slot.shape[1])
    return one_hot((rows(shape) == slot) & (lanes(shape) < staying))


def last_kernel(
    staying,
    got_ref, op_got_ref, local_ref, rest_ref, facts_ref, edge_ref, sol_ref,
    sol_out, op_out, rhs_out,
    op_ref, out_ref, sem,
):
    sol_copy = pltpu.make_async_copy(sol_ref, sol_out, sem.at[0])
    sol_copy.start()
    hits = sum_operators(staying, op_got_ref, local_ref, facts_ref, op_ref, got_ref.shape[2])
    op_copy = pltpu.make_async_copy(op_ref, op_out, sem.at[1])
    op_copy.start()
    pos = lax.axis_index("face")
    owners, slabs, depth, width = got_ref.shape
    aggregates = out_ref.shape[1]
    count = rest_ref.shape[1]
    edge = count // 4
    main = got_ref[:, pl.ds(pos, 1)].astype(F32).reshape(owners * depth, width).astype(BF16)
    side = got_ref[:, pl.ds(jnp.minimum(pos + 1, slabs - 1), 1)]
    side = jnp.where(pos < slabs - 1, side.astype(F32).reshape(owners * depth, width), 0.0).astype(BF16)
    main = block_sum(dot(main, hits, TN), width // GROUP, aggregates)
    side = block_sum(dot(side, hits, TN), width // GROUP, aggregates)[0:16]

    rim = got_ref[pl.ds(lax.axis_index("dom"), 1), pl.ds(jnp.maximum(pos - 1, 0), 1), 0:8]
    rim = jnp.where(pos > 0, rim.astype(F32).reshape(8, width), 0.0)
    rim = jnp.concatenate([rim, pltpu.roll(rim, count - edge, 1)], 0)
    rim = jnp.where(lanes(rim.shape) < edge, turn(rim, facts_ref[3:4]), 0.0)
    none = jnp.zeros((32, count), F32)
    rim = jnp.concatenate([none, rim, jnp.zeros((count - 48, count), F32)], 0)
    rest = rest_ref[...] + dot_split(edge_ref[...], halves(rim))
    nodes = dot(rest.astype(BF16), stay_hits(facts_ref, staying, aggregates), NT)
    side = jnp.concatenate(
        [jnp.zeros((48, aggregates), F32), side, jnp.zeros((count - 64, aggregates), F32)], 0
    )
    nodes = nodes + dot_split(edge_ref[...], halves(side))
    made = dot_split(small_table(), halves(nodes))
    out_ref[...] = (made + main)[:COARSE]
    rhs_copy = pltpu.make_async_copy(out_ref, rhs_out, sem.at[2])
    rhs_copy.start()
    sol_copy.wait()
    op_copy.wait()
    rhs_copy.wait()


def call(kernel, outs, args, spaces, out_spaces=None, scratch=(), flops=0, limit=VMEM_LIMIT):
    bytes_in = sum(a.size * a.dtype.itemsize for a in args)
    bytes_out = sum(o.size * o.dtype.itemsize for o in outs)
    out_spaces = out_spaces or [pltpu.VMEM] * len(outs)
    return pl.pallas_call(
        kernel,
        out_shape=tuple(outs),
        in_specs=[pl.BlockSpec(memory_space=space) for space in spaces],
        out_specs=tuple(pl.BlockSpec(memory_space=space) for space in out_spaces),
        scratch_shapes=list(scratch),
        compiler_params=pltpu.CompilerParams(vmem_limit_bytes=limit),
        cost_estimate=pl.CostEstimate(
            flops=flops, bytes_accessed=bytes_in + bytes_out, transcendentals=0
        ),
    )(*args)


def struct(shape, dtype):
    return jax.ShapeDtypeStruct(shape, dtype)


def block_table(table, copies, tall):
    out = []
    for part in split_table(table):
        full = np.zeros((copies * tall, copies * table.shape[1]), BF16)
        for copy in range(copies):
            full[
                copy * tall : copy * tall + table.shape[0],
                copy * table.shape[1] : (copy + 1) * table.shape[1],
            ] = part
        out.append(full)
    return np.concatenate(out, 0)


def per_device(start, rhs, diag_block, precond, lift, neighbour, orient, owner, slot):
    count = start.shape[1]
    staying = count // 4
    aggregates = count // 2
    owner_count = lax.axis_size("dom")
    slabs = lax.axis_size("face")
    movers = count - staying
    capacity = 2 * ((movers + owner_count - 2) // (owner_count - 1))
    depth = ceil_to(-(-max(capacity, count // 4) // GROUP), 8)
    places = GROUP * depth
    capacity = ceil_to(capacity, 4)
    chunk = 6 * capacity
    entries = 6 * 128
    owner = owner.reshape(1, count)
    slot = slot.reshape(1, count)
    table = jnp.asarray(block_table(restrict_table(), GROUP, 32))

    args = [diag_block, slot, owner, table, start, rhs, lift, neighbour, orient, precond]
    outs = [
        struct((owner_count, chunk, 128), BF16),
        struct((entries, count), BF16),
        struct((PACKED, count), F32),
    ]
    held = [each for each in args if each is not start and each is not rhs and each is not precond]
    op_send, local_op, pack = call(
        lambda *refs: galerkin_kernel(staying, owner_count, capacity, *refs),
        outs,
        args,
        [pl.ANY] * len(args),
        [pl.ANY] * len(outs),
        scratch=[pltpu.VMEM(each.shape, each.dtype) for each in held + outs]
        + [
            pltpu.VMEM((entries, count), F32),
            pltpu.SemaphoreType.DMA((2,)),
            pltpu.SemaphoreType.DMA((8,)),
            pltpu.SemaphoreType.DMA((2,)),
            pltpu.SemaphoreType.DMA((2,)),
        ],
        flops=200_000_000,
        limit=FIRST_LIMIT,
    )
    op_got = lax.all_to_all(op_send, "dom", split_axis=0, concat_axis=0, tiled=True)
    message, partial = call(
        lambda *refs: smooth_kernel(staying, owner_count, *refs),
        [struct((176, count), BF16), struct((NODES, count), F32)],
        [diag_block, precond, pack],
        [pltpu.VMEM] * 3,
        flops=100_000_000,
    )
    gathered = lax.all_gather(message, "face")
    sol, rest, rim, facts, edge = call(
        lambda *refs: middle_kernel(staying, places, *refs),
        [
            struct((NODES, count), F32),
            struct((NODES, count), F32),
            struct((16, count), F32),
            struct((8, count), jnp.int32),
            struct((NODES, count), F32),
        ],
        [gathered, diag_block, precond, pack, partial],
        [pltpu.VMEM] * 5,
        scratch=[pltpu.VMEM((NODES, count), F32)],
        flops=200_000_000,
    )
    (send,) = call(
        send_kernel,
        [struct((owner_count, slabs, depth, 128), BF16)],
        [rest, rim, facts, op_got],
        [pltpu.VMEM] * 3 + [pl.ANY],
        flops=100_000_000,
    )
    got = lax.all_to_all(
        send.reshape(owner_count * slabs, depth, 128), ("dom", "face"), split_axis=0, concat_axis=0, tiled=True
    ).reshape(owner_count, slabs, depth, 128)
    outs = [
        struct((NODES, count), F32),
        struct((aggregates, COARSE * COARSE), F32),
        struct((COARSE, aggregates), F32),
    ]
    sol, coarse_op, coarse_rhs = call(
        lambda *refs: last_kernel(staying, *refs),
        outs,
        [got, op_got, local_op, rest, facts, edge, sol],
        [pltpu.VMEM] * 7,
        [pl.ANY] * 3,
        scratch=[pltpu.VMEM(each.shape, each.dtype) for each in outs[1:]] + [pltpu.SemaphoreType.DMA((3,))],
        flops=100_000_000,
    )
    return (sol, coarse_op.T, coarse_rhs)


def solution(mesh):
    return jax.shard_map(
        per_device,
        mesh=mesh,
        in_specs=(
            P(None, ("dom", "face")),
            P(None, ("dom", "face")),
            P(None, None, ("dom", "face")),
            P(None, None, ("dom", "face")),
            P(),
            P(None, ("dom", "face")),
            P(None, ("dom", "face")),
            P(("dom", "face")),
            P(("dom", "face")),
        ),
        out_specs=(P(None, ("dom", "face")), P(None, ("dom", "face")), P(None, ("dom", "face"))),
        check_vma=False,
    )
```

```python
import jax
import jax.numpy as jnp
import numpy as np
from jax import lax
from jax.experimental import pallas as pl
from jax.experimental.pallas import tpu as pltpu
from jax.sharding import PartitionSpec as P

SWEEPS = 2
NODES = 64
COARSE = 27
FACES = 6
GROUP = 4
SPLIT = 23
F32 = jnp.float32
BF16 = jnp.bfloat16
VMEM_LIMIT = 24 * 1024 * 1024
FIRST_LIMIT = None

NN = (((1,), (0,)), ((), ()))
NT = (((1,), (1,)), ((), ()))
TN = (((0,), (0,)), ((), ()))


def restrict_line():
    fine = np.array([-1.0, -1.0 / np.sqrt(5.0), 1.0 / np.sqrt(5.0), 1.0])
    coarse = np.array([-1.0, 0.0, 1.0])
    basis = np.ones((4, 3))
    for column in range(3):
        for other in range(3):
            if other != column:
                basis[:, column] *= (fine - coarse[other]) / (coarse[column] - coarse[other])
    return basis.T


def restrict_table():
    line = restrict_line()
    return np.kron(np.kron(line, line), line)


def split_table(table):
    table = table.astype(np.float32)
    high = table.astype(BF16)
    low = (table - high.astype(np.float32)).astype(BF16)
    return high, low


def ceil_to(value, step):
    return -(-value // step) * step


def halves(values):
    high = values.astype(BF16)
    low = (values - high.astype(F32)).astype(BF16)
    return high, low


def dot(left, right, dims):
    return lax.dot_general(left, right, dims, preferred_element_type=F32)


def dot_split(left, right):
    left_high, left_low = halves(left)
    right_high, right_low = right
    size = left.shape[0]
    both = dot(jnp.concatenate([left_high, left_low], 0), right_high, NN)
    return both[:size] + both[size:] + dot(left_high, right_low, NN)


def small_table():
    shape = (32, NODES)
    line = restrict_line()
    row, col = rows(shape), lanes(shape)
    step = 9
    table = jnp.ones(shape, F32)
    left = row
    for digit in range(3):
        mine = (left >= step).astype(jnp.int32) + (left >= 2 * step).astype(jnp.int32)
        left = left - step * mine
        fine = (col >> (4 - 2 * digit)) & 3
        value = jnp.zeros(shape, F32)
        for i in range(3):
            for j in range(4):
                value = jnp.where((mine == i) & (fine == j), float(line[i, j]), value)
        table = table * value
        step //= 3
    return jnp.where(row < COARSE, table, 0.0)


def lanes(shape):
    return lax.broadcasted_iota(jnp.int32, shape, 1)


def rows(shape):
    return lax.broadcasted_iota(jnp.int32, shape, 0)


def face_traces(ref):
    return [
        ref[0:16],
        ref[48:64],
        jnp.concatenate([ref[16 * i : 16 * i + 4] for i in range(4)], 0),
        jnp.concatenate([ref[16 * i + 12 : 16 * i + 16] for i in range(4)], 0),
        ref[pl.ds(0, 16, stride=4)],
        ref[pl.ds(3, 16, stride=4)],
    ]


def take(values, index, axis):
    return jnp.take_along_axis(values, index, axis=axis, mode="promise_in_bounds")


def turn(values, orient_row):
    shape = values.shape
    orient = jnp.broadcast_to(orient_row, shape)
    place = rows(shape)
    first = (place >> 2) ^ ((orient & 1) * 3)
    second = (place & 3) ^ (((orient >> 1) & 1) * 3)
    flip = (orient & 4) > 0
    source = jnp.where(flip, 4 * second + first, 4 * first + second)
    out = []
    for half in (source[:8], source[8:]):
        within = half & 7
        out.append(jnp.where(half >= 8, take(values[8:], within, 0), take(values[:8], within, 0)))
    return jnp.concatenate(out, 0)


def pick(traces, neighbour_ref, face):
    values = traces[face ^ 1]
    count = values.shape[1]
    index = jnp.clip(neighbour_ref[face : face + 1] - (face ^ 1) * count, 0, count - 1)
    return take(values, jnp.broadcast_to(index, values.shape), 1)


def fold(parts):
    place = rows(parts[0].shape)
    step = 1
    while len(parts) > 1:
        even = (place & step) == 0
        parts = [
            jnp.where(even, x, y) + pltpu.roll(jnp.where(even, y, x), step, 0)
            for x, y in zip(parts[::2], parts[1::2])
        ]
        step *= 2
    return parts[0]


def apply_blocks(ref, values):
    count = values.shape[1]
    tiles = values.reshape(NODES // 8, 8, count)
    out = []
    for group in range(NODES // 8):
        parts = []
        for node in range(8 * group, 8 * group + 8):
            parts.append(jnp.sum(ref[node].astype(F32).reshape(NODES // 8, 8, count) * tiles, axis=0))
        out.append(fold(parts))
    return jnp.concatenate(out, 0)


def pack_rim(traces):
    shape = traces[2].shape
    return jnp.where(lanes(shape) < shape[1] // 2, traces[2], traces[3])


def coupling(traces, below, above, neighbour_ref, orient_ref, lift):
    count = below.shape[1]
    edge = count // 4
    turned = []
    for face in range(FACES):
        values = pick(traces, neighbour_ref, face)
        if face == 2:
            values = jnp.where(lanes(values.shape) < edge, below, values)
        if face == 3:
            values = jnp.where(lanes(values.shape) >= count - edge, above, values)
        turned.append(turn(values, orient_ref[face : face + 1]))
    turned = jnp.concatenate(turned + [jnp.zeros((count - FACES * 16, count), F32)], 0)
    return dot_split(lift, halves(turned))


def edge_mask(shape):
    return (lanes(shape) < shape[1] // 4) | (lanes(shape) >= shape[1] - shape[1] // 4)


def low_mask(shape):
    return ((lanes(shape) // (shape[1] // 4)) & 1) == 0


def both_halves(shape, low, high):
    return jnp.where(lanes(shape) < shape[1] // 2, low, high)


def response(precond_ref, edge):
    count = precond_ref.shape[2]
    parts = []
    for lift in (edge[0:16], edge[16:32]):
        parts.extend(halves(lift))
    stack = jnp.concatenate(parts, 0)
    shape = (NODES, count)
    out = []
    for spot in range(16):
        node = 16 * (spot // 4) + spot % 4
        block = both_halves(shape, precond_ref[node].astype(F32), precond_ref[node + 12].astype(F32))
        made = dot(stack, block.astype(BF16), NN)
        out.append(
            both_halves((16, count), made[0:16] + made[16:32], made[32:48] + made[48:64])
        )
    return out


def halo_lift(below, above, orient_ref, lift):
    shape = below.shape
    edge = shape[1] // 4
    low = jnp.where(lanes(shape) < edge, turn(below, orient_ref[2:3]), 0.0)
    high = jnp.where(lanes(shape) >= shape[1] - edge, turn(above, orient_ref[3:4]), 0.0)
    none = jnp.zeros((32, shape[1]), F32)
    rest = jnp.zeros((shape[1] - 64, shape[1]), F32)
    return dot_split(lift, halves(jnp.concatenate([none, low, high, rest], 0)))


START = 0
RHS = NODES
LIFT = 2 * NODES
EDGE = LIFT + NODES
TABLE = EDGE + 32
SIDE = TABLE + 32
COUPLED = SIDE + 32
NEIGHBOUR = COUPLED + NODES
ORIENT = NEIGHBOUR + 8
OWNER = ORIENT + 8
SLOT = OWNER + 1
PACKED = ORIENT + 16


class Packed:
    def __init__(self, ref):
        self.start = ref.at[START : START + NODES]
        self.rhs = ref.at[RHS : RHS + NODES]
        self.lift = ref[LIFT : LIFT + NODES]
        self.edge = ref[EDGE : EDGE + 32, 0:NODES]
        self.table = ref[TABLE : TABLE + 32, 0:NODES]
        self.side = ref[SIDE : SIDE + 32]
        self.coupled = ref[COUPLED : COUPLED + NODES]
        self.neighbour = ref[NEIGHBOUR : NEIGHBOUR + FACES].astype(jnp.int32)
        self.orient = ref[ORIENT : ORIENT + FACES].astype(jnp.int32)
        self.owner = ref[OWNER : OWNER + 1].astype(jnp.int32)
        self.slot = ref[SLOT : SLOT + 1].astype(jnp.int32)


def smooth_kernel(
    staying, owner_count,
    diag_ref, precond_ref, pack_ref,
    message_ref, partial_ref,
):
    count = diag_ref.shape[2]
    packed = Packed(pack_ref)
    start_ref, rhs_ref = packed.start, packed.rhs
    orient_ref = packed.orient
    traces = face_traces(start_ref)
    shape = traces[2].shape
    resid = rhs_ref[...] - (apply_blocks(diag_ref, start_ref[...]) - packed.coupled)
    partial_ref[...] = start_ref[...] + apply_blocks(precond_ref, resid)
    direct = edge_mask(shape)
    reply = response(precond_ref, packed.edge)
    for spot in range(8):
        message_ref[48 + 16 * spot : 64 + 16 * spot] = jnp.where(
            direct, reply[spot], pltpu.roll(reply[spot + 8], count // 2, 1)
        ).astype(BF16)
    later = pack_rim(face_traces(partial_ref))
    high, low = halves(jnp.where(direct, pack_rim(traces), pltpu.roll(later, count // 2, 1)))
    message_ref[0:16] = high
    message_ref[16:32] = low
    orient = both_halves((1, count), orient_ref[2:3], orient_ref[3:4])
    owner = packed.owner
    rank = rank_row(owner, staying, owner_count)
    place = rows(shape)
    facts = jnp.where(place < 4, orient, jnp.where(place < 8, owner, rank))
    message_ref[32:48] = facts.astype(F32).astype(BF16)


def merged(gathered_ref, at):
    slabs = gathered_ref.shape[0]
    pos = lax.axis_index("face")
    above = gathered_ref[jnp.minimum(pos + 1, slabs - 1), at].astype(F32)
    below = gathered_ref[jnp.maximum(pos - 1, 0), at].astype(F32)
    above = jnp.where(pos < slabs - 1, above, 0.0)
    below = jnp.where(pos > 0, below, 0.0)
    return jnp.where(low_mask(above.shape), above, below)


def aside(values):
    count = values.shape[1]
    return pltpu.roll(values, count // 4, 1), pltpu.roll(values, count - count // 4, 1)


def target_of(facts, staying, capacity):
    owner = facts[4:5].astype(jnp.int32)
    rank = facts[8:9].astype(jnp.int32)
    return jnp.where(lanes(owner.shape) >= staying, owner * capacity + rank, -1)


def middle_kernel(
    staying, capacity,
    gathered_ref, diag_ref, precond_ref, pack_ref, partial_ref,
    new_ref, rest_ref, facts_ref, edge_ref, send_ref, sol_ref,
):
    count = diag_ref.shape[2]
    shape = (16, count)
    pos = lax.axis_index("face")
    packed = Packed(pack_ref)
    rhs_ref, slot = packed.rhs, packed.slot
    lift, neighbour_ref, orient_ref = packed.lift, packed.neighbour, packed.orient
    head = merged(gathered_ref, pl.ds(0, 16)) + merged(gathered_ref, pl.ds(16, 16))
    known = merged(gathered_ref, pl.ds(32, 16))
    orient = known[0:1].astype(jnp.int32)
    own = gathered_ref[pos, pl.ds(0, 16)].astype(F32) + gathered_ref[pos, pl.ds(16, 16)].astype(F32)
    from_high, from_low = aside(own)
    sent = turn(both_halves(shape, from_high, from_low), orient)
    below, above = aside(head)
    delta = halo_lift(below, above, orient_ref, lift)
    sol_ref[...] = partial_ref[...] + apply_blocks(precond_ref, delta)
    later = pltpu.roll(head, count // 2, 1)
    reply = []
    for spot in range(8):
        block = merged(gathered_ref, pl.ds(48 + 16 * spot, 16))
        reply.append((block, pltpu.roll(block, count // 2, 1)))
    reply = [pair[0] for pair in reply] + [pair[1] for pair in reply]
    change = [block * sent for block in reply]
    change = [block[:8] + block[8:] for block in change]
    change = jnp.concatenate([fold(change[:8]), fold(change[8:])], 0)
    below, above = aside(later + change)
    traces = face_traces(sol_ref)
    coupled = coupling(traces, below, above, neighbour_ref, orient_ref, lift)
    resid = rhs_ref[...] - (apply_blocks(diag_ref, sol_ref[...]) - coupled)
    new_ref[...] = sol_ref[...] + apply_blocks(precond_ref, resid)
    traces = face_traces(new_ref)
    none = jnp.zeros(shape, F32)
    coupled = coupling(traces, none, none, neighbour_ref, orient_ref, lift)
    rest = rhs_ref[...] - (apply_blocks(diag_ref, new_ref[...]) - coupled)
    rest_ref[...] = rest
    mine = gathered_ref[pos, pl.ds(32, 16)].astype(F32)
    target = jnp.where(
        lanes((1, count)) >= count - count // 4, target_of(known, staying, capacity), -1
    )
    fill_messages(rest, traces, target_of(mine, staying, capacity), target, orient, packed.table, packed.side, send_ref)
    place = rows((8, count))
    facts_ref[...] = jnp.where(place < 4, orient_ref[2:3], slot)
    edge_ref[0:NODES] = lift
    edge_ref[NODES : NODES + 32, 0:NODES] = packed.table


def spread(values, copies):
    none = jnp.zeros(values.shape, values.dtype)
    return jnp.concatenate(
        [
            jnp.concatenate([values if i == j else none for j in range(copies)], 1)
            for i in range(copies)
        ],
        0,
    )


def packed_by_target(values, target, owners, depth):
    count = values.shape[1]
    shape = (owners * depth, count)
    place = rows(shape)
    base = (place // depth) * (GROUP * depth) + place % depth
    hits = jnp.concatenate([one_hot(base + depth * g == target) for g in range(GROUP)], 1)
    made = dot(hits, spread(values, GROUP), NT)
    return made.reshape(owners, depth, GROUP * values.shape[0])


def fill_messages(rest, traces, own_target, their_target, their_orient, table, side, send_ref):
    pos = lax.axis_index("face")
    count = rest.shape[1]
    edge = count // 4
    owners, slabs, depth, _ = send_ref.shape
    high, low = halves(rest)
    keep = lanes(low.shape) >= count - edge
    low = jnp.where(keep, low.astype(F32), 0.0).astype(BF16)
    made = dot_split(table, (high, low))
    ours = packed_by_target(made.astype(BF16), own_target, owners, depth)
    turned = turn(aside(traces[2])[1], their_orient)
    turned = jnp.concatenate([turned, jnp.zeros((count - 16, count), F32)], 0)
    lifted = dot_split(side, halves(turned))
    theirs = packed_by_target(lifted.astype(BF16), their_target, owners, depth)
    moved = aside(traces[3])[0]
    group = lanes((8, count)) // edge
    rim = jnp.where(group == 0, moved[0:8], pltpu.roll(moved[8:16], edge, 1))
    send_ref[...] = jnp.zeros(send_ref.shape, BF16)

    @pl.when(pos > 0)
    def _():
        send_ref[:, pl.ds(pos - 1, 1)] = theirs.astype(BF16)[:, None]

    @pl.when(pos < slabs - 1)
    def _():
        send_ref[pl.ds(lax.axis_index("dom"), 1), pl.ds(pos + 1, 1), 0:8] = rim.astype(BF16)[None, None]

    send_ref[:, pl.ds(pos, 1)] = ours.astype(BF16)[:, None]


def pass_kernel(made_ref, after_ref, send_ref):
    send_ref[...] = made_ref[...]


def rank_row(owner_row, staying, owner_count):
    count = owner_row.shape[1]
    shape = (owner_count, count)
    hits = (rows(shape) == owner_row) & (lanes(shape) >= staying)
    hits = jnp.where(hits, 1.0, 0.0)
    before = jnp.where(rows((count, count)) < lanes((count, count)), 1.0, 0.0)
    earlier = dot(hits.astype(BF16), before.astype(BF16), NN)
    return jnp.sum(hits * earlier, axis=0, keepdims=True).astype(jnp.int32)


def one_hot(condition):
    return jnp.where(condition, 1.0, 0.0).astype(BF16)


def contract(four, line):
    first, second = float(line[0, 1]), float(line[0, 2])
    middle = float(line[1, 1])
    return [
        four[0] + first * four[1] + second * four[2],
        middle * (four[1] + four[2]),
        four[3] + second * four[1] + first * four[2],
    ]


def galerkin_kernel(
    staying, owner_count, capacity,
    diag_in, slot_in, owner_in, table_in, start_in, rhs_in, lift_in, neighbour_in, orient_in,
    precond_in,
    send_out, local_out, pack_out,
    diag_ref, slot_ref, owner_ref, table_ref, lift_ref, neighbour_ref, orient_ref,
    send_ref, local_ref, pack_ref,
    full_ref, hits_ref, part_sem, sem, out_sem, send_sem,
):
    line = restrict_line()
    count = diag_ref.shape[2]
    chunk = 2 * GROUP
    wide_step = 4

    def part_copy(part):
        at = pl.ds(part * wide_step * chunk, wide_step * chunk)
        return pltpu.make_async_copy(diag_in.at[at], diag_ref.at[at], part_sem.at[part])

    pairs = [
        (slot_in, slot_ref), (owner_in, owner_ref), (table_in, table_ref),
        (start_in, pack_ref.at[START : START + NODES]), (rhs_in, pack_ref.at[RHS : RHS + NODES]),
        (lift_in, lift_ref), (neighbour_in, neighbour_ref), (orient_in, orient_ref),
    ]
    copies = [pltpu.make_async_copy(src, dst, sem.at[i]) for i, (src, dst) in enumerate(pairs)]
    for copy in copies:
        copy.start()
    for part in range(NODES // (wide_step * chunk)):
        part_copy(part).start()
    for copy in copies:
        copy.wait()
    stacked = lift_ref[...].reshape(FACES * 16, NODES)
    stacked = jnp.concatenate([stacked, jnp.zeros((count - FACES * 16, NODES), F32)], 0)
    lift = stacked.T
    pack_ref[LIFT : LIFT + NODES] = lift
    table = small_table()
    pack_ref[TABLE : TABLE + 32, 0:NODES] = table
    above = jnp.concatenate([stacked[48:64], jnp.zeros((count - 16, NODES), F32)], 0)
    pack_ref[SIDE : SIDE + 32] = dot_split(table, halves(above.T))
    traces = face_traces(pack_ref.at[START : START + NODES])
    none = jnp.zeros(traces[2].shape, F32)
    pack_ref[COUPLED : COUPLED + NODES] = coupling(traces, none, none, neighbour_ref[...], orient_ref[...], lift)
    pack_ref[EDGE : EDGE + 32, 0:NODES] = stacked[32:64]
    pack_ref[NEIGHBOUR : NEIGHBOUR + FACES] = neighbour_ref[...].astype(F32)
    pack_ref[ORIENT : ORIENT + FACES] = orient_ref[...].astype(F32)
    pack_ref[OWNER : OWNER + 1] = owner_ref[...].astype(F32)
    pack_ref[SLOT : SLOT + 1] = slot_ref[...].astype(F32)
    pack_copy = pltpu.make_async_copy(pack_ref, pack_out, out_sem.at[1])
    pack_copy.start()
    owner = owner_ref[...]
    rank = rank_row(owner, staying, owner_count)
    target = jnp.where(lanes(owner.shape) >= staying, owner * capacity + rank, -1)
    twice = jnp.concatenate([target, target], 1)
    shape = (2 * capacity, 2 * count)
    upper = (rows(shape) >= capacity).astype(jnp.int32)
    place = rows(shape) - capacity * upper
    place = jnp.where(upper == (lanes(shape) >= count).astype(jnp.int32), place, -2 * owner_count * capacity)
    for o in range(owner_count):
        hits_ref[2 * capacity * o : 2 * capacity * o + 2 * capacity] = one_hot(place + capacity * o == twice)
    table = table_ref[...]
    padded = table.shape[0] // 2
    tall = padded // GROUP
    planes = []
    for i in range(4):
        bars = []
        for half in range(2):
            part = 2 * i + half
            if part % wide_step == 0:
                part_copy(part // wide_step).wait()
            wide = [
                diag_ref[chunk * part + GROUP * j : chunk * part + GROUP * j + GROUP].reshape(GROUP * NODES, count)
                for j in range(2)
            ]
            both = dot(table, jnp.concatenate(wide, 1), NN)
            made = both[:padded] + both[padded:]
            for j in range(2):
                four = [made[tall * k : tall * k + tall, count * j : count * j + count] for k in range(4)]
                bars.append(contract(four, line))
        sheet = [contract([bars[j][k] for j in range(4)], line) for k in range(3)]
        planes.append([sheet[k][j] for j in range(3) for k in range(3)])
    made = [contract([planes[i][rest] for i in range(4)], line) for rest in range(9)]
    full_ref[5 * 128 - 16 : 5 * 128] = jnp.zeros((16, count), F32)
    for c in range(COARSE):
        at = COARSE * c if c < SPLIT else 5 * 128 + COARSE * (c - SPLIT)
        full_ref[at : at + tall] = made[c % 9][c // 9]
    full_ref[5 * 128 + COARSE * (COARSE - SPLIT) :] = jnp.zeros((128 - COARSE * (COARSE - SPLIT), count), F32)
    slot = (slot_ref[...] + 1).astype(F32)
    full_ref[5 * 128 - 1 : 5 * 128] = slot
    full_ref[6 * 128 - 1 : 6 * 128] = slot
    local = full_ref[...].astype(BF16)
    local_ref[...] = local
    local_copy = pltpu.make_async_copy(local_ref, local_out, out_sem.at[0])
    local_copy.start()
    wide = [
        jnp.concatenate([local[256 * pair : 256 * pair + 128], local[256 * pair + 128 : 256 * pair + 256]], 1)
        for pair in range(3)
    ]
    send_copies = []
    share = max(owner_count // 2, 1)
    for first in range(0, owner_count, share):
        some = pl.ds(first, share)
        hits = hits_ref[2 * capacity * first : 2 * capacity * (first + share)]
        for pair in range(3):
            made = dot(hits, wide[pair], NT).reshape(share, 2 * capacity, 128).astype(BF16)
            send_ref[some, 2 * capacity * pair : 2 * capacity * pair + 2 * capacity] = made
        copy = pltpu.make_async_copy(send_ref.at[some], send_out.at[some], send_sem.at[first // share])
        copy.start()
        send_copies.append(copy)
    for copy in send_copies:
        copy.wait()
    pack_copy.wait()
    local_copy.wait()


def block_sum(made, height, width):
    total = made[0:height, 0:width]
    for g in range(1, GROUP):
        total = total + made[height * g : height * g + height, width * g : width * g + width]
    return total


def sum_operators(staying, got_ref, local_ref, facts_ref, op_ref, op_out, sem, depth):
    aggregates = op_ref.shape[0]
    owners, size, count = got_ref.shape
    both = size // 3
    capacity = both // 2
    ids = got_ref[:, 2 * both : size].astype(F32).reshape(owners * both, count)[:, count - 1 : count]
    shape = (owners * both, 2 * aggregates)
    column = lanes(shape)
    column = jnp.where(column >= aggregates, column - aggregates, column)
    hits = jnp.where(ids == (column + 1).astype(F32), 1.0, 0.0).reshape(owners, both, 2 * aggregates)
    shape = (owners, both, 2 * aggregates)
    upper = lax.broadcasted_iota(jnp.int32, shape, 1) >= capacity
    right = lax.broadcasted_iota(jnp.int32, shape, 2) >= aggregates
    paired = jnp.where(upper == right, hits, 0.0).reshape(owners * both, 2 * aggregates).astype(BF16)
    stay = stay_hits(facts_ref, staying, aggregates)
    cut = SPLIT * COARSE
    copies = []
    for pair in range(3):
        block = got_ref[:, both * pair : both * pair + both].astype(F32).reshape(owners * both, count).astype(BF16)
        total = dot(paired, block, TN)
        out = []
        for side in range(2):
            at = 128 * (2 * pair + side)
            out.append(
                total[aggregates * side : aggregates * side + aggregates] + dot(stay, local_ref[at : at + 128], NT)
            )
        first, last = 256 * pair, min(256 * pair + 256, COARSE * COARSE)
        middle = cut if pair == 2 else first + 128
        op_ref[:, first:middle] = out[0][:, : middle - first]
        op_ref[:, middle:last] = out[1][:, : last - middle]
        some = pl.ds(first, last - first)
        copies.append(pltpu.make_async_copy(op_ref.at[:, some], op_out.at[:, some], sem.at[pair]))
        copies[-1].start()
    parts = []
    for g in range(GROUP):
        part = hits[:, depth * g : depth * g + depth] if depth * g + depth <= both else None
        if part is None:
            part = jnp.zeros((owners, depth, 2 * aggregates), F32)
        parts.append(part.reshape(owners * depth, 2 * aggregates)[:, :aggregates])
    return jnp.concatenate(parts, 1).astype(BF16), copies


def stay_hits(facts_ref, staying, aggregates):
    slot = facts_ref[4:5]
    shape = (aggregates, slot.shape[1])
    return one_hot((rows(shape) == slot) & (lanes(shape) < staying))


def last_kernel(
    staying,
    got_ref, op_got_ref, local_ref, rest_ref, facts_ref, edge_ref, sol_ref,
    sol_out, op_out, rhs_out,
    op_ref, out_ref, sem, op_sem,
):
    sol_copy = pltpu.make_async_copy(sol_ref, sol_out, sem.at[0])
    sol_copy.start()
    hits, copies = sum_operators(
        staying, op_got_ref, local_ref, facts_ref, op_ref, op_out, op_sem, got_ref.shape[2]
    )
    pos = lax.axis_index("face")
    owners, slabs, depth, width = got_ref.shape
    aggregates = out_ref.shape[1]
    count = rest_ref.shape[1]
    edge = count // 4
    main = got_ref[:, pl.ds(pos, 1)].astype(F32).reshape(owners * depth, width).astype(BF16)
    side = got_ref[:, pl.ds(jnp.minimum(pos + 1, slabs - 1), 1)]
    side = jnp.where(pos < slabs - 1, side.astype(F32).reshape(owners * depth, width), 0.0).astype(BF16)
    main = dot(jnp.concatenate([main, side], 0), jnp.concatenate([hits, hits], 0), TN)
    main = block_sum(main, width // GROUP, aggregates)

    rim = got_ref[pl.ds(lax.axis_index("dom"), 1), pl.ds(jnp.maximum(pos - 1, 0), 1), 0:8]
    rim = jnp.where(pos > 0, rim.astype(F32).reshape(8, width), 0.0)
    rim = jnp.concatenate([rim, pltpu.roll(rim, count - edge, 1)], 0)
    rim = jnp.where(lanes(rim.shape) < edge, turn(rim, facts_ref[0:1]), 0.0)
    none = jnp.zeros((32, count), F32)
    rim = jnp.concatenate([none, rim, jnp.zeros((count - 48, count), F32)], 0)
    rest = rest_ref[...] + dot_split(edge_ref[0:NODES], halves(rim))
    nodes = dot(rest.astype(BF16), stay_hits(facts_ref, staying, aggregates), NT)
    made = dot_split(edge_ref[NODES : NODES + 32, 0:NODES], halves(nodes))
    out_ref[...] = (made + main)[:COARSE]
    rhs_copy = pltpu.make_async_copy(out_ref, rhs_out, sem.at[1])
    rhs_copy.start()
    for copy in [sol_copy, rhs_copy] + copies:
        copy.wait()


def call(kernel, outs, args, spaces, out_spaces=None, scratch=(), flops=0, limit=VMEM_LIMIT):
    bytes_in = sum(a.size * a.dtype.itemsize for a in args)
    bytes_out = sum(o.size * o.dtype.itemsize for o in outs)
    out_spaces = out_spaces or [pltpu.VMEM] * len(outs)
    return pl.pallas_call(
        kernel,
        out_shape=tuple(outs),
        in_specs=[pl.BlockSpec(memory_space=space) for space in spaces],
        out_specs=tuple(pl.BlockSpec(memory_space=space) for space in out_spaces),
        scratch_shapes=list(scratch),
        compiler_params=pltpu.CompilerParams(vmem_limit_bytes=limit),
        cost_estimate=pl.CostEstimate(
            flops=flops, bytes_accessed=bytes_in + bytes_out, transcendentals=0
        ),
    )(*args)


def struct(shape, dtype):
    return jax.ShapeDtypeStruct(shape, dtype)


def block_table(table, copies, tall):
    out = []
    for part in split_table(table):
        full = np.zeros((copies * tall, copies * table.shape[1]), BF16)
        for copy in range(copies):
            full[
                copy * tall : copy * tall + table.shape[0],
                copy * table.shape[1] : (copy + 1) * table.shape[1],
            ] = part
        out.append(full)
    return np.concatenate(out, 0)


def per_device(start, rhs, diag_block, precond, lift, neighbour, orient, owner, slot):
    count = start.shape[1]
    staying = count // 4
    aggregates = count // 2
    owner_count = lax.axis_size("dom")
    slabs = lax.axis_size("face")
    movers = count - staying
    capacity = 2 * ((movers + owner_count - 2) // (owner_count - 1))
    depth = ceil_to(-(-max(capacity, count // 4) // GROUP), 8)
    places = GROUP * depth
    capacity = ceil_to(capacity, 4)
    chunk = 6 * capacity
    entries = 6 * 128
    owner = owner.reshape(1, count)
    slot = slot.reshape(1, count)
    table = jnp.asarray(block_table(restrict_table(), GROUP, 32))

    args = [diag_block, slot, owner, table, start, rhs, lift, neighbour, orient, precond]
    outs = [
        struct((owner_count, chunk, 128), BF16),
        struct((entries, count), BF16),
        struct((PACKED, count), F32),
    ]
    held = [each for each in args if each is not start and each is not rhs and each is not precond]
    op_send, local_op, pack = call(
        lambda *refs: galerkin_kernel(staying, owner_count, capacity, *refs),
        outs,
        args,
        [pl.ANY] * len(args),
        [pl.ANY] * len(outs),
        scratch=[pltpu.VMEM(each.shape, each.dtype) for each in held + outs]
        + [
            pltpu.VMEM((entries, count), F32),
            pltpu.VMEM((2 * capacity * owner_count, 2 * count), BF16),
            pltpu.SemaphoreType.DMA((2,)),
            pltpu.SemaphoreType.DMA((8,)),
            pltpu.SemaphoreType.DMA((2,)),
            pltpu.SemaphoreType.DMA((2,)),
        ],
        flops=200_000_000,
        limit=FIRST_LIMIT,
    )
    op_got = lax.all_to_all(op_send, "dom", split_axis=0, concat_axis=0, tiled=True)
    message, partial = call(
        lambda *refs: smooth_kernel(staying, owner_count, *refs),
        [struct((176, count), BF16), struct((NODES, count), F32)],
        [diag_block, precond, pack],
        [pltpu.VMEM] * 3,
        flops=100_000_000,
    )
    gathered = lax.all_gather(message, "face")
    sol, rest, facts, edge, made = call(
        lambda *refs: middle_kernel(staying, places, *refs),
        [
            struct((NODES, count), F32),
            struct((NODES, count), F32),
            struct((8, count), jnp.int32),
            struct((NODES + 32, count), F32),
            struct((owner_count, slabs, depth, 128), BF16),
        ],
        [gathered, diag_block, precond, pack, partial],
        [pltpu.VMEM] * 5,
        scratch=[pltpu.VMEM((NODES, count), F32)],
        flops=200_000_000,
    )
    (send,) = call(
        pass_kernel,
        [struct(made.shape, made.dtype)],
        [made, op_got],
        [pltpu.VMEM, pl.ANY],
        flops=1_000_000,
    )
    got = lax.all_to_all(
        send.reshape(owner_count * slabs, depth, 128), ("dom", "face"), split_axis=0, concat_axis=0, tiled=True
    ).reshape(owner_count, slabs, depth, 128)
    outs = [
        struct((NODES, count), F32),
        struct((aggregates, COARSE * COARSE), F32),
        struct((COARSE, aggregates), F32),
    ]
    sol, coarse_op, coarse_rhs = call(
        lambda *refs: last_kernel(staying, *refs),
        outs,
        [got, op_got, local_op, rest, facts, edge, sol],
        [pltpu.VMEM] * 7,
        [pl.ANY] * 3,
        scratch=[pltpu.VMEM(each.shape, each.dtype) for each in outs[1:]] + [pltpu.SemaphoreType.DMA((2,)), pltpu.SemaphoreType.DMA((3,))],
        flops=100_000_000,
    )
    return (sol, coarse_op.T, coarse_rhs)


def solution(mesh):
    return jax.shard_map(
        per_device,
        mesh=mesh,
        in_specs=(
            P(None, ("dom", "face")),
            P(None, ("dom", "face")),
            P(None, None, ("dom", "face")),
            P(None, None, ("dom", "face")),
            P(),
            P(None, ("dom", "face")),
            P(None, ("dom", "face")),
            P(("dom", "face")),
            P(("dom", "face")),
        ),
        out_specs=(P(None, ("dom", "face")), P(None, ("dom", "face")), P(None, ("dom", "face"))),
        check_vma=False,
    )
```

```python
import jax
import jax.numpy as jnp
import numpy as np
from jax import lax
from jax.experimental import pallas as pl
from jax.experimental.pallas import tpu as pltpu
from jax.sharding import PartitionSpec as P

SWEEPS = 2
NODES = 64
COARSE = 27
FACES = 6
GROUP = 4
SPLIT = 23
F32 = jnp.float32
BF16 = jnp.bfloat16
VMEM_LIMIT = 24 * 1024 * 1024
FIRST_LIMIT = None

NN = (((1,), (0,)), ((), ()))
NT = (((1,), (1,)), ((), ()))
TN = (((0,), (0,)), ((), ()))


def restrict_line():
    fine = np.array([-1.0, -1.0 / np.sqrt(5.0), 1.0 / np.sqrt(5.0), 1.0])
    coarse = np.array([-1.0, 0.0, 1.0])
    basis = np.ones((4, 3))
    for column in range(3):
        for other in range(3):
            if other != column:
                basis[:, column] *= (fine - coarse[other]) / (coarse[column] - coarse[other])
    return basis.T


def restrict_table():
    line = restrict_line()
    return np.kron(np.kron(line, line), line)


def split_table(table):
    table = table.astype(np.float32)
    high = table.astype(BF16)
    low = (table - high.astype(np.float32)).astype(BF16)
    return high, low


def ceil_to(value, step):
    return -(-value // step) * step


def halves(values):
    high = values.astype(BF16)
    low = (values - high.astype(F32)).astype(BF16)
    return high, low


def dot(left, right, dims):
    return lax.dot_general(left, right, dims, preferred_element_type=F32)


def dot_split(left, right):
    left_high, left_low = halves(left)
    right_high, right_low = right
    size = left.shape[0]
    both = dot(jnp.concatenate([left_high, left_low], 0), right_high, NN)
    return both[:size] + both[size:] + dot(left_high, right_low, NN)


def small_table():
    shape = (32, NODES)
    line = restrict_line()
    row, col = rows(shape), lanes(shape)
    step = 9
    table = jnp.ones(shape, F32)
    left = row
    for digit in range(3):
        mine = (left >= step).astype(jnp.int32) + (left >= 2 * step).astype(jnp.int32)
        left = left - step * mine
        fine = (col >> (4 - 2 * digit)) & 3
        value = jnp.zeros(shape, F32)
        for i in range(3):
            for j in range(4):
                value = jnp.where((mine == i) & (fine == j), float(line[i, j]), value)
        table = table * value
        step //= 3
    return jnp.where(row < COARSE, table, 0.0)


def lanes(shape):
    return lax.broadcasted_iota(jnp.int32, shape, 1)


def rows(shape):
    return lax.broadcasted_iota(jnp.int32, shape, 0)


def face_traces(ref):
    return [
        ref[0:16],
        ref[48:64],
        jnp.concatenate([ref[16 * i : 16 * i + 4] for i in range(4)], 0),
        jnp.concatenate([ref[16 * i + 12 : 16 * i + 16] for i in range(4)], 0),
        ref[pl.ds(0, 16, stride=4)],
        ref[pl.ds(3, 16, stride=4)],
    ]


def take(values, index, axis):
    return jnp.take_along_axis(values, index, axis=axis, mode="promise_in_bounds")


def turn(values, orient_row):
    shape = values.shape
    orient = jnp.broadcast_to(orient_row, shape)
    place = rows(shape)
    first = (place >> 2) ^ ((orient & 1) * 3)
    second = (place & 3) ^ (((orient >> 1) & 1) * 3)
    flip = (orient & 4) > 0
    source = jnp.where(flip, 4 * second + first, 4 * first + second)
    out = []
    for half in (source[:8], source[8:]):
        within = half & 7
        out.append(jnp.where(half >= 8, take(values[8:], within, 0), take(values[:8], within, 0)))
    return jnp.concatenate(out, 0)


def pick(traces, neighbour_ref, face):
    values = traces[face ^ 1]
    count = values.shape[1]
    index = jnp.clip(neighbour_ref[face : face + 1] - (face ^ 1) * count, 0, count - 1)
    return take(values, jnp.broadcast_to(index, values.shape), 1)


def fold(parts):
    place = rows(parts[0].shape)
    step = 1
    while len(parts) > 1:
        even = (place & step) == 0
        parts = [
            jnp.where(even, x, y) + pltpu.roll(jnp.where(even, y, x), step, 0)
            for x, y in zip(parts[::2], parts[1::2])
        ]
        step *= 2
    return parts[0]


def apply_blocks(ref, values):
    count = values.shape[1]
    tiles = values.reshape(NODES // 8, 8, count)
    out = []
    for group in range(NODES // 8):
        parts = []
        for node in range(8 * group, 8 * group + 8):
            parts.append(jnp.sum(ref[node].astype(F32).reshape(NODES // 8, 8, count) * tiles, axis=0))
        out.append(fold(parts))
    return jnp.concatenate(out, 0)


def pack_rim(traces):
    shape = traces[2].shape
    return jnp.where(lanes(shape) < shape[1] // 2, traces[2], traces[3])


def coupling(traces, below, above, neighbour_ref, orient_ref, lift):
    count = below.shape[1]
    edge = count // 4
    turned = []
    for face in range(FACES):
        values = pick(traces, neighbour_ref, face)
        if face == 2:
            values = jnp.where(lanes(values.shape) < edge, below, values)
        if face == 3:
            values = jnp.where(lanes(values.shape) >= count - edge, above, values)
        turned.append(turn(values, orient_ref[face : face + 1]))
    turned = jnp.concatenate(turned + [jnp.zeros((count - FACES * 16, count), F32)], 0)
    return dot_split(lift, halves(turned))


def edge_mask(shape):
    return (lanes(shape) < shape[1] // 4) | (lanes(shape) >= shape[1] - shape[1] // 4)


def low_mask(shape):
    return ((lanes(shape) // (shape[1] // 4)) & 1) == 0


def both_halves(shape, low, high):
    return jnp.where(lanes(shape) < shape[1] // 2, low, high)


def response(precond_ref, edge):
    count = precond_ref.shape[2]
    parts = []
    for lift in (edge[0:16], edge[16:32]):
        parts.extend(halves(lift))
    stack = jnp.concatenate(parts, 0)
    shape = (NODES, count)
    out = []
    for spot in range(16):
        node = 16 * (spot // 4) + spot % 4
        block = both_halves(shape, precond_ref[node].astype(F32), precond_ref[node + 12].astype(F32))
        made = dot(stack, block.astype(BF16), NN)
        out.append(
            both_halves((16, count), made[0:16] + made[16:32], made[32:48] + made[48:64])
        )
    return out


def halo_lift(below, above, orient_ref, lift):
    shape = below.shape
    edge = shape[1] // 4
    low = jnp.where(lanes(shape) < edge, turn(below, orient_ref[2:3]), 0.0)
    high = jnp.where(lanes(shape) >= shape[1] - edge, turn(above, orient_ref[3:4]), 0.0)
    none = jnp.zeros((32, shape[1]), F32)
    rest = jnp.zeros((shape[1] - 64, shape[1]), F32)
    return dot_split(lift, halves(jnp.concatenate([none, low, high, rest], 0)))


RHS = 0
PARTIAL = NODES
LIFT = 2 * NODES
EDGE = LIFT + NODES
TABLE = EDGE + 32
NEIGHBOUR = TABLE + 32
ORIENT = NEIGHBOUR + 8
OWNER = ORIENT + 8
RANK = OWNER + 1
SLOT = OWNER + 2
PACKED = ORIENT + 16


class Packed:
    def __init__(self, ref):
        self.rhs = ref.at[RHS : RHS + NODES]
        self.partial = ref.at[PARTIAL : PARTIAL + NODES]
        self.lift = ref[LIFT : LIFT + NODES]
        self.table = ref[TABLE : TABLE + 32, 0:NODES]
        self.neighbour = ref[NEIGHBOUR : NEIGHBOUR + FACES].astype(jnp.int32)
        self.orient = ref[ORIENT : ORIENT + FACES].astype(jnp.int32)
        self.owner = ref[OWNER : OWNER + 1].astype(jnp.int32)
        self.rank = ref[RANK : RANK + 1].astype(jnp.int32)
        self.slot = ref[SLOT : SLOT + 1].astype(jnp.int32)

    def target(self, staying, capacity):
        return jnp.where(lanes(self.owner.shape) >= staying, self.owner * capacity + self.rank, -1)


def smooth_kernel(
    staying, owner_count,
    diag_in, precond_in, start_in, rhs_in, lift_in, neighbour_in, orient_in, owner_in, slot_in,
    message_out, pack_out,
    diag_ref, precond_ref, start_ref, lift_ref, neighbour_ref, orient_ref, owner_ref, slot_ref,
    message_ref, pack_ref, sem, diag_sem, precond_sem, out_sem,
):
    count = diag_ref.shape[2]
    pairs = [
        (start_in, start_ref), (neighbour_in, neighbour_ref), (orient_in, orient_ref), (lift_in, lift_ref),
        (rhs_in, pack_ref.at[RHS : RHS + NODES]), (owner_in, owner_ref), (slot_in, slot_ref),
    ]
    copies = [pltpu.make_async_copy(src, dst, sem.at[i]) for i, (src, dst) in enumerate(pairs)]
    diag_copy = pltpu.make_async_copy(diag_in, diag_ref, diag_sem)
    precond_copy = pltpu.make_async_copy(precond_in, precond_ref, precond_sem)
    for copy in copies + [diag_copy, precond_copy]:
        copy.start()
    for copy in copies:
        copy.wait()
    stacked = lift_ref[...].reshape(FACES * 16, NODES)
    lift = jnp.concatenate([stacked, jnp.zeros((count - FACES * 16, NODES), F32)], 0).T
    pack_ref[LIFT : LIFT + NODES] = lift
    pack_ref[EDGE : EDGE + 32, 0:NODES] = stacked[32:64]
    pack_ref[TABLE : TABLE + 32, 0:NODES] = small_table()
    pack_ref[NEIGHBOUR : NEIGHBOUR + FACES] = neighbour_ref[...].astype(F32)
    pack_ref[ORIENT : ORIENT + FACES] = orient_ref[...].astype(F32)
    owner = owner_ref[...]
    rank = rank_row(owner, staying, owner_count)
    pack_ref[OWNER : OWNER + 1] = owner.astype(F32)
    pack_ref[RANK : RANK + 1] = rank.astype(F32)
    pack_ref[SLOT : SLOT + 1] = slot_ref[...].astype(F32)
    traces = face_traces(start_ref)
    shape = traces[2].shape
    direct = edge_mask(shape)
    none = jnp.zeros(shape, F32)
    coupled = coupling(traces, none, none, neighbour_ref[...], orient_ref[...], lift)
    orient = both_halves((1, count), orient_ref[2:3], orient_ref[3:4])
    message_ref[32:48] = jnp.broadcast_to(orient.astype(F32), shape).astype(BF16)
    diag_copy.wait()
    resid = pack_ref[RHS : RHS + NODES] - (apply_blocks(diag_ref, start_ref[...]) - coupled)
    precond_copy.wait()
    reply = response(precond_ref, stacked[32:64])
    for spot in range(8):
        message_ref[48 + 16 * spot : 64 + 16 * spot] = jnp.where(
            direct, reply[spot], pltpu.roll(reply[spot + 8], count // 2, 1)
        ).astype(BF16)
    partial_ref = pack_ref.at[PARTIAL : PARTIAL + NODES]
    partial_ref[...] = start_ref[...] + apply_blocks(precond_ref, resid)
    pack_copy = pltpu.make_async_copy(pack_ref, pack_out, out_sem.at[0])
    pack_copy.start()
    later = pack_rim(face_traces(partial_ref))
    high, low = halves(jnp.where(direct, pack_rim(traces), pltpu.roll(later, count // 2, 1)))
    message_ref[0:16] = high
    message_ref[16:32] = low
    message_copy = pltpu.make_async_copy(message_ref, message_out, out_sem.at[1])
    message_copy.start()
    pack_copy.wait()
    message_copy.wait()


def sides(first, second):
    pos, slabs = lax.axis_index("face"), lax.axis_size("face")
    even = lax.rem(pos, 2) == 0
    above = jnp.where(even, first, second)
    below = jnp.where(even, second, first)
    return jnp.where(pos < slabs - 1, above, 0.0), jnp.where(pos > 0, below, 0.0)


def merged(first_ref, second_ref, at):
    above, below = sides(first_ref[at].astype(F32), second_ref[at].astype(F32))
    return jnp.where(low_mask(above.shape), above, below)


def aside(values):
    count = values.shape[1]
    return pltpu.roll(values, count // 4, 1), pltpu.roll(values, count - count // 4, 1)


def middle_kernel(
    first_ref, second_ref, message_ref, diag_ref, precond_ref, pack_ref, after_ref,
    new_ref, rest_ref, rim_ref, sol_ref,
):
    count = diag_ref.shape[2]
    shape = (16, count)
    packed = Packed(pack_ref)
    rhs_ref, partial_ref = packed.rhs, packed.partial
    lift, neighbour_ref, orient_ref = packed.lift, packed.neighbour, packed.orient
    head = merged(first_ref, second_ref, pl.ds(0, 16)) + merged(first_ref, second_ref, pl.ds(16, 16))
    orient = merged(first_ref, second_ref, pl.ds(32, 16))[0:1].astype(jnp.int32)
    own = message_ref[0:16].astype(F32) + message_ref[16:32].astype(F32)
    from_high, from_low = aside(own)
    sent = turn(both_halves(shape, from_high, from_low), orient)
    below, above = aside(head)
    delta = halo_lift(below, above, orient_ref, lift)
    sol_ref[...] = partial_ref[...] + apply_blocks(precond_ref, delta)
    later = pltpu.roll(head, count // 2, 1)
    reply = []
    for spot in range(8):
        block = merged(first_ref, second_ref, pl.ds(48 + 16 * spot, 16))
        reply.append((block, pltpu.roll(block, count // 2, 1)))
    reply = [pair[0] for pair in reply] + [pair[1] for pair in reply]
    change = [block * sent for block in reply]
    change = [block[:8] + block[8:] for block in change]
    change = jnp.concatenate([fold(change[:8]), fold(change[8:])], 0)
    below, above = aside(later + change)
    traces = face_traces(sol_ref)
    coupled = coupling(traces, below, above, neighbour_ref, orient_ref, lift)
    resid = rhs_ref[...] - (apply_blocks(diag_ref, sol_ref[...]) - coupled)
    new_ref[...] = sol_ref[...] + apply_blocks(precond_ref, resid)
    traces = face_traces(new_ref)
    rim_ref[...] = pack_rim(traces)
    none = jnp.zeros(shape, F32)
    coupled = coupling(traces, none, none, neighbour_ref, orient_ref, lift)
    rest_ref[...] = rhs_ref[...] - (apply_blocks(diag_ref, new_ref[...]) - coupled)


def spread(values, copies):
    none = jnp.zeros(values.shape, values.dtype)
    return jnp.concatenate(
        [
            jnp.concatenate([values if i == j else none for j in range(copies)], 1)
            for i in range(copies)
        ],
        0,
    )


def packed_by_target(values, target, owners, depth):
    count = values.shape[1]
    shape = (owners * depth, count)
    place = rows(shape)
    base = (place // depth) * (GROUP * depth) + place % depth
    hits = jnp.concatenate([one_hot(base + depth * g == target) for g in range(GROUP)], 1)
    made = dot(hits, spread(values, GROUP), NT)
    return made.reshape(owners, depth, GROUP * values.shape[0])


def send_kernel(staying, first_ref, second_ref, rest_ref, pack_ref, made_ref, low_ref, send_ref):
    packed = Packed(pack_ref)
    owners, size, _ = made_ref.shape
    depth = send_ref.shape[1] - size
    above, below = sides(first_ref[...], second_ref[...])
    below, above = aside(below)[0], aside(above)[1]
    low = (rest_ref[...] + halo_lift(below, above, packed.orient, packed.lift)).astype(BF16)
    low_ref[...] = low
    table_high, table_low = halves(packed.table)
    both = dot(jnp.concatenate([table_high, table_low], 0), low, NN)
    made = both[:32] + both[32:]
    ours = packed_by_target(made.astype(BF16), packed.target(staying, GROUP * depth), owners, depth)
    send_ref[:, 0:size] = made_ref[...]
    send_ref[:, size:] = ours.astype(BF16)


def rank_row(owner_row, staying, owner_count):
    count = owner_row.shape[1]
    shape = (owner_count, count)
    hits = (rows(shape) == owner_row) & (lanes(shape) >= staying)
    hits = jnp.where(hits, 1.0, 0.0)
    before = jnp.where(rows((count, count)) < lanes((count, count)), 1.0, 0.0)
    earlier = dot(hits.astype(BF16), before.astype(BF16), NN)
    return jnp.sum(hits * earlier, axis=0, keepdims=True).astype(jnp.int32)


def one_hot(condition):
    return jnp.where(condition, 1.0, 0.0).astype(BF16)


def contract(four, line):
    first, second = float(line[0, 1]), float(line[0, 2])
    middle = float(line[1, 1])
    return [
        four[0] + first * four[1] + second * four[2],
        middle * (four[1] + four[2]),
        four[3] + second * four[1] + first * four[2],
    ]


def galerkin_kernel(staying, capacity, diag_ref, pack_ref, table_ref, send_ref, local_ref, full_ref):
    line = restrict_line()
    count = diag_ref.shape[2]
    owner_count = send_ref.shape[0]
    packed = Packed(pack_ref)
    target = packed.target(staying, capacity)
    twice = jnp.concatenate([target, target], 1)
    shape = (2 * capacity, 2 * count)
    upper = (rows(shape) >= capacity).astype(jnp.int32)
    place = rows(shape) - capacity * upper
    place = jnp.where(upper == (lanes(shape) >= count).astype(jnp.int32), place, -2 * owner_count * capacity)
    hits = jnp.concatenate([one_hot(place + capacity * o == twice) for o in range(owner_count)], 0)
    table = table_ref[...]
    padded = table.shape[0] // 2
    tall = padded // GROUP
    planes = []
    for i in range(4):
        bars = []
        for half in range(2):
            first = 2 * GROUP * (2 * i + half)
            wide = [
                diag_ref[first + GROUP * j : first + GROUP * j + GROUP].reshape(GROUP * NODES, count)
                for j in range(2)
            ]
            both = dot(table, jnp.concatenate(wide, 1), NN)
            made = both[:padded] + both[padded:]
            for j in range(2):
                four = [made[tall * k : tall * k + tall, count * j : count * j + count] for k in range(4)]
                bars.append(contract(four, line))
        sheet = [contract([bars[j][k] for j in range(4)], line) for k in range(3)]
        planes.append([sheet[k][j] for j in range(3) for k in range(3)])
    made = [contract([planes[i][rest] for i in range(4)], line) for rest in range(9)]
    full_ref[5 * 128 - 16 : 5 * 128] = jnp.zeros((16, count), F32)
    for c in range(COARSE):
        at = COARSE * c if c < SPLIT else 5 * 128 + COARSE * (c - SPLIT)
        full_ref[at : at + tall] = made[c % 9][c // 9]
    full_ref[5 * 128 + COARSE * (COARSE - SPLIT) :] = jnp.zeros((128 - COARSE * (COARSE - SPLIT), count), F32)
    slot = (packed.slot + 1).astype(F32)
    full_ref[5 * 128 - 1 : 5 * 128] = slot
    full_ref[6 * 128 - 1 : 6 * 128] = slot
    local = full_ref[...].astype(BF16)
    local_ref[...] = local
    for pair in range(3):
        wide = jnp.concatenate([local[256 * pair : 256 * pair + 128], local[256 * pair + 128 : 256 * pair + 256]], 1)
        made = dot(hits, wide, NT).reshape(owner_count, 2 * capacity, 128).astype(BF16)
        send_ref[:, 2 * capacity * pair : 2 * capacity * pair + 2 * capacity] = made


def block_sum(made, height, width):
    total = made[0:height, 0:width]
    for g in range(1, GROUP):
        total = total + made[height * g : height * g + height, width * g : width * g + width]
    return total


def sum_operators(got_ref, size, local_ref, stay, op_ref, op_out, sem, depth):
    aggregates = op_ref.shape[0]
    owners, _, count = got_ref.shape
    both = size // 3
    capacity = both // 2
    ids = got_ref[:, 2 * both : size].astype(F32).reshape(owners * both, count)[:, count - 1 : count]
    shape = (owners * both, 2 * aggregates)
    column = lanes(shape)
    column = jnp.where(column >= aggregates, column - aggregates, column)
    hits = jnp.where(ids == (column + 1).astype(F32), 1.0, 0.0).reshape(owners, both, 2 * aggregates)
    shape = (owners, both, 2 * aggregates)
    upper = lax.broadcasted_iota(jnp.int32, shape, 1) >= capacity
    right = lax.broadcasted_iota(jnp.int32, shape, 2) >= aggregates
    paired = jnp.where(upper == right, hits, 0.0).reshape(owners * both, 2 * aggregates).astype(BF16)
    cut = SPLIT * COARSE
    copies = []
    for pair in range(3):
        block = got_ref[:, both * pair : both * pair + both].astype(F32).reshape(owners * both, count).astype(BF16)
        total = dot(paired, block, TN)
        out = []
        for side in range(2):
            at = 128 * (2 * pair + side)
            out.append(
                total[aggregates * side : aggregates * side + aggregates] + dot(stay, local_ref[at : at + 128], NT)
            )
        first, last = 256 * pair, min(256 * pair + 256, COARSE * COARSE)
        middle = cut if pair == 2 else first + 128
        op_ref[:, first:middle] = out[0][:, : middle - first]
        op_ref[:, middle:last] = out[1][:, : last - middle]
        some = pl.ds(first, last - first)
        copies.append(pltpu.make_async_copy(op_ref.at[:, some], op_out.at[:, some], sem.at[pair]))
        copies[-1].start()
    parts = []
    for g in range(GROUP):
        part = hits[:, depth * g : depth * g + depth] if depth * g + depth <= both else None
        if part is None:
            part = jnp.zeros((owners, depth, 2 * aggregates), F32)
        parts.append(part.reshape(owners * depth, 2 * aggregates)[:, :aggregates])
    return jnp.concatenate(parts, 1).astype(BF16), copies


def last_kernel(
    staying, depth, got_ref, local_ref, low_ref, pack_ref, sol_ref,
    sol_out, op_out, rhs_out,
    op_ref, out_ref, sem, op_sem,
):
    sol_copy = pltpu.make_async_copy(sol_ref, sol_out, sem.at[0])
    sol_copy.start()
    packed = Packed(pack_ref)
    owners, size, width = got_ref.shape
    aggregates = out_ref.shape[1]
    shape = (aggregates, low_ref.shape[1])
    stay = one_hot((rows(shape) == packed.slot) & (lanes(shape) < staying))
    hits, copies = sum_operators(got_ref, size - depth, local_ref, stay, op_ref, op_out, op_sem, depth)
    main = got_ref[:, size - depth :].astype(F32).reshape(owners * depth, width).astype(BF16)
    main = block_sum(dot(main, hits, TN), width // GROUP, aggregates)
    nodes = dot(low_ref[...], stay, NT)
    made = dot_split(packed.table, halves(nodes))
    out_ref[...] = (made + main)[:COARSE]
    rhs_copy = pltpu.make_async_copy(out_ref, rhs_out, sem.at[1])
    rhs_copy.start()
    for copy in [sol_copy, rhs_copy] + copies:
        copy.wait()


def call(kernel, outs, args, spaces, out_spaces=None, scratch=(), flops=0, limit=VMEM_LIMIT):
    bytes_in = sum(a.size * a.dtype.itemsize for a in args)
    bytes_out = sum(o.size * o.dtype.itemsize for o in outs)
    out_spaces = out_spaces or [pltpu.VMEM] * len(outs)
    return pl.pallas_call(
        kernel,
        out_shape=tuple(outs),
        in_specs=[pl.BlockSpec(memory_space=space) for space in spaces],
        out_specs=tuple(pl.BlockSpec(memory_space=space) for space in out_spaces),
        scratch_shapes=list(scratch),
        compiler_params=pltpu.CompilerParams(vmem_limit_bytes=limit),
        cost_estimate=pl.CostEstimate(
            flops=flops, bytes_accessed=bytes_in + bytes_out, transcendentals=0
        ),
    )(*args)


def struct(shape, dtype):
    return jax.ShapeDtypeStruct(shape, dtype)


def block_table(table, copies, tall):
    out = []
    for part in split_table(table):
        full = np.zeros((copies * tall, copies * table.shape[1]), BF16)
        for copy in range(copies):
            full[
                copy * tall : copy * tall + table.shape[0],
                copy * table.shape[1] : (copy + 1) * table.shape[1],
            ] = part
        out.append(full)
    return np.concatenate(out, 0)


def per_device(start, rhs, diag_block, precond, lift, neighbour, orient, owner, slot):
    count = start.shape[1]
    staying = count // 4
    aggregates = count // 2
    owner_count = lax.axis_size("dom")
    slabs = lax.axis_size("face")
    movers = count - staying
    capacity = 2 * ((movers + owner_count - 2) // (owner_count - 1))
    depth = ceil_to(-(-capacity // GROUP), 8)
    capacity = ceil_to(capacity, 4)
    chunk = 6 * capacity
    entries = 6 * 128
    owner = owner.reshape(1, count)
    slot = slot.reshape(1, count)
    table = jnp.asarray(block_table(restrict_table(), GROUP, 32))
    pairs = [(i, i ^ 1) for i in range(slabs)]
    others = [(i, (i + 1 if i % 2 else i - 1) % slabs) for i in range(slabs)]

    def exchange(values):
        return lax.ppermute(values, "face", pairs), lax.ppermute(values, "face", others)

    args = [diag_block, precond, start, rhs, lift, neighbour, orient, owner, slot]
    outs = [struct((176, count), BF16), struct((PACKED, count), F32)]
    held = [each for each in args if each is not rhs]
    message, pack = call(
        lambda *refs: smooth_kernel(staying, owner_count, *refs),
        outs,
        args,
        [pl.ANY] * len(args),
        [pl.ANY] * len(outs),
        scratch=[pltpu.VMEM(each.shape, each.dtype) for each in held + outs]
        + [
            pltpu.SemaphoreType.DMA((7,)),
            pltpu.SemaphoreType.DMA(()),
            pltpu.SemaphoreType.DMA(()),
            pltpu.SemaphoreType.DMA((2,)),
        ],
        flops=100_000_000,
        limit=FIRST_LIMIT,
    )
    first, second = exchange(message)
    made, local_op = call(
        lambda *refs: galerkin_kernel(staying, capacity, *refs),
        [struct((owner_count, chunk, 128), BF16), struct((entries, count), BF16)],
        [diag_block, pack, table],
        [pltpu.VMEM] * 3,
        scratch=[pltpu.VMEM((entries, count), F32)],
        flops=1_000_000_000,
    )
    sol, rest, rim = call(
        middle_kernel,
        [struct((NODES, count), F32), struct((NODES, count), F32), struct((16, count), F32)],
        [first, second, message, diag_block, precond, pack, made],
        [pltpu.VMEM] * 6 + [pl.ANY],
        scratch=[pltpu.VMEM((NODES, count), F32)],
        flops=200_000_000,
    )
    first, second = exchange(rim)
    low, send = call(
        lambda *refs: send_kernel(staying, *refs),
        [struct((NODES, count), BF16), struct((owner_count, chunk + depth, 128), BF16)],
        [first, second, rest, pack, made],
        [pltpu.VMEM] * 5,
        flops=50_000_000,
    )
    got = lax.all_to_all(send, "dom", split_axis=0, concat_axis=0, tiled=True)
    outs = [
        struct((NODES, count), F32),
        struct((aggregates, COARSE * COARSE), F32),
        struct((COARSE, aggregates), F32),
    ]
    sol, coarse_op, coarse_rhs = call(
        lambda *refs: last_kernel(staying, depth, *refs),
        outs,
        [got, local_op, low, pack, sol],
        [pltpu.VMEM] * 5,
        [pl.ANY] * 3,
        scratch=[pltpu.VMEM(each.shape, each.dtype) for each in outs[1:]]
        + [pltpu.SemaphoreType.DMA((2,)), pltpu.SemaphoreType.DMA((3,))],
        flops=100_000_000,
    )
    return (sol, coarse_op.T, coarse_rhs)


def solution(mesh):
    return jax.shard_map(
        per_device,
        mesh=mesh,
        in_specs=(
            P(None, ("dom", "face")),
            P(None, ("dom", "face")),
            P(None, None, ("dom", "face")),
            P(None, None, ("dom", "face")),
            P(),
            P(None, ("dom", "face")),
            P(None, ("dom", "face")),
            P(("dom", "face")),
            P(("dom", "face")),
        ),
        out_specs=(P(None, ("dom", "face")), P(None, ("dom", "face")), P(None, ("dom", "face"))),
        check_vma=False,
    )
```

```python
import jax
import jax.numpy as jnp
import numpy as np
from jax import lax
from jax.experimental import pallas as pl
from jax.experimental.pallas import tpu as pltpu
from jax.sharding import PartitionSpec as P

SWEEPS = 2
NODES = 64
COARSE = 27
FACES = 6
GROUP = 4
SPLIT = 23
CUT = 15
RIM_ROWS = ((0, 64),)
F32 = jnp.float32
BF16 = jnp.bfloat16
VMEM_LIMIT = 24 * 1024 * 1024
FIRST_LIMIT = None

NN = (((1,), (0,)), ((), ()))
NT = (((1,), (1,)), ((), ()))
TN = (((0,), (0,)), ((), ()))


def restrict_line():
    fine = np.array([-1.0, -1.0 / np.sqrt(5.0), 1.0 / np.sqrt(5.0), 1.0])
    coarse = np.array([-1.0, 0.0, 1.0])
    basis = np.ones((4, 3))
    for column in range(3):
        for other in range(3):
            if other != column:
                basis[:, column] *= (fine - coarse[other]) / (coarse[column] - coarse[other])
    return basis.T


def restrict_table():
    line = restrict_line()
    return np.kron(np.kron(line, line), line)


def split_table(table):
    table = table.astype(np.float32)
    high = table.astype(BF16)
    low = (table - high.astype(np.float32)).astype(BF16)
    return high, low


def ceil_to(value, step):
    return -(-value // step) * step


def halves(values):
    high = values.astype(BF16)
    low = (values - high.astype(F32)).astype(BF16)
    return high, low


def dot(left, right, dims):
    return lax.dot_general(left, right, dims, preferred_element_type=F32)


def dot_split(left, right):
    left_high, left_low = halves(left)
    right_high, right_low = right
    size = left.shape[0]
    both = dot(jnp.concatenate([left_high, left_low], 0), right_high, NN)
    return both[:size] + both[size:] + dot(left_high, right_low, NN)


def small_table():
    shape = (32, NODES)
    line = restrict_line()
    row, col = rows(shape), lanes(shape)
    step = 9
    table = jnp.ones(shape, F32)
    place = jnp.where(row > CUT, row - 1, row)
    left = place
    for digit in range(3):
        mine = (left >= step).astype(jnp.int32) + (left >= 2 * step).astype(jnp.int32)
        left = left - step * mine
        fine = (col >> (4 - 2 * digit)) & 3
        value = jnp.zeros(shape, F32)
        for i in range(3):
            for j in range(4):
                value = jnp.where((mine == i) & (fine == j), float(line[i, j]), value)
        table = table * value
        step //= 3
    return jnp.where((row != CUT) & (place < COARSE), table, 0.0)


def lanes(shape):
    return lax.broadcasted_iota(jnp.int32, shape, 1)


def rows(shape):
    return lax.broadcasted_iota(jnp.int32, shape, 0)


def face_traces(ref):
    return [
        ref[0:16],
        ref[48:64],
        jnp.concatenate([ref[16 * i : 16 * i + 4] for i in range(4)], 0),
        jnp.concatenate([ref[16 * i + 12 : 16 * i + 16] for i in range(4)], 0),
        ref[pl.ds(0, 16, stride=4)],
        ref[pl.ds(3, 16, stride=4)],
    ]


def take(values, index, axis):
    return jnp.take_along_axis(values, index, axis=axis, mode="promise_in_bounds")


def turn(values, orient_row):
    shape = values.shape
    orient = jnp.broadcast_to(orient_row, shape)
    place = rows(shape)
    first = (place >> 2) ^ ((orient & 1) * 3)
    second = (place & 3) ^ (((orient >> 1) & 1) * 3)
    flip = (orient & 4) > 0
    source = jnp.where(flip, 4 * second + first, 4 * first + second)
    out = []
    for half in (source[:8], source[8:]):
        within = half & 7
        out.append(jnp.where(half >= 8, take(values[8:], within, 0), take(values[:8], within, 0)))
    return jnp.concatenate(out, 0)


def pick(traces, neighbour_ref, face):
    values = traces[face ^ 1]
    count = values.shape[1]
    index = jnp.clip(neighbour_ref[face : face + 1] - (face ^ 1) * count, 0, count - 1)
    return take(values, jnp.broadcast_to(index, values.shape), 1)


def fold(parts):
    place = rows(parts[0].shape)
    step = 1
    while len(parts) > 1:
        even = (place & step) == 0
        parts = [
            jnp.where(even, x, y) + pltpu.roll(jnp.where(even, y, x), step, 0)
            for x, y in zip(parts[::2], parts[1::2])
        ]
        step *= 2
    return parts[0]


def block_row(ref, node, tiles):
    return jnp.sum(ref[node].astype(F32).reshape(tiles.shape) * tiles, axis=0)


def apply_blocks(ref, values):
    tiles = values.reshape(NODES // 8, 8, values.shape[1])
    out = []
    for group in range(NODES // 8):
        out.append(fold([block_row(ref, node, tiles) for node in range(8 * group, 8 * group + 8)]))
    return jnp.concatenate(out, 0)


def pack_rim(traces):
    shape = traces[2].shape
    return jnp.where(lanes(shape) < shape[1] // 2, traces[2], traces[3])


def coupling(traces, below, above, neighbour_ref, orient_ref, lift):
    count = below.shape[1]
    edge = count // 4
    turned = []
    for face in range(FACES):
        values = pick(traces, neighbour_ref, face)
        if face == 2:
            values = jnp.where(lanes(values.shape) < edge, below, values)
        if face == 3:
            values = jnp.where(lanes(values.shape) >= count - edge, above, values)
        turned.append(turn(values, orient_ref[face : face + 1]))
    turned = jnp.concatenate(turned + [jnp.zeros((count - FACES * 16, count), F32)], 0)
    return dot_split(lift, halves(turned))


def both_halves(shape, low, high):
    return jnp.where(lanes(shape) < shape[1] // 2, low, high)


def response(precond_ref, edge):
    count = precond_ref.shape[2]
    parts = []
    for lift in (edge[0:16], edge[16:32]):
        parts.extend(halves(lift))
    stack = jnp.concatenate(parts, 0)
    shape = (NODES, count)
    out = []
    for spot in range(16):
        node = 16 * (spot // 4) + spot % 4
        block = both_halves(shape, precond_ref[node].astype(F32), precond_ref[node + 12].astype(F32))
        made = dot(stack, block.astype(BF16), NN)
        out.append(
            both_halves((16, count), made[0:16] + made[16:32], made[32:48] + made[48:64])
        )
    return out


def halo_lift(below, above, orient_ref, lift):
    shape = below.shape
    edge = shape[1] // 4
    low = jnp.where(lanes(shape) < edge, turn(below, orient_ref[2:3]), 0.0)
    high = jnp.where(lanes(shape) >= shape[1] - edge, turn(above, orient_ref[3:4]), 0.0)
    none = jnp.zeros((32, shape[1]), F32)
    rest = jnp.zeros((shape[1] - 64, shape[1]), F32)
    return dot_split(lift, halves(jnp.concatenate([none, low, high, rest], 0)))


RHS = 0
START = NODES
RESID = 2 * NODES
LIFT = 3 * NODES
EDGE = LIFT + NODES
TABLE = EDGE + 32
NEIGHBOUR = TABLE + 32
ORIENT = NEIGHBOUR + 8
OWNER = ORIENT + 8
RANK = OWNER + 1
SLOT = OWNER + 2
PACKED = ORIENT + 16


class Packed:
    def __init__(self, ref):
        self.rhs = ref.at[RHS : RHS + NODES]
        self.start = ref.at[START : START + NODES]
        self.resid = ref.at[RESID : RESID + NODES]
        self.lift = ref[LIFT : LIFT + NODES]
        self.table = ref[TABLE : TABLE + 32, 0:NODES]
        self.neighbour = ref[NEIGHBOUR : NEIGHBOUR + FACES].astype(jnp.int32)
        self.orient = ref[ORIENT : ORIENT + FACES].astype(jnp.int32)
        self.owner = ref[OWNER : OWNER + 1].astype(jnp.int32)
        self.rank = ref[RANK : RANK + 1].astype(jnp.int32)
        self.slot = ref[SLOT : SLOT + 1].astype(jnp.int32)

    def target(self, staying, capacity):
        return jnp.where(lanes(self.owner.shape) >= staying, self.owner * capacity + self.rank, -1)


def smooth_kernel(
    staying, owner_count,
    diag_in, precond_in, start_in, rhs_in, lift_in, neighbour_in, orient_in, owner_in, slot_in, table_in,
    first_out, second_out, pack_out,
    diag_ref, precond_ref, lift_ref, neighbour_ref, orient_ref, owner_ref, slot_ref,
    first_ref, second_ref, pack_ref, sem, diag_sem, precond_sem, out_sem,
):
    count = diag_ref.shape[2]
    start_ref = pack_ref.at[START : START + NODES]
    pairs = [
        (start_in, start_ref), (neighbour_in, neighbour_ref), (orient_in, orient_ref), (lift_in, lift_ref),
        (rhs_in, pack_ref.at[RHS : RHS + NODES]), (owner_in, owner_ref), (slot_in, slot_ref),
    ]
    copies = [pltpu.make_async_copy(src, dst, sem.at[i]) for i, (src, dst) in enumerate(pairs)]
    diag_copy = pltpu.make_async_copy(diag_in, diag_ref, diag_sem)
    precond_copies = []
    for part, (begin, end) in enumerate(RIM_ROWS):
        at = pl.ds(begin, end - begin)
        precond_copies.append(
            pltpu.make_async_copy(precond_in.at[at], precond_ref.at[at], precond_sem.at[part])
        )
    for copy in copies + [diag_copy] + precond_copies:
        copy.start()
    for copy in copies:
        copy.wait()
    stacked = lift_ref[...].reshape(FACES * 16, NODES)
    lift = jnp.concatenate([stacked, jnp.zeros((count - FACES * 16, NODES), F32)], 0).T
    pack_ref[LIFT : LIFT + NODES] = lift
    pack_ref[EDGE : EDGE + 32, 0:NODES] = stacked[32:64]
    pack_ref[TABLE : TABLE + 32, 0:NODES] = small_table()
    pack_ref[NEIGHBOUR : NEIGHBOUR + FACES] = neighbour_ref[...].astype(F32)
    pack_ref[ORIENT : ORIENT + FACES] = orient_ref[...].astype(F32)
    owner = owner_ref[...]
    rank = rank_row(owner, staying, owner_count)
    pack_ref[OWNER : OWNER + 1] = owner.astype(F32)
    pack_ref[RANK : RANK + 1] = rank.astype(F32)
    pack_ref[SLOT : SLOT + 1] = slot_ref[...].astype(F32)
    traces = face_traces(start_ref)
    shape = traces[2].shape
    none = jnp.zeros(shape, F32)
    coupled = coupling(traces, none, none, neighbour_ref[...], orient_ref[...], lift)
    orient = both_halves((1, count), orient_ref[2:3], orient_ref[3:4])
    even = lax.rem(lax.axis_index("face"), 2) == 0

    def write(at, values):
        low, high = fold_lanes(values)
        first_ref[at : at + 16] = jnp.where(even, high, low).astype(BF16)
        second_ref[at : at + 16] = jnp.where(even, low, high).astype(BF16)

    write(16, [jnp.broadcast_to(orient.astype(F32), shape)] * GROUP)
    diag_copy.wait()
    resid = pack_ref[RHS : RHS + NODES] - (apply_blocks(diag_ref, start_ref[...]) - coupled)
    pack_ref[RESID : RESID + NODES] = resid
    pack_copy = pltpu.make_async_copy(pack_ref, pack_out, out_sem.at[0])
    pack_copy.start()
    for copy in precond_copies:
        copy.wait()
    reply = response(precond_ref, stacked[32:64])
    for q in range(4):
        write(32 + 16 * q, reply[GROUP * q : GROUP * q + GROUP])
    tiles = resid.reshape(NODES // 8, 8, count)
    steps = []
    for i in range(4):
        nodes = [16 * i + k for k in range(4)] + [16 * i + 12 + k for k in range(4)]
        steps.append(fold([block_row(precond_ref, node, tiles) for node in nodes]))
    change = both_halves(
        shape,
        jnp.concatenate([step[0:4] for step in steps], 0),
        jnp.concatenate([step[4:8] for step in steps], 0),
    )
    parts = []
    for values in (pack_rim(traces), pack_rim(traces) + change):
        high, low = halves(values)
        parts.extend([high.astype(F32), low.astype(F32)])
    write(0, parts)
    message_copies = [
        pltpu.make_async_copy(first_ref, first_out, out_sem.at[1]),
        pltpu.make_async_copy(second_ref, second_out, out_sem.at[2]),
    ]
    for copy in message_copies:
        copy.start()
    for copy in [pack_copy] + message_copies:
        copy.wait()


def sides(first, second):
    pos, slabs = lax.axis_index("face"), lax.axis_size("face")
    even = lax.rem(pos, 2) == 0
    above = jnp.where(even, first, second)
    below = jnp.where(even, second, first)
    return jnp.where(pos < slabs - 1, above, 0.0), jnp.where(pos > 0, below, 0.0)


def fold_lanes(values):
    shape = values[0].shape
    edge = shape[1] // GROUP
    rolled = [values[0]] + [pltpu.roll(values[g], g * edge, 1) for g in range(1, GROUP)]
    group = lanes(shape) // edge
    low, high = rolled[0], rolled[1]
    for g in range(1, GROUP):
        low = jnp.where(group == g, rolled[g], low)
        high = jnp.where(group == g, rolled[(g + 1) % GROUP], high)
    return low, high


def unfold_lanes(above, below):
    shape = above.shape
    edge = shape[1] // GROUP
    out = []
    for g in range(GROUP):
        if g:
            up = pltpu.roll(above, shape[1] - g * edge, 1)
            down = pltpu.roll(below, shape[1] - g * edge, 1)
        else:
            up, down = above, below
        out.append(both_halves(shape, up, down))
    return out


def aside(values):
    count = values.shape[1]
    return pltpu.roll(values, count // 4, 1), pltpu.roll(values, count - count // 4, 1)


def middle_kernel(
    first_ref, second_ref, diag_ref, precond_ref, pack_ref, partial_ref,
    new_ref, rim_ref, sol_ref,
):
    count = diag_ref.shape[2]
    shape = (16, count)
    packed = Packed(pack_ref)
    rhs_ref = packed.rhs
    lift, neighbour_ref, orient_ref = packed.lift, packed.neighbour, packed.orient
    above, below = sides(first_ref[...].astype(F32), second_ref[...].astype(F32))
    head_high, head_low, later_high, later_low = unfold_lanes(above[0:16], below[0:16])
    head, later = head_high + head_low, later_high + later_low
    orient = both_halves((16, count), above[16:32], below[16:32])[0:1].astype(jnp.int32)
    from_high, from_low = aside(pack_rim(face_traces(packed.start)))
    sent = turn(both_halves(shape, from_high, from_low), orient)
    reply = []
    for q in range(4):
        at = slice(32 + 16 * q, 48 + 16 * q)
        reply.extend(unfold_lanes(above[at], below[at]))
    below, above = aside(head)
    delta = halo_lift(below, above, orient_ref, lift)
    sol_ref[...] = partial_ref[...] + apply_blocks(precond_ref, delta)
    change = [block * sent for block in reply]
    change = [block[:8] + block[8:] for block in change]
    change = jnp.concatenate([fold(change[:8]), fold(change[8:])], 0)
    below, above = aside(later + change)
    traces = face_traces(sol_ref)
    coupled = coupling(traces, below, above, neighbour_ref, orient_ref, lift)
    resid = rhs_ref[...] - (apply_blocks(diag_ref, sol_ref[...]) - coupled)
    new_ref[...] = sol_ref[...] + apply_blocks(precond_ref, resid)
    rim_ref[...] = pack_rim(face_traces(new_ref))


def rest_kernel(diag_ref, pack_ref, sol_ref, rest_ref):
    packed = Packed(pack_ref)
    traces = face_traces(sol_ref)
    none = jnp.zeros(traces[2].shape, F32)
    coupled = coupling(traces, none, none, packed.neighbour, packed.orient, packed.lift)
    rest_ref[...] = packed.rhs[...] - (apply_blocks(diag_ref, sol_ref[...]) - coupled)


def send_kernel(first_ref, second_ref, rest_ref, pack_ref, made_ref, hits_ref, low_ref, send_ref):
    packed = Packed(pack_ref)
    owners, size, count = made_ref.shape
    both = size // 3
    above, below = sides(first_ref[...], second_ref[...])
    below, above = aside(below)[0], aside(above)[1]
    low = (rest_ref[...] + halo_lift(below, above, packed.orient, packed.lift)).astype(BF16)
    low_ref[...] = low
    table_high, table_low = halves(packed.table)
    made = dot(jnp.concatenate([table_high, table_low], 0), low, NN)
    made = (made[:32] + made[32:]).astype(BF16)
    none = jnp.zeros((count - 16, count), BF16)
    wide = jnp.concatenate(
        [jnp.concatenate([none, made[:16]], 0), jnp.concatenate([none, made[16:]], 0)], 1
    )
    extra = dot(hits_ref[...], wide, NT).reshape(owners, both, count)
    send_ref[:, 0 : 2 * both] = made_ref[:, 0 : 2 * both]
    send_ref[:, 2 * both :] = (made_ref[:, 2 * both :].astype(F32) + extra).astype(BF16)


def rank_row(owner_row, staying, owner_count):
    count = owner_row.shape[1]
    shape = (owner_count, count)
    hits = (rows(shape) == owner_row) & (lanes(shape) >= staying)
    hits = jnp.where(hits, 1.0, 0.0)
    before = jnp.where(rows((count, count)) < lanes((count, count)), 1.0, 0.0)
    earlier = dot(hits.astype(BF16), before.astype(BF16), NN)
    return jnp.sum(hits * earlier, axis=0, keepdims=True).astype(jnp.int32)


def one_hot(condition):
    return jnp.where(condition, 1.0, 0.0).astype(BF16)


def contract(four, line):
    first, second = float(line[0, 1]), float(line[0, 2])
    middle = float(line[1, 1])
    return [
        four[0] + first * four[1] + second * four[2],
        middle * (four[1] + four[2]),
        four[3] + second * four[1] + first * four[2],
    ]


def galerkin_kernel(
    staying, capacity, diag_ref, precond_ref, pack_ref, table_ref,
    send_ref, local_ref, hits_ref, partial_ref, full_ref,
):
    line = restrict_line()
    count = diag_ref.shape[2]
    owner_count = send_ref.shape[0]
    packed = Packed(pack_ref)
    partial_ref[...] = packed.start[...] + apply_blocks(precond_ref, packed.resid[...])
    target = packed.target(staying, capacity)
    twice = jnp.concatenate([target, target], 1)
    shape = (2 * capacity, 2 * count)
    upper = (rows(shape) >= capacity).astype(jnp.int32)
    place = rows(shape) - capacity * upper
    place = jnp.where(upper == (lanes(shape) >= count).astype(jnp.int32), place, -2 * owner_count * capacity)
    hits = jnp.concatenate([one_hot(place + capacity * o == twice) for o in range(owner_count)], 0)
    hits_ref[...] = hits
    table = table_ref[...]
    padded = table.shape[0] // 2
    tall = padded // GROUP
    planes = []
    for i in range(4):
        bars = []
        for half in range(2):
            first = 2 * GROUP * (2 * i + half)
            wide = [
                diag_ref[first + GROUP * j : first + GROUP * j + GROUP].reshape(GROUP * NODES, count)
                for j in range(2)
            ]
            both = dot(table, jnp.concatenate(wide, 1), NN)
            made = both[:padded] + both[padded:]
            for j in range(2):
                four = [made[tall * k : tall * k + tall, count * j : count * j + count] for k in range(4)]
                bars.append(contract(four, line))
        sheet = [contract([bars[j][k] for j in range(4)], line) for k in range(3)]
        planes.append([sheet[k][j] for j in range(3) for k in range(3)])
    made = [contract([planes[i][rest] for i in range(4)], line) for rest in range(9)]
    full_ref[5 * 128 - 16 : 5 * 128] = jnp.zeros((16, count), F32)
    for c in range(COARSE):
        at = COARSE * c if c < SPLIT else 5 * 128 + COARSE * (c - SPLIT)
        full_ref[at : at + tall] = made[c % 9][c // 9]
    full_ref[5 * 128 + COARSE * (COARSE - SPLIT) :] = jnp.zeros((128 - COARSE * (COARSE - SPLIT), count), F32)
    slot = (packed.slot + 1).astype(F32)
    full_ref[5 * 128 - 1 : 5 * 128] = slot
    full_ref[6 * 128 - 1 : 6 * 128] = slot
    local = full_ref[...].astype(BF16)
    local_ref[...] = local
    for pair in range(3):
        wide = jnp.concatenate([local[256 * pair : 256 * pair + 128], local[256 * pair + 128 : 256 * pair + 256]], 1)
        made = dot(hits, wide, NT).reshape(owner_count, 2 * capacity, 128).astype(BF16)
        send_ref[:, 2 * capacity * pair : 2 * capacity * pair + 2 * capacity] = made


def last_kernel(
    staying, got_ref, local_ref, low_ref, pack_ref, sol_ref,
    sol_out, op_out, rhs_out,
    op_ref, out_ref, sem, op_sem,
):
    sol_copy = pltpu.make_async_copy(sol_ref, sol_out, sem.at[0])
    sol_copy.start()
    packed = Packed(pack_ref)
    aggregates = op_ref.shape[0]
    owners, size, count = got_ref.shape
    both = size // 3
    capacity = both // 2
    shape = (aggregates, low_ref.shape[1])
    stay = one_hot((rows(shape) == packed.slot) & (lanes(shape) < staying))
    ids = got_ref[:, 2 * both : size].astype(F32).reshape(owners * both, count)[:, count - 1 : count]
    shape = (owners * both, 2 * aggregates)
    column = lanes(shape)
    column = jnp.where(column >= aggregates, column - aggregates, column)
    hits = jnp.where(ids == (column + 1).astype(F32), 1.0, 0.0).reshape(owners, both, 2 * aggregates)
    shape = (owners, both, 2 * aggregates)
    upper = lax.broadcasted_iota(jnp.int32, shape, 1) >= capacity
    right = lax.broadcasted_iota(jnp.int32, shape, 2) >= aggregates
    paired = jnp.where(upper == right, hits, 0.0).reshape(owners * both, 2 * aggregates).astype(BF16)
    cut = SPLIT * COARSE
    copies = []
    for pair in (2, 0, 1):
        block = got_ref[:, both * pair : both * pair + both].astype(F32).reshape(owners * both, count).astype(BF16)
        total = dot(paired, block, TN)
        out = []
        for side in range(2):
            at = 128 * (2 * pair + side)
            out.append(
                total[aggregates * side : aggregates * side + aggregates] + dot(stay, local_ref[at : at + 128], NT)
            )
        first, last = 256 * pair, min(256 * pair + 256, COARSE * COARSE)
        middle = cut if pair == 2 else first + 128
        op_ref[:, first:middle] = out[0][:, : middle - first]
        op_ref[:, middle:last] = out[1][:, : last - middle]
        some = pl.ds(first, last - first)
        copies.append(pltpu.make_async_copy(op_ref.at[:, some], op_out.at[:, some], op_sem.at[pair]))
        copies[-1].start()
        if pair == 2:
            nodes = dot(low_ref[...], stay, NT)
            made = dot_split(packed.table, halves(nodes))
            sums = [made[16 * side : 16 * side + 16] + out[side].T[count - 16 :] for side in range(2)]
            out_ref[0:CUT] = sums[0][0:CUT]
            out_ref[CUT:COARSE] = sums[1][0 : COARSE - CUT]
            copies.append(pltpu.make_async_copy(out_ref, rhs_out, sem.at[1]))
            copies[-1].start()
    for copy in [sol_copy] + copies:
        copy.wait()


def call(kernel, outs, args, spaces, out_spaces=None, scratch=(), flops=0, limit=VMEM_LIMIT):
    bytes_in = sum(a.size * a.dtype.itemsize for a in args)
    bytes_out = sum(o.size * o.dtype.itemsize for o in outs)
    out_spaces = out_spaces or [pltpu.VMEM] * len(outs)
    return pl.pallas_call(
        kernel,
        out_shape=tuple(outs),
        in_specs=[pl.BlockSpec(memory_space=space) for space in spaces],
        out_specs=tuple(pl.BlockSpec(memory_space=space) for space in out_spaces),
        scratch_shapes=list(scratch),
        compiler_params=pltpu.CompilerParams(vmem_limit_bytes=limit),
        cost_estimate=pl.CostEstimate(
            flops=flops, bytes_accessed=bytes_in + bytes_out, transcendentals=0
        ),
    )(*args)


def struct(shape, dtype):
    return jax.ShapeDtypeStruct(shape, dtype)


def block_table(table, copies, tall):
    out = []
    for part in split_table(table):
        full = np.zeros((copies * tall, copies * table.shape[1]), BF16)
        for copy in range(copies):
            full[
                copy * tall : copy * tall + table.shape[0],
                copy * table.shape[1] : (copy + 1) * table.shape[1],
            ] = part
        out.append(full)
    return np.concatenate(out, 0)


def per_device(start, rhs, diag_block, precond, lift, neighbour, orient, owner, slot):
    count = start.shape[1]
    staying = count // 4
    aggregates = count // 2
    owner_count = lax.axis_size("dom")
    slabs = lax.axis_size("face")
    movers = count - staying
    capacity = 2 * ((movers + owner_count - 2) // (owner_count - 1))
    capacity = ceil_to(capacity, 4)
    chunk = 6 * capacity
    entries = 6 * 128
    owner = owner.reshape(1, count)
    slot = slot.reshape(1, count)
    table = jnp.asarray(block_table(restrict_table(), GROUP, 32))
    pairs = [(i, i ^ 1) for i in range(slabs)]
    others = [(i, (i + 1 if i % 2 else i - 1) % slabs) for i in range(slabs)]

    def exchange(one, other):
        return lax.ppermute(one, "face", pairs), lax.ppermute(other, "face", others)

    args = [diag_block, precond, start, rhs, lift, neighbour, orient, owner, slot, table]
    outs = [struct((96, count), BF16), struct((96, count), BF16), struct((PACKED, count), F32)]
    held = [each for each in args if each is not rhs and each is not start and each is not table]
    to_first, to_second, pack = call(
        lambda *refs: smooth_kernel(staying, owner_count, *refs),
        outs,
        args,
        [pl.ANY] * len(args),
        [pl.ANY] * len(outs),
        scratch=[pltpu.VMEM(each.shape, each.dtype) for each in held + outs]
        + [
            pltpu.SemaphoreType.DMA((7,)),
            pltpu.SemaphoreType.DMA(()),
            pltpu.SemaphoreType.DMA((len(RIM_ROWS),)),
            pltpu.SemaphoreType.DMA((3,)),
        ],
        flops=100_000_000,
        limit=FIRST_LIMIT,
    )
    first, second = exchange(to_first, to_second)
    made, local_op, hits, partial = call(
        lambda *refs: galerkin_kernel(staying, capacity, *refs),
        [
            struct((owner_count, chunk, 128), BF16),
            struct((entries, count), BF16),
            struct((2 * capacity * owner_count, 2 * count), BF16),
            struct((NODES, count), F32),
        ],
        [diag_block, precond, pack, table],
        [pltpu.VMEM] * 4,
        scratch=[pltpu.VMEM((entries, count), F32)],
        flops=1_000_000_000,
    )
    sol, rim = call(
        middle_kernel,
        [struct((NODES, count), F32), struct((16, count), F32)],
        [first, second, diag_block, precond, pack, partial],
        [pltpu.VMEM] * 6,
        scratch=[pltpu.VMEM((NODES, count), F32)],
        flops=200_000_000,
    )
    first, second = exchange(rim, rim)
    (rest,) = call(
        rest_kernel,
        [struct((NODES, count), F32)],
        [diag_block, pack, sol],
        [pltpu.VMEM] * 3,
        flops=1_000_000_000,
    )
    low, send = call(
        send_kernel,
        [struct((NODES, count), BF16), struct((owner_count, chunk, 128), BF16)],
        [first, second, rest, pack, made, hits],
        [pltpu.VMEM] * 6,
        flops=50_000_000,
    )
    got = lax.all_to_all(send, "dom", split_axis=0, concat_axis=0, tiled=True)
    outs = [
        struct((NODES, count), F32),
        struct((aggregates, COARSE * COARSE), F32),
        struct((COARSE, aggregates), F32),
    ]
    sol, coarse_op, coarse_rhs = call(
        lambda *refs: last_kernel(staying, *refs),
        outs,
        [got, local_op, low, pack, sol],
        [pltpu.VMEM] * 5,
        [pl.ANY] * 3,
        scratch=[pltpu.VMEM(each.shape, each.dtype) for each in outs[1:]]
        + [pltpu.SemaphoreType.DMA((2,)), pltpu.SemaphoreType.DMA((3,))],
        flops=100_000_000,
    )
    return (sol, coarse_op.T, coarse_rhs)


def solution(mesh):
    return jax.shard_map(
        per_device,
        mesh=mesh,
        in_specs=(
            P(None, ("dom", "face")),
            P(None, ("dom", "face")),
            P(None, None, ("dom", "face")),
            P(None, None, ("dom", "face")),
            P(),
            P(None, ("dom", "face")),
            P(None, ("dom", "face")),
            P(("dom", "face")),
            P(("dom", "face")),
        ),
        out_specs=(P(None, ("dom", "face")), P(None, ("dom", "face")), P(None, ("dom", "face"))),
        check_vma=False,
    )
```

```python
import jax
import jax.numpy as jnp
import numpy as np
from jax import lax
from jax.experimental import pallas as pl
from jax.experimental.pallas import tpu as pltpu
from jax.sharding import PartitionSpec as P

SWEEPS = 2
NODES = 64
COARSE = 27
FACES = 6
GROUP = 4
SPLIT = 23
CUT = 15
RIM_ROWS = ((0, 64),)
F32 = jnp.float32
BF16 = jnp.bfloat16
VMEM_LIMIT = 24 * 1024 * 1024
FIRST_LIMIT = None

NN = (((1,), (0,)), ((), ()))
NT = (((1,), (1,)), ((), ()))
TN = (((0,), (0,)), ((), ()))


def restrict_line():
    fine = np.array([-1.0, -1.0 / np.sqrt(5.0), 1.0 / np.sqrt(5.0), 1.0])
    coarse = np.array([-1.0, 0.0, 1.0])
    basis = np.ones((4, 3))
    for column in range(3):
        for other in range(3):
            if other != column:
                basis[:, column] *= (fine - coarse[other]) / (coarse[column] - coarse[other])
    return basis.T


def restrict_table():
    line = restrict_line()
    return np.kron(np.kron(line, line), line)


def split_table(table):
    table = table.astype(np.float32)
    high = table.astype(BF16)
    low = (table - high.astype(np.float32)).astype(BF16)
    return high, low


def ceil_to(value, step):
    return -(-value // step) * step


def halves(values):
    high = values.astype(BF16)
    low = (values - high.astype(F32)).astype(BF16)
    return high, low


def dot(left, right, dims):
    return lax.dot_general(left, right, dims, preferred_element_type=F32)


def dot_split(left, right):
    left_high, left_low = halves(left)
    right_high, right_low = right
    size = left.shape[0]
    both = dot(jnp.concatenate([left_high, left_low], 0), right_high, NN)
    return both[:size] + both[size:] + dot(left_high, right_low, NN)


def small_table():
    shape = (32, NODES)
    line = restrict_line()
    row, col = rows(shape), lanes(shape)
    step = 9
    table = jnp.ones(shape, F32)
    place = jnp.where(row > CUT, row - 1, row)
    left = place
    for digit in range(3):
        mine = (left >= step).astype(jnp.int32) + (left >= 2 * step).astype(jnp.int32)
        left = left - step * mine
        fine = (col >> (4 - 2 * digit)) & 3
        value = jnp.zeros(shape, F32)
        for i in range(3):
            for j in range(4):
                value = jnp.where((mine == i) & (fine == j), float(line[i, j]), value)
        table = table * value
        step //= 3
    return jnp.where((row != CUT) & (place < COARSE), table, 0.0)


def lanes(shape):
    return lax.broadcasted_iota(jnp.int32, shape, 1)


def rows(shape):
    return lax.broadcasted_iota(jnp.int32, shape, 0)


def face_traces(ref):
    return [
        ref[0:16],
        ref[48:64],
        jnp.concatenate([ref[16 * i : 16 * i + 4] for i in range(4)], 0),
        jnp.concatenate([ref[16 * i + 12 : 16 * i + 16] for i in range(4)], 0),
        ref[pl.ds(0, 16, stride=4)],
        ref[pl.ds(3, 16, stride=4)],
    ]


def take(values, index, axis):
    return jnp.take_along_axis(values, index, axis=axis, mode="promise_in_bounds")


def turn(values, orient_row):
    shape = values.shape
    orient = jnp.broadcast_to(orient_row, shape)
    place = rows(shape)
    first = (place >> 2) ^ ((orient & 1) * 3)
    second = (place & 3) ^ (((orient >> 1) & 1) * 3)
    flip = (orient & 4) > 0
    source = jnp.where(flip, 4 * second + first, 4 * first + second)
    out = []
    for half in (source[:8], source[8:]):
        within = half & 7
        out.append(jnp.where(half >= 8, take(values[8:], within, 0), take(values[:8], within, 0)))
    return jnp.concatenate(out, 0)


def pick(traces, neighbour_ref, face):
    values = traces[face ^ 1]
    count = values.shape[1]
    index = jnp.clip(neighbour_ref[face : face + 1] - (face ^ 1) * count, 0, count - 1)
    return take(values, jnp.broadcast_to(index, values.shape), 1)


def fold(parts):
    place = rows(parts[0].shape)
    step = 1
    while len(parts) > 1:
        even = (place & step) == 0
        parts = [
            jnp.where(even, x, y) + pltpu.roll(jnp.where(even, y, x), step, 0)
            for x, y in zip(parts[::2], parts[1::2])
        ]
        step *= 2
    return parts[0]


def block_row(ref, node, tiles):
    return jnp.sum(ref[node].astype(F32).reshape(tiles.shape) * tiles, axis=0)


def apply_blocks(ref, values):
    tiles = values.reshape(NODES // 8, 8, values.shape[1])
    out = []
    for group in range(NODES // 8):
        out.append(fold([block_row(ref, node, tiles) for node in range(8 * group, 8 * group + 8)]))
    return jnp.concatenate(out, 0)


def pack_rim(traces):
    shape = traces[2].shape
    return jnp.where(lanes(shape) < shape[1] // 2, traces[2], traces[3])


def coupling(traces, below, above, neighbour_ref, orient_ref, lift):
    count = below.shape[1]
    edge = count // 4
    turned = []
    for face in range(FACES):
        values = pick(traces, neighbour_ref, face)
        if face == 2:
            values = jnp.where(lanes(values.shape) < edge, below, values)
        if face == 3:
            values = jnp.where(lanes(values.shape) >= count - edge, above, values)
        turned.append(turn(values, orient_ref[face : face + 1]))
    turned = jnp.concatenate(turned + [jnp.zeros((count - FACES * 16, count), F32)], 0)
    return dot_split(lift, halves(turned))


def both_halves(shape, low, high):
    return jnp.where(lanes(shape) < shape[1] // 2, low, high)


def response(precond_ref, edge):
    count = precond_ref.shape[2]
    parts = []
    for lift in (edge[0:16], edge[16:32]):
        parts.extend(halves(lift))
    stack = jnp.concatenate(parts, 0)
    shape = (NODES, count)
    out = []
    for spot in range(16):
        node = 16 * (spot // 4) + spot % 4
        block = both_halves(shape, precond_ref[node].astype(F32), precond_ref[node + 12].astype(F32))
        made = dot(stack, block.astype(BF16), NN)
        out.append(
            both_halves((16, count), made[0:16] + made[16:32], made[32:48] + made[48:64])
        )
    return out


def halo_lift(below, above, orient_ref, lift):
    shape = below.shape
    edge = shape[1] // 4
    low = jnp.where(lanes(shape) < edge, turn(below, orient_ref[2:3]), 0.0)
    high = jnp.where(lanes(shape) >= shape[1] - edge, turn(above, orient_ref[3:4]), 0.0)
    none = jnp.zeros((32, shape[1]), F32)
    rest = jnp.zeros((shape[1] - 64, shape[1]), F32)
    return dot_split(lift, halves(jnp.concatenate([none, low, high, rest], 0)))


RHS = 0
START = NODES
RESID = 2 * NODES
LIFT = 3 * NODES
EDGE = LIFT + NODES
TABLE = EDGE + 32
NEIGHBOUR = TABLE + 32
ORIENT = NEIGHBOUR + 8
OWNER = ORIENT + 8
RANK = OWNER + 1
SLOT = OWNER + 2
PACKED = ORIENT + 16


class Packed:
    def __init__(self, ref):
        self.rhs = ref.at[RHS : RHS + NODES]
        self.start = ref.at[START : START + NODES]
        self.resid = ref.at[RESID : RESID + NODES]
        self.lift = ref[LIFT : LIFT + NODES]
        self.table = ref[TABLE : TABLE + 32, 0:NODES]
        self.edge = ref[EDGE : EDGE + 32, 0:NODES]
        self.neighbour = ref[NEIGHBOUR : NEIGHBOUR + FACES].astype(jnp.int32)
        self.orient = ref[ORIENT : ORIENT + FACES].astype(jnp.int32)
        self.owner = ref[OWNER : OWNER + 1].astype(jnp.int32)
        self.rank = ref[RANK : RANK + 1].astype(jnp.int32)
        self.slot = ref[SLOT : SLOT + 1].astype(jnp.int32)

    def target(self, staying, capacity):
        return jnp.where(lanes(self.owner.shape) >= staying, self.owner * capacity + self.rank, -1)


def smooth_kernel(
    staying, owner_count,
    diag_in, precond_in, start_in, rhs_in, lift_in, neighbour_in, orient_in, owner_in, slot_in, table_in,
    first_out, second_out, pack_out,
    diag_ref, precond_ref, lift_ref, neighbour_ref, orient_ref, owner_ref, slot_ref,
    first_ref, second_ref, pack_ref, sem, diag_sem, precond_sem, out_sem,
):
    count = diag_ref.shape[2]
    start_ref = pack_ref.at[START : START + NODES]
    pairs = [
        (start_in, start_ref), (neighbour_in, neighbour_ref), (orient_in, orient_ref), (lift_in, lift_ref),
        (rhs_in, pack_ref.at[RHS : RHS + NODES]), (owner_in, owner_ref), (slot_in, slot_ref),
    ]
    copies = [pltpu.make_async_copy(src, dst, sem.at[i]) for i, (src, dst) in enumerate(pairs)]
    diag_copy = pltpu.make_async_copy(diag_in, diag_ref, diag_sem)
    precond_copies = []
    for part, (begin, end) in enumerate(RIM_ROWS):
        at = pl.ds(begin, end - begin)
        precond_copies.append(
            pltpu.make_async_copy(precond_in.at[at], precond_ref.at[at], precond_sem.at[part])
        )
    for copy in copies + [diag_copy] + precond_copies:
        copy.start()
    for copy in copies:
        copy.wait()
    stacked = lift_ref[...].reshape(FACES * 16, NODES)
    lift = jnp.concatenate([stacked, jnp.zeros((count - FACES * 16, NODES), F32)], 0).T
    pack_ref[LIFT : LIFT + NODES] = lift
    pack_ref[EDGE : EDGE + 32, 0:NODES] = stacked[32:64]
    pack_ref[TABLE : TABLE + 32, 0:NODES] = small_table()
    pack_ref[NEIGHBOUR : NEIGHBOUR + FACES] = neighbour_ref[...].astype(F32)
    pack_ref[ORIENT : ORIENT + FACES] = orient_ref[...].astype(F32)
    owner = owner_ref[...]
    rank = rank_row(owner, staying, owner_count)
    pack_ref[OWNER : OWNER + 1] = owner.astype(F32)
    pack_ref[RANK : RANK + 1] = rank.astype(F32)
    pack_ref[SLOT : SLOT + 1] = slot_ref[...].astype(F32)
    traces = face_traces(start_ref)
    shape = traces[2].shape
    none = jnp.zeros(shape, F32)
    coupled = coupling(traces, none, none, neighbour_ref[...], orient_ref[...], lift)
    orient = both_halves((1, count), orient_ref[2:3], orient_ref[3:4])
    even = lax.rem(lax.axis_index("face"), 2) == 0

    def write(at, values):
        low, high = fold_lanes(values)
        first_ref[at : at + 16] = jnp.where(even, high, low).astype(BF16)
        second_ref[at : at + 16] = jnp.where(even, low, high).astype(BF16)

    write(16, [jnp.broadcast_to(orient.astype(F32), shape)] * GROUP)
    diag_copy.wait()
    resid = pack_ref[RHS : RHS + NODES] - (apply_blocks(diag_ref, start_ref[...]) - coupled)
    pack_ref[RESID : RESID + NODES] = resid
    pack_copy = pltpu.make_async_copy(pack_ref, pack_out, out_sem.at[0])
    pack_copy.start()
    for copy in precond_copies:
        copy.wait()
    reply = response(precond_ref, stacked[32:64])
    for q in range(4):
        write(32 + 16 * q, reply[GROUP * q : GROUP * q + GROUP])
    tiles = resid.reshape(NODES // 8, 8, count)
    steps = []
    for i in range(4):
        nodes = [16 * i + k for k in range(4)] + [16 * i + 12 + k for k in range(4)]
        steps.append(fold([block_row(precond_ref, node, tiles) for node in nodes]))
    change = both_halves(
        shape,
        jnp.concatenate([step[0:4] for step in steps], 0),
        jnp.concatenate([step[4:8] for step in steps], 0),
    )
    parts = []
    for values in (pack_rim(traces), pack_rim(traces) + change):
        high, low = halves(values)
        parts.extend([high.astype(F32), low.astype(F32)])
    write(0, parts)
    message_copies = [
        pltpu.make_async_copy(first_ref, first_out, out_sem.at[1]),
        pltpu.make_async_copy(second_ref, second_out, out_sem.at[2]),
    ]
    for copy in message_copies:
        copy.start()
    for copy in [pack_copy] + message_copies:
        copy.wait()


def sides(first, second):
    pos, slabs = lax.axis_index("face"), lax.axis_size("face")
    even = lax.rem(pos, 2) == 0
    above = jnp.where(even, first, second)
    below = jnp.where(even, second, first)
    return jnp.where(pos < slabs - 1, above, 0.0), jnp.where(pos > 0, below, 0.0)


def fold_lanes(values):
    shape = values[0].shape
    edge = shape[1] // GROUP
    rolled = [values[0]] + [pltpu.roll(values[g], g * edge, 1) for g in range(1, GROUP)]
    group = lanes(shape) // edge
    low, high = rolled[0], rolled[1]
    for g in range(1, GROUP):
        low = jnp.where(group == g, rolled[g], low)
        high = jnp.where(group == g, rolled[(g + 1) % GROUP], high)
    return low, high


def unfold_lanes(above, below):
    shape = above.shape
    edge = shape[1] // GROUP
    out = []
    for g in range(GROUP):
        if g:
            up = pltpu.roll(above, shape[1] - g * edge, 1)
            down = pltpu.roll(below, shape[1] - g * edge, 1)
        else:
            up, down = above, below
        out.append(both_halves(shape, up, down))
    return out


def aside(values):
    count = values.shape[1]
    return pltpu.roll(values, count // 4, 1), pltpu.roll(values, count - count // 4, 1)


def middle_kernel(
    first_ref, second_ref, diag_ref, precond_ref, pack_ref, partial_ref, answer_ref,
    new_ref, rim_ref, sol_ref,
):
    count = diag_ref.shape[2]
    shape = (16, count)
    packed = Packed(pack_ref)
    rhs_ref = packed.rhs
    lift, neighbour_ref, orient_ref = packed.lift, packed.neighbour, packed.orient
    above, below = sides(first_ref[...].astype(F32), second_ref[...].astype(F32))
    head_high, head_low, later_high, later_low = unfold_lanes(above[0:16], below[0:16])
    head, later = head_high + head_low, later_high + later_low
    orient = both_halves((16, count), above[16:32], below[16:32])[0:1].astype(jnp.int32)
    from_high, from_low = aside(pack_rim(face_traces(packed.start)))
    sent = turn(both_halves(shape, from_high, from_low), orient)
    reply = []
    for q in range(4):
        at = slice(32 + 16 * q, 48 + 16 * q)
        reply.extend(unfold_lanes(above[at], below[at]))
    below, above = aside(head)
    edge = count // 4
    low = jnp.where(lanes(shape) < edge, turn(below, orient_ref[2:3]), 0.0)
    high = jnp.where(lanes(shape) >= count - edge, turn(above, orient_ref[3:4]), 0.0)
    arrived = low + high
    for group in range(NODES // 8):
        parts = [answer_ref[node] * arrived for node in range(8 * group, 8 * group + 8)]
        at = slice(8 * group, 8 * group + 8)
        sol_ref[at] = partial_ref[at] + fold([part[:8] + part[8:] for part in parts])
    change = [block * sent for block in reply]
    change = [block[:8] + block[8:] for block in change]
    change = jnp.concatenate([fold(change[:8]), fold(change[8:])], 0)
    below, above = aside(later + change)
    traces = face_traces(sol_ref)
    coupled = coupling(traces, below, above, neighbour_ref, orient_ref, lift)
    resid = rhs_ref[...] - (apply_blocks(diag_ref, sol_ref[...]) - coupled)
    new_ref[...] = sol_ref[...] + apply_blocks(precond_ref, resid)
    rim_ref[...] = pack_rim(face_traces(new_ref))


def stay_hits(packed, staying, aggregates):
    shape = (aggregates, packed.slot.shape[1])
    return one_hot((rows(shape) == packed.slot) & (lanes(shape) < staying))


def rest_kernel(staying, diag_ref, pack_ref, sol_ref, local_ref, rest_ref, kept_ref):
    packed = Packed(pack_ref)
    kept_ref[...] = dot(stay_hits(packed, staying, kept_ref.shape[0]), local_ref[...], NT)
    traces = face_traces(sol_ref)
    none = jnp.zeros(traces[2].shape, F32)
    coupled = coupling(traces, none, none, packed.neighbour, packed.orient, packed.lift)
    rest_ref[...] = packed.rhs[...] - (apply_blocks(diag_ref, sol_ref[...]) - coupled)


def send_kernel(first_ref, second_ref, rest_ref, pack_ref, made_ref, hits_ref, low_ref, send_ref):
    packed = Packed(pack_ref)
    owners, size, count = made_ref.shape
    both = size // 3
    above, below = sides(first_ref[...], second_ref[...])
    below, above = aside(below)[0], aside(above)[1]
    low = (rest_ref[...] + halo_lift(below, above, packed.orient, packed.lift)).astype(BF16)
    low_ref[...] = low
    table_high, table_low = halves(packed.table)
    made = dot(jnp.concatenate([table_high, table_low], 0), low, NN)
    made = (made[:32] + made[32:]).astype(BF16)
    none = jnp.zeros((count - 16, count), BF16)
    wide = jnp.concatenate(
        [jnp.concatenate([none, made[:16]], 0), jnp.concatenate([none, made[16:]], 0)], 1
    )
    extra = dot(hits_ref[...], wide, NT).reshape(owners, both, count)
    send_ref[:, 0 : 2 * both] = made_ref[:, 0 : 2 * both]
    send_ref[:, 2 * both :] = (made_ref[:, 2 * both :].astype(F32) + extra).astype(BF16)


def rank_row(owner_row, staying, owner_count):
    count = owner_row.shape[1]
    shape = (owner_count, count)
    hits = (rows(shape) == owner_row) & (lanes(shape) >= staying)
    hits = jnp.where(hits, 1.0, 0.0)
    before = jnp.where(rows((count, count)) < lanes((count, count)), 1.0, 0.0)
    earlier = dot(hits.astype(BF16), before.astype(BF16), NN)
    return jnp.sum(hits * earlier, axis=0, keepdims=True).astype(jnp.int32)


def one_hot(condition):
    return jnp.where(condition, 1.0, 0.0).astype(BF16)


def contract(four, line):
    first, second = float(line[0, 1]), float(line[0, 2])
    middle = float(line[1, 1])
    return [
        four[0] + first * four[1] + second * four[2],
        middle * (four[1] + four[2]),
        four[3] + second * four[1] + first * four[2],
    ]


def galerkin_kernel(
    staying, capacity, diag_ref, precond_ref, pack_ref, table_ref,
    send_ref, local_ref, hits_ref, partial_ref, answer_ref, full_ref,
):
    line = restrict_line()
    count = diag_ref.shape[2]
    owner_count = send_ref.shape[0]
    packed = Packed(pack_ref)
    partial_ref[...] = packed.start[...] + apply_blocks(precond_ref, packed.resid[...])
    edge = packed.edge
    stack = jnp.concatenate([part for lift in (edge[0:16], edge[16:32]) for part in halves(lift)], 0)
    none = jnp.zeros(stack.shape, BF16)
    stack = jnp.concatenate(
        [jnp.concatenate([stack if i == j else none for j in range(GROUP)], 1) for i in range(GROUP)], 0
    )
    for first in range(0, NODES, 2 * GROUP):
        wide = [
            precond_ref[first + GROUP * j : first + GROUP * j + GROUP].reshape(GROUP * NODES, count)
            for j in range(2)
        ]
        made = dot(stack, jnp.concatenate(wide, 1), NN)
        for j in range(2):
            for k in range(GROUP):
                block = made[64 * k : 64 * k + 64, count * j : count * j + count]
                answer_ref[first + GROUP * j + k] = both_halves(
                    (16, count), block[0:16] + block[16:32], block[32:48] + block[48:64]
                )
    target = packed.target(staying, capacity)
    twice = jnp.concatenate([target, target], 1)
    shape = (2 * capacity, 2 * count)
    upper = (rows(shape) >= capacity).astype(jnp.int32)
    place = rows(shape) - capacity * upper
    place = jnp.where(upper == (lanes(shape) >= count).astype(jnp.int32), place, -2 * owner_count * capacity)
    hits = jnp.concatenate([one_hot(place + capacity * o == twice) for o in range(owner_count)], 0)
    hits_ref[...] = hits
    table = table_ref[...]
    padded = table.shape[0] // 2
    tall = padded // GROUP
    planes = []
    for i in range(4):
        bars = []
        for half in range(2):
            first = 2 * GROUP * (2 * i + half)
            wide = [
                diag_ref[first + GROUP * j : first + GROUP * j + GROUP].reshape(GROUP * NODES, count)
                for j in range(2)
            ]
            both = dot(table, jnp.concatenate(wide, 1), NN)
            made = both[:padded] + both[padded:]
            for j in range(2):
                four = [made[tall * k : tall * k + tall, count * j : count * j + count] for k in range(4)]
                bars.append(contract(four, line))
        sheet = [contract([bars[j][k] for j in range(4)], line) for k in range(3)]
        planes.append([sheet[k][j] for j in range(3) for k in range(3)])
    made = [contract([planes[i][rest] for i in range(4)], line) for rest in range(9)]
    full_ref[5 * 128 - 16 : 5 * 128] = jnp.zeros((16, count), F32)
    for c in range(COARSE):
        at = COARSE * c if c < SPLIT else 5 * 128 + COARSE * (c - SPLIT)
        full_ref[at : at + tall] = made[c % 9][c // 9]
    full_ref[5 * 128 + COARSE * (COARSE - SPLIT) :] = jnp.zeros((128 - COARSE * (COARSE - SPLIT), count), F32)
    slot = (packed.slot + 1).astype(F32)
    full_ref[5 * 128 - 1 : 5 * 128] = slot
    full_ref[6 * 128 - 1 : 6 * 128] = slot
    local = full_ref[...].astype(BF16)
    local_ref[...] = local
    for pair in range(3):
        wide = jnp.concatenate([local[256 * pair : 256 * pair + 128], local[256 * pair + 128 : 256 * pair + 256]], 1)
        made = dot(hits, wide, NT).reshape(owner_count, 2 * capacity, 128).astype(BF16)
        send_ref[:, 2 * capacity * pair : 2 * capacity * pair + 2 * capacity] = made


def last_kernel(
    staying, got_ref, kept_ref, low_ref, pack_ref, sol_ref,
    sol_out, op_out, rhs_out,
    op_ref, out_ref, sem, op_sem,
):
    sol_copy = pltpu.make_async_copy(sol_ref, sol_out, sem.at[0])
    sol_copy.start()
    packed = Packed(pack_ref)
    aggregates = op_ref.shape[0]
    owners, size, count = got_ref.shape
    both = size // 3
    capacity = both // 2
    stay = stay_hits(packed, staying, aggregates)
    ids = got_ref[:, 2 * both : size].astype(F32).reshape(owners * both, count)[:, count - 1 : count]
    shape = (owners * both, 2 * aggregates)
    column = lanes(shape)
    column = jnp.where(column >= aggregates, column - aggregates, column)
    hits = jnp.where(ids == (column + 1).astype(F32), 1.0, 0.0).reshape(owners, both, 2 * aggregates)
    shape = (owners, both, 2 * aggregates)
    upper = lax.broadcasted_iota(jnp.int32, shape, 1) >= capacity
    right = lax.broadcasted_iota(jnp.int32, shape, 2) >= aggregates
    paired = jnp.where(upper == right, hits, 0.0).reshape(owners * both, 2 * aggregates).astype(BF16)
    cut = SPLIT * COARSE
    copies = []
    for pair in (2, 0, 1):
        block = got_ref[:, both * pair : both * pair + both].astype(F32).reshape(owners * both, count).astype(BF16)
        total = dot(paired, block, TN)
        out = []
        for side in range(2):
            at = 128 * (2 * pair + side)
            out.append(total[aggregates * side : aggregates * side + aggregates] + kept_ref[:, at : at + 128])
        first, last = 256 * pair, min(256 * pair + 256, COARSE * COARSE)
        middle = cut if pair == 2 else first + 128
        op_ref[:, first:middle] = out[0][:, : middle - first]
        op_ref[:, middle:last] = out[1][:, : last - middle]
        some = pl.ds(first, last - first)
        copies.append(pltpu.make_async_copy(op_ref.at[:, some], op_out.at[:, some], op_sem.at[pair]))
        copies[-1].start()
        if pair == 2:
            nodes = dot(low_ref[...], stay, NT)
            made = dot_split(packed.table, halves(nodes))
            sums = [made[16 * side : 16 * side + 16] + out[side].T[count - 16 :] for side in range(2)]
            out_ref[0:CUT] = sums[0][0:CUT]
            out_ref[CUT:COARSE] = sums[1][0 : COARSE - CUT]
            copies.append(pltpu.make_async_copy(out_ref, rhs_out, sem.at[1]))
            copies[-1].start()
    for copy in [sol_copy] + copies:
        copy.wait()


def call(kernel, outs, args, spaces, out_spaces=None, scratch=(), flops=0, limit=VMEM_LIMIT):
    bytes_in = sum(a.size * a.dtype.itemsize for a in args)
    bytes_out = sum(o.size * o.dtype.itemsize for o in outs)
    out_spaces = out_spaces or [pltpu.VMEM] * len(outs)
    return pl.pallas_call(
        kernel,
        out_shape=tuple(outs),
        in_specs=[pl.BlockSpec(memory_space=space) for space in spaces],
        out_specs=tuple(pl.BlockSpec(memory_space=space) for space in out_spaces),
        scratch_shapes=list(scratch),
        compiler_params=pltpu.CompilerParams(vmem_limit_bytes=limit),
        cost_estimate=pl.CostEstimate(
            flops=flops, bytes_accessed=bytes_in + bytes_out, transcendentals=0
        ),
    )(*args)


def struct(shape, dtype):
    return jax.ShapeDtypeStruct(shape, dtype)


def block_table(table, copies, tall):
    out = []
    for part in split_table(table):
        full = np.zeros((copies * tall, copies * table.shape[1]), BF16)
        for copy in range(copies):
            full[
                copy * tall : copy * tall + table.shape[0],
                copy * table.shape[1] : (copy + 1) * table.shape[1],
            ] = part
        out.append(full)
    return np.concatenate(out, 0)


def per_device(start, rhs, diag_block, precond, lift, neighbour, orient, owner, slot):
    count = start.shape[1]
    staying = count // 4
    aggregates = count // 2
    owner_count = lax.axis_size("dom")
    slabs = lax.axis_size("face")
    movers = count - staying
    capacity = 2 * ((movers + owner_count - 2) // (owner_count - 1))
    capacity = ceil_to(capacity, 4)
    chunk = 6 * capacity
    entries = 6 * 128
    owner = owner.reshape(1, count)
    slot = slot.reshape(1, count)
    table = jnp.asarray(block_table(restrict_table(), GROUP, 32))
    pairs = [(i, i ^ 1) for i in range(slabs)]
    others = [(i, (i + 1 if i % 2 else i - 1) % slabs) for i in range(slabs)]

    def exchange(one, other):
        return lax.ppermute(one, "face", pairs), lax.ppermute(other, "face", others)

    args = [diag_block, precond, start, rhs, lift, neighbour, orient, owner, slot, table]
    outs = [struct((96, count), BF16), struct((96, count), BF16), struct((PACKED, count), F32)]
    held = [each for each in args if each is not rhs and each is not start and each is not table]
    to_first, to_second, pack = call(
        lambda *refs: smooth_kernel(staying, owner_count, *refs),
        outs,
        args,
        [pl.ANY] * len(args),
        [pl.ANY] * len(outs),
        scratch=[pltpu.VMEM(each.shape, each.dtype) for each in held + outs]
        + [
            pltpu.SemaphoreType.DMA((7,)),
            pltpu.SemaphoreType.DMA(()),
            pltpu.SemaphoreType.DMA((len(RIM_ROWS),)),
            pltpu.SemaphoreType.DMA((3,)),
        ],
        flops=100_000_000,
        limit=FIRST_LIMIT,
    )
    first, second = exchange(to_first, to_second)
    made, local_op, hits, partial, answer = call(
        lambda *refs: galerkin_kernel(staying, capacity, *refs),
        [
            struct((owner_count, chunk, 128), BF16),
            struct((entries, count), BF16),
            struct((2 * capacity * owner_count, 2 * count), BF16),
            struct((NODES, count), F32),
            struct((NODES, 16, count), F32),
        ],
        [diag_block, precond, pack, table],
        [pltpu.VMEM] * 4,
        scratch=[pltpu.VMEM((entries, count), F32)],
        flops=1_000_000_000,
    )
    sol, rim = call(
        middle_kernel,
        [struct((NODES, count), F32), struct((16, count), F32)],
        [first, second, diag_block, precond, pack, partial, answer],
        [pltpu.VMEM] * 7,
        scratch=[pltpu.VMEM((NODES, count), F32)],
        flops=200_000_000,
    )
    first, second = exchange(rim, rim)
    rest, kept = call(
        lambda *refs: rest_kernel(staying, *refs),
        [struct((NODES, count), F32), struct((aggregates, entries), F32)],
        [diag_block, pack, sol, local_op],
        [pltpu.VMEM] * 4,
        flops=1_000_000_000,
    )
    low, send = call(
        send_kernel,
        [struct((NODES, count), BF16), struct((owner_count, chunk, 128), BF16)],
        [first, second, rest, pack, made, hits],
        [pltpu.VMEM] * 6,
        flops=50_000_000,
    )
    got = lax.all_to_all(send, "dom", split_axis=0, concat_axis=0, tiled=True)
    outs = [
        struct((NODES, count), F32),
        struct((aggregates, COARSE * COARSE), F32),
        struct((COARSE, aggregates), F32),
    ]
    sol, coarse_op, coarse_rhs = call(
        lambda *refs: last_kernel(staying, *refs),
        outs,
        [got, kept, low, pack, sol],
        [pltpu.VMEM] * 5,
        [pl.ANY] * 3,
        scratch=[pltpu.VMEM(each.shape, each.dtype) for each in outs[1:]]
        + [pltpu.SemaphoreType.DMA((2,)), pltpu.SemaphoreType.DMA((3,))],
        flops=100_000_000,
    )
    return (sol, coarse_op.T, coarse_rhs)


def solution(mesh):
    return jax.shard_map(
        per_device,
        mesh=mesh,
        in_specs=(
            P(None, ("dom", "face")),
            P(None, ("dom", "face")),
            P(None, None, ("dom", "face")),
            P(None, None, ("dom", "face")),
            P(),
            P(None, ("dom", "face")),
            P(None, ("dom", "face")),
            P(("dom", "face")),
            P(("dom", "face")),
        ),
        out_specs=(P(None, ("dom", "face")), P(None, ("dom", "face")), P(None, ("dom", "face"))),
        check_vma=False,
    )
```

```python
import jax
import jax.numpy as jnp
import numpy as np
from jax import lax
from jax.experimental import pallas as pl
from jax.experimental.pallas import tpu as pltpu
from jax.sharding import PartitionSpec as P

SWEEPS = 2
NODES = 64
COARSE = 27
FACES = 6
GROUP = 4
SPLIT = 23
CUT = 15
RIM_ROWS = ((0, 64),)
F32 = jnp.float32
BF16 = jnp.bfloat16
VMEM_LIMIT = 24 * 1024 * 1024
FIRST_LIMIT = None

NN = (((1,), (0,)), ((), ()))
NT = (((1,), (1,)), ((), ()))
TN = (((0,), (0,)), ((), ()))


def restrict_line():
    fine = np.array([-1.0, -1.0 / np.sqrt(5.0), 1.0 / np.sqrt(5.0), 1.0])
    coarse = np.array([-1.0, 0.0, 1.0])
    basis = np.ones((4, 3))
    for column in range(3):
        for other in range(3):
            if other != column:
                basis[:, column] *= (fine - coarse[other]) / (coarse[column] - coarse[other])
    return basis.T


def restrict_table():
    line = restrict_line()
    return np.kron(np.kron(line, line), line)


def split_table(table):
    table = table.astype(np.float32)
    high = table.astype(BF16)
    low = (table - high.astype(np.float32)).astype(BF16)
    return high, low


def ceil_to(value, step):
    return -(-value // step) * step


def halves(values):
    high = values.astype(BF16)
    low = (values - high.astype(F32)).astype(BF16)
    return high, low


def dot(left, right, dims):
    return lax.dot_general(left, right, dims, preferred_element_type=F32)


def dot_split(left, right):
    left_high, left_low = halves(left)
    right_high, right_low = right
    size = left.shape[0]
    both = dot(jnp.concatenate([left_high, left_low], 0), right_high, NN)
    return both[:size] + both[size:] + dot(left_high, right_low, NN)


def small_table():
    shape = (32, NODES)
    line = restrict_line()
    row, col = rows(shape), lanes(shape)
    step = 9
    table = jnp.ones(shape, F32)
    place = jnp.where(row > CUT, row - 1, row)
    left = place
    for digit in range(3):
        mine = (left >= step).astype(jnp.int32) + (left >= 2 * step).astype(jnp.int32)
        left = left - step * mine
        fine = (col >> (4 - 2 * digit)) & 3
        value = jnp.zeros(shape, F32)
        for i in range(3):
            for j in range(4):
                value = jnp.where((mine == i) & (fine == j), float(line[i, j]), value)
        table = table * value
        step //= 3
    return jnp.where((row != CUT) & (place < COARSE), table, 0.0)


def lanes(shape):
    return lax.broadcasted_iota(jnp.int32, shape, 1)


def rows(shape):
    return lax.broadcasted_iota(jnp.int32, shape, 0)


def face_traces(ref):
    return [
        ref[0:16],
        ref[48:64],
        jnp.concatenate([ref[16 * i : 16 * i + 4] for i in range(4)], 0),
        jnp.concatenate([ref[16 * i + 12 : 16 * i + 16] for i in range(4)], 0),
        ref[pl.ds(0, 16, stride=4)],
        ref[pl.ds(3, 16, stride=4)],
    ]


def take(values, index, axis):
    return jnp.take_along_axis(values, index, axis=axis, mode="promise_in_bounds")


def turn(values, orient_row):
    shape = values.shape
    orient = jnp.broadcast_to(orient_row, shape)
    place = rows(shape)
    first = (place >> 2) ^ ((orient & 1) * 3)
    second = (place & 3) ^ (((orient >> 1) & 1) * 3)
    flip = (orient & 4) > 0
    source = jnp.where(flip, 4 * second + first, 4 * first + second)
    out = []
    for half in (source[:8], source[8:]):
        within = half & 7
        out.append(jnp.where(half >= 8, take(values[8:], within, 0), take(values[:8], within, 0)))
    return jnp.concatenate(out, 0)


def pick(traces, neighbour_ref, face):
    values = traces[face ^ 1]
    count = values.shape[1]
    index = jnp.clip(neighbour_ref[face : face + 1] - (face ^ 1) * count, 0, count - 1)
    return take(values, jnp.broadcast_to(index, values.shape), 1)


def fold(parts):
    place = rows(parts[0].shape)
    step = 1
    while len(parts) > 1:
        even = (place & step) == 0
        parts = [
            jnp.where(even, x, y) + pltpu.roll(jnp.where(even, y, x), step, 0)
            for x, y in zip(parts[::2], parts[1::2])
        ]
        step *= 2
    return parts[0]


def block_row(ref, node, tiles):
    return jnp.sum(ref[node].astype(F32).reshape(tiles.shape) * tiles, axis=0)


def apply_blocks(ref, values):
    tiles = values.reshape(NODES // 8, 8, values.shape[1])
    out = []
    for group in range(NODES // 8):
        out.append(fold([block_row(ref, node, tiles) for node in range(8 * group, 8 * group + 8)]))
    return jnp.concatenate(out, 0)


def rim_change(ref, resid):
    count = resid.shape[1]
    tiles = resid.reshape(NODES // 8, 8, count)
    steps = []
    for i in range(4):
        nodes = [16 * i + k for k in range(4)] + [16 * i + 12 + k for k in range(4)]
        steps.append(fold([block_row(ref, node, tiles) for node in nodes]))
    return both_halves(
        (16, count),
        jnp.concatenate([step[0:4] for step in steps], 0),
        jnp.concatenate([step[4:8] for step in steps], 0),
    )


def pack_rim(traces):
    shape = traces[2].shape
    return jnp.where(lanes(shape) < shape[1] // 2, traces[2], traces[3])


def coupling(traces, below, above, neighbour_ref, orient_ref, lift):
    count = below.shape[1]
    edge = count // 4
    turned = []
    for face in range(FACES):
        values = pick(traces, neighbour_ref, face)
        if face == 2:
            values = jnp.where(lanes(values.shape) < edge, below, values)
        if face == 3:
            values = jnp.where(lanes(values.shape) >= count - edge, above, values)
        turned.append(turn(values, orient_ref[face : face + 1]))
    turned = jnp.concatenate(turned + [jnp.zeros((count - FACES * 16, count), F32)], 0)
    return dot_split(lift, halves(turned))


def both_halves(shape, low, high):
    return jnp.where(lanes(shape) < shape[1] // 2, low, high)


def response(precond_ref, edge):
    count = precond_ref.shape[2]
    parts = []
    for lift in (edge[0:16], edge[16:32]):
        parts.extend(halves(lift))
    stack = jnp.concatenate(parts, 0)
    shape = (NODES, count)
    out = []
    for spot in range(16):
        node = 16 * (spot // 4) + spot % 4
        block = both_halves(shape, precond_ref[node].astype(F32), precond_ref[node + 12].astype(F32))
        made = dot(stack, block.astype(BF16), NN)
        out.append(
            both_halves((16, count), made[0:16] + made[16:32], made[32:48] + made[48:64])
        )
    return out


def halo_lift(below, above, orient_ref, lift):
    shape = below.shape
    edge = shape[1] // 4
    low = jnp.where(lanes(shape) < edge, turn(below, orient_ref[2:3]), 0.0)
    high = jnp.where(lanes(shape) >= shape[1] - edge, turn(above, orient_ref[3:4]), 0.0)
    none = jnp.zeros((32, shape[1]), F32)
    rest = jnp.zeros((shape[1] - 64, shape[1]), F32)
    return dot_split(lift, halves(jnp.concatenate([none, low, high, rest], 0)))


RHS = 0
START = NODES
RESID = 2 * NODES
LIFT = 3 * NODES
EDGE = LIFT + NODES
TABLE = EDGE + 32
NEIGHBOUR = TABLE + 32
ORIENT = NEIGHBOUR + 8
OWNER = ORIENT + 8
RANK = OWNER + 1
SLOT = OWNER + 2
PACKED = ORIENT + 16


class Packed:
    def __init__(self, ref):
        self.rhs = ref.at[RHS : RHS + NODES]
        self.start = ref.at[START : START + NODES]
        self.resid = ref.at[RESID : RESID + NODES]
        self.lift = ref[LIFT : LIFT + NODES]
        self.table = ref[TABLE : TABLE + 32, 0:NODES]
        self.edge = ref[EDGE : EDGE + 32, 0:NODES]
        self.neighbour = ref[NEIGHBOUR : NEIGHBOUR + FACES].astype(jnp.int32)
        self.orient = ref[ORIENT : ORIENT + FACES].astype(jnp.int32)
        self.owner = ref[OWNER : OWNER + 1].astype(jnp.int32)
        self.rank = ref[RANK : RANK + 1].astype(jnp.int32)
        self.slot = ref[SLOT : SLOT + 1].astype(jnp.int32)

    def target(self, staying, capacity):
        return jnp.where(lanes(self.owner.shape) >= staying, self.owner * capacity + self.rank, -1)


def smooth_kernel(
    staying, owner_count,
    diag_in, precond_in, start_in, rhs_in, lift_in, neighbour_in, orient_in, owner_in, slot_in, table_in,
    first_out, second_out, pack_out,
    diag_ref, precond_ref, lift_ref, neighbour_ref, orient_ref, owner_ref, slot_ref,
    first_ref, second_ref, pack_ref, sem, diag_sem, precond_sem, out_sem,
):
    count = diag_ref.shape[2]
    start_ref = pack_ref.at[START : START + NODES]
    pairs = [
        (start_in, start_ref), (neighbour_in, neighbour_ref), (orient_in, orient_ref), (lift_in, lift_ref),
        (rhs_in, pack_ref.at[RHS : RHS + NODES]), (owner_in, owner_ref), (slot_in, slot_ref),
    ]
    copies = [pltpu.make_async_copy(src, dst, sem.at[i]) for i, (src, dst) in enumerate(pairs)]
    diag_copy = pltpu.make_async_copy(diag_in, diag_ref, diag_sem)
    precond_copies = []
    for part, (begin, end) in enumerate(RIM_ROWS):
        at = pl.ds(begin, end - begin)
        precond_copies.append(
            pltpu.make_async_copy(precond_in.at[at], precond_ref.at[at], precond_sem.at[part])
        )
    for copy in copies + [diag_copy] + precond_copies:
        copy.start()
    for copy in copies:
        copy.wait()
    stacked = lift_ref[...].reshape(FACES * 16, NODES)
    lift = jnp.concatenate([stacked, jnp.zeros((count - FACES * 16, NODES), F32)], 0).T
    pack_ref[LIFT : LIFT + NODES] = lift
    pack_ref[EDGE : EDGE + 32, 0:NODES] = stacked[32:64]
    pack_ref[TABLE : TABLE + 32, 0:NODES] = small_table()
    pack_ref[NEIGHBOUR : NEIGHBOUR + FACES] = neighbour_ref[...].astype(F32)
    pack_ref[ORIENT : ORIENT + FACES] = orient_ref[...].astype(F32)
    owner = owner_ref[...]
    rank = rank_row(owner, staying, owner_count)
    pack_ref[OWNER : OWNER + 1] = owner.astype(F32)
    pack_ref[RANK : RANK + 1] = rank.astype(F32)
    pack_ref[SLOT : SLOT + 1] = slot_ref[...].astype(F32)
    traces = face_traces(start_ref)
    shape = traces[2].shape
    none = jnp.zeros(shape, F32)
    coupled = coupling(traces, none, none, neighbour_ref[...], orient_ref[...], lift)
    orient = both_halves((1, count), orient_ref[2:3], orient_ref[3:4])
    even = lax.rem(lax.axis_index("face"), 2) == 0

    def write(at, values):
        low, high = fold_lanes(values)
        first_ref[at : at + 16] = jnp.where(even, high, low).astype(BF16)
        second_ref[at : at + 16] = jnp.where(even, low, high).astype(BF16)

    write(16, [jnp.broadcast_to(orient.astype(F32), shape)] * GROUP)
    diag_copy.wait()
    resid = pack_ref[RHS : RHS + NODES] - (apply_blocks(diag_ref, start_ref[...]) - coupled)
    pack_ref[RESID : RESID + NODES] = resid
    pack_copy = pltpu.make_async_copy(pack_ref, pack_out, out_sem.at[0])
    pack_copy.start()
    for copy in precond_copies:
        copy.wait()
    reply = response(precond_ref, stacked[32:64])
    for q in range(4):
        write(32 + 16 * q, reply[GROUP * q : GROUP * q + GROUP])
    change = rim_change(precond_ref, resid)
    parts = []
    for values in (pack_rim(traces), pack_rim(traces) + change):
        high, low = halves(values)
        parts.extend([high.astype(F32), low.astype(F32)])
    write(0, parts)
    message_copies = [
        pltpu.make_async_copy(first_ref, first_out, out_sem.at[1]),
        pltpu.make_async_copy(second_ref, second_out, out_sem.at[2]),
    ]
    for copy in message_copies:
        copy.start()
    for copy in [pack_copy] + message_copies:
        copy.wait()


def sides(first, second):
    pos, slabs = lax.axis_index("face"), lax.axis_size("face")
    even = lax.rem(pos, 2) == 0
    above = jnp.where(even, first, second)
    below = jnp.where(even, second, first)
    return jnp.where(pos < slabs - 1, above, 0.0), jnp.where(pos > 0, below, 0.0)


def fold_lanes(values):
    shape = values[0].shape
    edge = shape[1] // GROUP
    rolled = [values[0]] + [pltpu.roll(values[g], g * edge, 1) for g in range(1, GROUP)]
    group = lanes(shape) // edge
    low, high = rolled[0], rolled[1]
    for g in range(1, GROUP):
        low = jnp.where(group == g, rolled[g], low)
        high = jnp.where(group == g, rolled[(g + 1) % GROUP], high)
    return low, high


def unfold_lanes(above, below):
    shape = above.shape
    edge = shape[1] // GROUP
    out = []
    for g in range(GROUP):
        if g:
            up = pltpu.roll(above, shape[1] - g * edge, 1)
            down = pltpu.roll(below, shape[1] - g * edge, 1)
        else:
            up, down = above, below
        out.append(both_halves(shape, up, down))
    return out


def aside(values):
    count = values.shape[1]
    return pltpu.roll(values, count // 4, 1), pltpu.roll(values, count - count // 4, 1)


def middle_kernel(
    first_ref, second_ref, diag_ref, precond_ref, pack_ref, partial_ref, answer_ref,
    sol_ref, resid_ref, rim_ref,
):
    count = diag_ref.shape[2]
    shape = (16, count)
    packed = Packed(pack_ref)
    rhs_ref = packed.rhs
    lift, neighbour_ref, orient_ref = packed.lift, packed.neighbour, packed.orient
    above, below = sides(first_ref[...].astype(F32), second_ref[...].astype(F32))
    head_high, head_low, later_high, later_low = unfold_lanes(above[0:16], below[0:16])
    head, later = head_high + head_low, later_high + later_low
    orient = both_halves((16, count), above[16:32], below[16:32])[0:1].astype(jnp.int32)
    from_high, from_low = aside(pack_rim(face_traces(packed.start)))
    sent = turn(both_halves(shape, from_high, from_low), orient)
    reply = []
    for q in range(4):
        at = slice(32 + 16 * q, 48 + 16 * q)
        reply.extend(unfold_lanes(above[at], below[at]))
    below, above = aside(head)
    edge = count // 4
    low = jnp.where(lanes(shape) < edge, turn(below, orient_ref[2:3]), 0.0)
    high = jnp.where(lanes(shape) >= count - edge, turn(above, orient_ref[3:4]), 0.0)
    arrived = low + high
    for group in range(NODES // 8):
        parts = [answer_ref[node] * arrived for node in range(8 * group, 8 * group + 8)]
        at = slice(8 * group, 8 * group + 8)
        sol_ref[at] = partial_ref[at] + fold([part[:8] + part[8:] for part in parts])
    change = [block * sent for block in reply]
    change = [block[:8] + block[8:] for block in change]
    change = jnp.concatenate([fold(change[:8]), fold(change[8:])], 0)
    below, above = aside(later + change)
    traces = face_traces(sol_ref)
    coupled = coupling(traces, below, above, neighbour_ref, orient_ref, lift)
    resid = rhs_ref[...] - (apply_blocks(diag_ref, sol_ref[...]) - coupled)
    rim_ref[...] = pack_rim(traces) + rim_change(precond_ref, resid)
    resid_ref[...] = resid


def stay_hits(packed, staying, aggregates):
    shape = (aggregates, packed.slot.shape[1])
    return one_hot((rows(shape) == packed.slot) & (lanes(shape) < staying))


def rest_kernel(
    staying, diag_ref, precond_ref, pack_ref, before_ref, resid_ref, local_ref,
    sol_ref, rest_ref, kept_ref,
):
    packed = Packed(pack_ref)
    sol_ref[...] = before_ref[...] + apply_blocks(precond_ref, resid_ref[...])
    kept_ref[...] = dot(stay_hits(packed, staying, kept_ref.shape[0]), local_ref[...], NT)
    traces = face_traces(sol_ref)
    none = jnp.zeros(traces[2].shape, F32)
    coupled = coupling(traces, none, none, packed.neighbour, packed.orient, packed.lift)
    rest_ref[...] = packed.rhs[...] - (apply_blocks(diag_ref, sol_ref[...]) - coupled)


def send_kernel(first_ref, second_ref, rest_ref, pack_ref, made_ref, hits_ref, low_ref, send_ref):
    packed = Packed(pack_ref)
    owners, size, count = made_ref.shape
    both = size // 3
    above, below = sides(first_ref[...], second_ref[...])
    below, above = aside(below)[0], aside(above)[1]
    low = (rest_ref[...] + halo_lift(below, above, packed.orient, packed.lift)).astype(BF16)
    low_ref[...] = low
    table_high, table_low = halves(packed.table)
    made = dot(jnp.concatenate([table_high, table_low], 0), low, NN)
    made = (made[:32] + made[32:]).astype(BF16)
    none = jnp.zeros((count - 16, count), BF16)
    wide = jnp.concatenate(
        [jnp.concatenate([none, made[:16]], 0), jnp.concatenate([none, made[16:]], 0)], 1
    )
    extra = dot(hits_ref[...], wide, NT).reshape(owners, both, count)
    send_ref[:, 0 : 2 * both] = made_ref[:, 0 : 2 * both]
    send_ref[:, 2 * both :] = (made_ref[:, 2 * both :].astype(F32) + extra).astype(BF16)


def rank_row(owner_row, staying, owner_count):
    count = owner_row.shape[1]
    shape = (owner_count, count)
    hits = (rows(shape) == owner_row) & (lanes(shape) >= staying)
    hits = jnp.where(hits, 1.0, 0.0)
    before = jnp.where(rows((count, count)) < lanes((count, count)), 1.0, 0.0)
    earlier = dot(hits.astype(BF16), before.astype(BF16), NN)
    return jnp.sum(hits * earlier, axis=0, keepdims=True).astype(jnp.int32)


def one_hot(condition):
    return jnp.where(condition, 1.0, 0.0).astype(BF16)


def contract(four, line):
    first, second = float(line[0, 1]), float(line[0, 2])
    middle = float(line[1, 1])
    return [
        four[0] + first * four[1] + second * four[2],
        middle * (four[1] + four[2]),
        four[3] + second * four[1] + first * four[2],
    ]


def galerkin_kernel(
    staying, capacity, diag_ref, precond_ref, pack_ref, table_ref,
    send_ref, local_ref, hits_ref, partial_ref, answer_ref, full_ref,
):
    line = restrict_line()
    count = diag_ref.shape[2]
    owner_count = send_ref.shape[0]
    packed = Packed(pack_ref)
    partial_ref[...] = packed.start[...] + apply_blocks(precond_ref, packed.resid[...])
    edge = packed.edge
    stack = jnp.concatenate([part for lift in (edge[0:16], edge[16:32]) for part in halves(lift)], 0)
    none = jnp.zeros(stack.shape, BF16)
    stack = jnp.concatenate(
        [jnp.concatenate([stack if i == j else none for j in range(GROUP)], 1) for i in range(GROUP)], 0
    )
    for first in range(0, NODES, 2 * GROUP):
        wide = [
            precond_ref[first + GROUP * j : first + GROUP * j + GROUP].reshape(GROUP * NODES, count)
            for j in range(2)
        ]
        made = dot(stack, jnp.concatenate(wide, 1), NN)
        for j in range(2):
            for k in range(GROUP):
                block = made[64 * k : 64 * k + 64, count * j : count * j + count]
                answer_ref[first + GROUP * j + k] = both_halves(
                    (16, count), block[0:16] + block[16:32], block[32:48] + block[48:64]
                )
    target = packed.target(staying, capacity)
    twice = jnp.concatenate([target, target], 1)
    shape = (2 * capacity, 2 * count)
    upper = (rows(shape) >= capacity).astype(jnp.int32)
    place = rows(shape) - capacity * upper
    place = jnp.where(upper == (lanes(shape) >= count).astype(jnp.int32), place, -2 * owner_count * capacity)
    hits = jnp.concatenate([one_hot(place + capacity * o == twice) for o in range(owner_count)], 0)
    hits_ref[...] = hits
    table = table_ref[...]
    padded = table.shape[0] // 2
    tall = padded // GROUP
    planes = []
    for i in range(4):
        bars = []
        for half in range(2):
            first = 2 * GROUP * (2 * i + half)
            wide = [
                diag_ref[first + GROUP * j : first + GROUP * j + GROUP].reshape(GROUP * NODES, count)
                for j in range(2)
            ]
            both = dot(table, jnp.concatenate(wide, 1), NN)
            made = both[:padded] + both[padded:]
            for j in range(2):
                four = [made[tall * k : tall * k + tall, count * j : count * j + count] for k in range(4)]
                bars.append(contract(four, line))
        sheet = [contract([bars[j][k] for j in range(4)], line) for k in range(3)]
        planes.append([sheet[k][j] for j in range(3) for k in range(3)])
    made = [contract([planes[i][rest] for i in range(4)], line) for rest in range(9)]
    full_ref[5 * 128 - 16 : 5 * 128] = jnp.zeros((16, count), F32)
    for c in range(COARSE):
        at = COARSE * c if c < SPLIT else 5 * 128 + COARSE * (c - SPLIT)
        full_ref[at : at + tall] = made[c % 9][c // 9]
    full_ref[5 * 128 + COARSE * (COARSE - SPLIT) :] = jnp.zeros((128 - COARSE * (COARSE - SPLIT), count), F32)
    slot = (packed.slot + 1).astype(F32)
    full_ref[5 * 128 - 1 : 5 * 128] = slot
    full_ref[6 * 128 - 1 : 6 * 128] = slot
    local = full_ref[...].astype(BF16)
    local_ref[...] = local
    for pair in range(3):
        wide = jnp.concatenate([local[256 * pair : 256 * pair + 128], local[256 * pair + 128 : 256 * pair + 256]], 1)
        made = dot(hits, wide, NT).reshape(owner_count, 2 * capacity, 128).astype(BF16)
        send_ref[:, 2 * capacity * pair : 2 * capacity * pair + 2 * capacity] = made


def last_kernel(
    staying, got_ref, kept_ref, low_ref, pack_ref, sol_ref,
    sol_out, op_out, rhs_out,
    op_ref, out_ref, sem, op_sem,
):
    sol_copy = pltpu.make_async_copy(sol_ref, sol_out, sem.at[0])
    sol_copy.start()
    packed = Packed(pack_ref)
    aggregates = op_ref.shape[0]
    owners, size, count = got_ref.shape
    both = size // 3
    capacity = both // 2
    stay = stay_hits(packed, staying, aggregates)
    ids = got_ref[:, 2 * both : size].astype(F32).reshape(owners * both, count)[:, count - 1 : count]
    shape = (owners * both, 2 * aggregates)
    column = lanes(shape)
    column = jnp.where(column >= aggregates, column - aggregates, column)
    hits = jnp.where(ids == (column + 1).astype(F32), 1.0, 0.0).reshape(owners, both, 2 * aggregates)
    shape = (owners, both, 2 * aggregates)
    upper = lax.broadcasted_iota(jnp.int32, shape, 1) >= capacity
    right = lax.broadcasted_iota(jnp.int32, shape, 2) >= aggregates
    paired = jnp.where(upper == right, hits, 0.0).reshape(owners * both, 2 * aggregates).astype(BF16)
    cut = SPLIT * COARSE
    copies = []
    for pair in (2, 0, 1):
        block = got_ref[:, both * pair : both * pair + both].astype(F32).reshape(owners * both, count).astype(BF16)
        total = dot(paired, block, TN)
        out = []
        for side in range(2):
            at = 128 * (2 * pair + side)
            out.append(total[aggregates * side : aggregates * side + aggregates] + kept_ref[:, at : at + 128])
        first, last = 256 * pair, min(256 * pair + 256, COARSE * COARSE)
        middle = cut if pair == 2 else first + 128
        op_ref[:, first:middle] = out[0][:, : middle - first]
        op_ref[:, middle:last] = out[1][:, : last - middle]
        some = pl.ds(first, last - first)
        copies.append(pltpu.make_async_copy(op_ref.at[:, some], op_out.at[:, some], op_sem.at[pair]))
        copies[-1].start()
        if pair == 2:
            nodes = dot(low_ref[...], stay, NT)
            made = dot_split(packed.table, halves(nodes))
            sums = [made[16 * side : 16 * side + 16] + out[side].T[count - 16 :] for side in range(2)]
            out_ref[0:CUT] = sums[0][0:CUT]
            out_ref[CUT:COARSE] = sums[1][0 : COARSE - CUT]
            copies.append(pltpu.make_async_copy(out_ref, rhs_out, sem.at[1]))
            copies[-1].start()
    for copy in [sol_copy] + copies:
        copy.wait()


def call(kernel, outs, args, spaces, out_spaces=None, scratch=(), flops=0, limit=VMEM_LIMIT):
    bytes_in = sum(a.size * a.dtype.itemsize for a in args)
    bytes_out = sum(o.size * o.dtype.itemsize for o in outs)
    out_spaces = out_spaces or [pltpu.VMEM] * len(outs)
    return pl.pallas_call(
        kernel,
        out_shape=tuple(outs),
        in_specs=[pl.BlockSpec(memory_space=space) for space in spaces],
        out_specs=tuple(pl.BlockSpec(memory_space=space) for space in out_spaces),
        scratch_shapes=list(scratch),
        compiler_params=pltpu.CompilerParams(vmem_limit_bytes=limit),
        cost_estimate=pl.CostEstimate(
            flops=flops, bytes_accessed=bytes_in + bytes_out, transcendentals=0
        ),
    )(*args)


def struct(shape, dtype):
    return jax.ShapeDtypeStruct(shape, dtype)


def block_table(table, copies, tall):
    out = []
    for part in split_table(table):
        full = np.zeros((copies * tall, copies * table.shape[1]), BF16)
        for copy in range(copies):
            full[
                copy * tall : copy * tall + table.shape[0],
                copy * table.shape[1] : (copy + 1) * table.shape[1],
            ] = part
        out.append(full)
    return np.concatenate(out, 0)


def per_device(start, rhs, diag_block, precond, lift, neighbour, orient, owner, slot):
    count = start.shape[1]
    staying = count // 4
    aggregates = count // 2
    owner_count = lax.axis_size("dom")
    slabs = lax.axis_size("face")
    movers = count - staying
    capacity = 2 * ((movers + owner_count - 2) // (owner_count - 1))
    capacity = ceil_to(capacity, 4)
    chunk = 6 * capacity
    entries = 6 * 128
    owner = owner.reshape(1, count)
    slot = slot.reshape(1, count)
    table = jnp.asarray(block_table(restrict_table(), GROUP, 32))
    pairs = [(i, i ^ 1) for i in range(slabs)]
    others = [(i, (i + 1 if i % 2 else i - 1) % slabs) for i in range(slabs)]

    def exchange(one, other):
        return lax.ppermute(one, "face", pairs), lax.ppermute(other, "face", others)

    args = [diag_block, precond, start, rhs, lift, neighbour, orient, owner, slot, table]
    outs = [struct((96, count), BF16), struct((96, count), BF16), struct((PACKED, count), F32)]
    held = [each for each in args if each is not rhs and each is not start and each is not table]
    to_first, to_second, pack = call(
        lambda *refs: smooth_kernel(staying, owner_count, *refs),
        outs,
        args,
        [pl.ANY] * len(args),
        [pl.ANY] * len(outs),
        scratch=[pltpu.VMEM(each.shape, each.dtype) for each in held + outs]
        + [
            pltpu.SemaphoreType.DMA((7,)),
            pltpu.SemaphoreType.DMA(()),
            pltpu.SemaphoreType.DMA((len(RIM_ROWS),)),
            pltpu.SemaphoreType.DMA((3,)),
        ],
        flops=100_000_000,
        limit=FIRST_LIMIT,
    )
    first, second = exchange(to_first, to_second)
    made, local_op, hits, partial, answer = call(
        lambda *refs: galerkin_kernel(staying, capacity, *refs),
        [
            struct((owner_count, chunk, 128), BF16),
            struct((entries, count), BF16),
            struct((2 * capacity * owner_count, 2 * count), BF16),
            struct((NODES, count), F32),
            struct((NODES, 16, count), F32),
        ],
        [diag_block, precond, pack, table],
        [pltpu.VMEM] * 4,
        scratch=[pltpu.VMEM((entries, count), F32)],
        flops=1_000_000_000,
    )
    sol, resid, rim = call(
        middle_kernel,
        [struct((NODES, count), F32), struct((NODES, count), F32), struct((16, count), F32)],
        [first, second, diag_block, precond, pack, partial, answer],
        [pltpu.VMEM] * 7,
        flops=200_000_000,
    )
    first, second = exchange(rim, rim)
    sol, rest, kept = call(
        lambda *refs: rest_kernel(staying, *refs),
        [struct((NODES, count), F32), struct((NODES, count), F32), struct((aggregates, entries), F32)],
        [diag_block, precond, pack, sol, resid, local_op],
        [pltpu.VMEM] * 6,
        flops=1_000_000_000,
    )
    low, send = call(
        send_kernel,
        [struct((NODES, count), BF16), struct((owner_count, chunk, 128), BF16)],
        [first, second, rest, pack, made, hits],
        [pltpu.VMEM] * 6,
        flops=50_000_000,
    )
    got = lax.all_to_all(send, "dom", split_axis=0, concat_axis=0, tiled=True)
    outs = [
        struct((NODES, count), F32),
        struct((aggregates, COARSE * COARSE), F32),
        struct((COARSE, aggregates), F32),
    ]
    sol, coarse_op, coarse_rhs = call(
        lambda *refs: last_kernel(staying, *refs),
        outs,
        [got, kept, low, pack, sol],
        [pltpu.VMEM] * 5,
        [pl.ANY] * 3,
        scratch=[pltpu.VMEM(each.shape, each.dtype) for each in outs[1:]]
        + [pltpu.SemaphoreType.DMA((2,)), pltpu.SemaphoreType.DMA((3,))],
        flops=100_000_000,
    )
    return (sol, coarse_op.T, coarse_rhs)


def solution(mesh):
    return jax.shard_map(
        per_device,
        mesh=mesh,
        in_specs=(
            P(None, ("dom", "face")),
            P(None, ("dom", "face")),
            P(None, None, ("dom", "face")),
            P(None, None, ("dom", "face")),
            P(),
            P(None, ("dom", "face")),
            P(None, ("dom", "face")),
            P(("dom", "face")),
            P(("dom", "face")),
        ),
        out_specs=(P(None, ("dom", "face")), P(None, ("dom", "face")), P(None, ("dom", "face"))),
        check_vma=False,
    )
```

```python
import jax
import jax.numpy as jnp
import numpy as np
from jax import lax
from jax.experimental import pallas as pl
from jax.experimental.pallas import tpu as pltpu
from jax.sharding import PartitionSpec as P

SWEEPS = 2
NODES = 64
COARSE = 27
FACES = 6
GROUP = 4
SPLIT = 23
CUT = 15
RIM_ROWS = ((0, 64),)
F32 = jnp.float32
BF16 = jnp.bfloat16
VMEM_LIMIT = 24 * 1024 * 1024
FIRST_LIMIT = None

NN = (((1,), (0,)), ((), ()))
NT = (((1,), (1,)), ((), ()))
TN = (((0,), (0,)), ((), ()))


def restrict_line():
    fine = np.array([-1.0, -1.0 / np.sqrt(5.0), 1.0 / np.sqrt(5.0), 1.0])
    coarse = np.array([-1.0, 0.0, 1.0])
    basis = np.ones((4, 3))
    for column in range(3):
        for other in range(3):
            if other != column:
                basis[:, column] *= (fine - coarse[other]) / (coarse[column] - coarse[other])
    return basis.T


def restrict_table():
    line = restrict_line()
    return np.kron(np.kron(line, line), line)


def split_table(table):
    table = table.astype(np.float32)
    high = table.astype(BF16)
    low = (table - high.astype(np.float32)).astype(BF16)
    return high, low


def ceil_to(value, step):
    return -(-value // step) * step


def halves(values):
    high = values.astype(BF16)
    low = (values - high.astype(F32)).astype(BF16)
    return high, low


def dot(left, right, dims):
    return lax.dot_general(left, right, dims, preferred_element_type=F32)


def dot_split(left, right):
    left_high, left_low = halves(left)
    right_high, right_low = right
    size = left.shape[0]
    both = dot(jnp.concatenate([left_high, left_low], 0), right_high, NN)
    return both[:size] + both[size:] + dot(left_high, right_low, NN)


def small_table():
    shape = (32, NODES)
    line = restrict_line()
    row, col = rows(shape), lanes(shape)
    step = 9
    table = jnp.ones(shape, F32)
    place = jnp.where(row > CUT, row - 1, row)
    left = place
    for digit in range(3):
        mine = (left >= step).astype(jnp.int32) + (left >= 2 * step).astype(jnp.int32)
        left = left - step * mine
        fine = (col >> (4 - 2 * digit)) & 3
        value = jnp.zeros(shape, F32)
        for i in range(3):
            for j in range(4):
                value = jnp.where((mine == i) & (fine == j), float(line[i, j]), value)
        table = table * value
        step //= 3
    return jnp.where((row != CUT) & (place < COARSE), table, 0.0)


def lanes(shape):
    return lax.broadcasted_iota(jnp.int32, shape, 1)


def rows(shape):
    return lax.broadcasted_iota(jnp.int32, shape, 0)


def face_traces(ref):
    return [
        ref[0:16],
        ref[48:64],
        jnp.concatenate([ref[16 * i : 16 * i + 4] for i in range(4)], 0),
        jnp.concatenate([ref[16 * i + 12 : 16 * i + 16] for i in range(4)], 0),
        ref[pl.ds(0, 16, stride=4)],
        ref[pl.ds(3, 16, stride=4)],
    ]


def take(values, index, axis):
    return jnp.take_along_axis(values, index, axis=axis, mode="promise_in_bounds")


def turn(values, orient_row):
    shape = values.shape
    orient = jnp.broadcast_to(orient_row, shape)
    place = rows(shape)
    first = (place >> 2) ^ ((orient & 1) * 3)
    second = (place & 3) ^ (((orient >> 1) & 1) * 3)
    flip = (orient & 4) > 0
    source = jnp.where(flip, 4 * second + first, 4 * first + second)
    out = []
    for half in (source[:8], source[8:]):
        within = half & 7
        out.append(jnp.where(half >= 8, take(values[8:], within, 0), take(values[:8], within, 0)))
    return jnp.concatenate(out, 0)


def pick(traces, neighbour_ref, face):
    values = traces[face ^ 1]
    count = values.shape[1]
    index = jnp.clip(neighbour_ref[face : face + 1] - (face ^ 1) * count, 0, count - 1)
    return take(values, jnp.broadcast_to(index, values.shape), 1)


def fold(parts):
    place = rows(parts[0].shape)
    step = 1
    while len(parts) > 1:
        even = (place & step) == 0
        parts = [
            jnp.where(even, x, y) + pltpu.roll(jnp.where(even, y, x), step, 0)
            for x, y in zip(parts[::2], parts[1::2])
        ]
        step *= 2
    return parts[0]


def block_row(ref, node, tiles):
    return jnp.sum(ref[node].astype(F32).reshape(tiles.shape) * tiles, axis=0)


def apply_blocks(ref, values):
    tiles = values.reshape(NODES // 8, 8, values.shape[1])
    out = []
    for group in range(NODES // 8):
        out.append(fold([block_row(ref, node, tiles) for node in range(8 * group, 8 * group + 8)]))
    return jnp.concatenate(out, 0)


def rim_change(ref, resid):
    count = resid.shape[1]
    tiles = resid.reshape(NODES // 8, 8, count)
    steps = []
    for i in range(4):
        nodes = [16 * i + k for k in range(4)] + [16 * i + 12 + k for k in range(4)]
        steps.append(fold([block_row(ref, node, tiles) for node in nodes]))
    return both_halves(
        (16, count),
        jnp.concatenate([step[0:4] for step in steps], 0),
        jnp.concatenate([step[4:8] for step in steps], 0),
    )


def pack_rim(traces):
    shape = traces[2].shape
    return jnp.where(lanes(shape) < shape[1] // 2, traces[2], traces[3])


def coupling(traces, below, above, neighbour_ref, orient_ref, lift):
    count = below.shape[1]
    edge = count // 4
    turned = []
    for face in range(FACES):
        values = pick(traces, neighbour_ref, face)
        if face == 2:
            values = jnp.where(lanes(values.shape) < edge, below, values)
        if face == 3:
            values = jnp.where(lanes(values.shape) >= count - edge, above, values)
        turned.append(turn(values, orient_ref[face : face + 1]))
    turned = jnp.concatenate(turned + [jnp.zeros((count - FACES * 16, count), F32)], 0)
    return dot_split(lift, halves(turned))


def both_halves(shape, low, high):
    return jnp.where(lanes(shape) < shape[1] // 2, low, high)


def response(precond_ref, edge):
    count = precond_ref.shape[2]
    parts = []
    for lift in (edge[0:16], edge[16:32]):
        parts.extend(halves(lift))
    stack = jnp.concatenate(parts, 0)
    shape = (NODES, count)
    out = []
    for spot in range(16):
        node = 16 * (spot // 4) + spot % 4
        block = both_halves(shape, precond_ref[node].astype(F32), precond_ref[node + 12].astype(F32))
        made = dot(stack, block.astype(BF16), NN)
        out.append(
            both_halves((16, count), made[0:16] + made[16:32], made[32:48] + made[48:64])
        )
    return out


def halo_lift(below, above, orient_ref, lift):
    shape = below.shape
    edge = shape[1] // 4
    low = jnp.where(lanes(shape) < edge, turn(below, orient_ref[2:3]), 0.0)
    high = jnp.where(lanes(shape) >= shape[1] - edge, turn(above, orient_ref[3:4]), 0.0)
    none = jnp.zeros((32, shape[1]), F32)
    rest = jnp.zeros((shape[1] - 64, shape[1]), F32)
    return dot_split(lift, halves(jnp.concatenate([none, low, high, rest], 0)))


RHS = 0
START = NODES
RESID = 2 * NODES
LIFT = 3 * NODES
EDGE = LIFT + NODES
TABLE = EDGE + 32
SIDE = TABLE + 32
NEIGHBOUR = SIDE + 32
ORIENT = NEIGHBOUR + 8
OWNER = ORIENT + 8
RANK = OWNER + 1
SLOT = OWNER + 2
PACKED = ORIENT + 16


class Packed:
    def __init__(self, ref):
        self.rhs = ref.at[RHS : RHS + NODES]
        self.start = ref.at[START : START + NODES]
        self.resid = ref.at[RESID : RESID + NODES]
        self.lift = ref[LIFT : LIFT + NODES]
        self.table = ref[TABLE : TABLE + 32, 0:NODES]
        self.edge = ref[EDGE : EDGE + 32, 0:NODES]
        self.side = ref[SIDE : SIDE + 32]
        self.neighbour = ref[NEIGHBOUR : NEIGHBOUR + FACES].astype(jnp.int32)
        self.orient = ref[ORIENT : ORIENT + FACES].astype(jnp.int32)
        self.owner = ref[OWNER : OWNER + 1].astype(jnp.int32)
        self.rank = ref[RANK : RANK + 1].astype(jnp.int32)
        self.slot = ref[SLOT : SLOT + 1].astype(jnp.int32)

    def target(self, staying, capacity):
        return jnp.where(lanes(self.owner.shape) >= staying, self.owner * capacity + self.rank, -1)


def smooth_kernel(
    staying, owner_count,
    diag_in, precond_in, start_in, rhs_in, lift_in, neighbour_in, orient_in, owner_in, slot_in, table_in,
    first_out, second_out, pack_out,
    diag_ref, precond_ref, lift_ref, neighbour_ref, orient_ref, owner_ref, slot_ref,
    first_ref, second_ref, pack_ref, sem, diag_sem, precond_sem, out_sem,
):
    count = diag_ref.shape[2]
    start_ref = pack_ref.at[START : START + NODES]
    pairs = [
        (start_in, start_ref), (neighbour_in, neighbour_ref), (orient_in, orient_ref), (lift_in, lift_ref),
        (rhs_in, pack_ref.at[RHS : RHS + NODES]), (owner_in, owner_ref), (slot_in, slot_ref),
    ]
    copies = [pltpu.make_async_copy(src, dst, sem.at[i]) for i, (src, dst) in enumerate(pairs)]
    diag_copy = pltpu.make_async_copy(diag_in, diag_ref, diag_sem)
    precond_copies = []
    for part, (begin, end) in enumerate(RIM_ROWS):
        at = pl.ds(begin, end - begin)
        precond_copies.append(
            pltpu.make_async_copy(precond_in.at[at], precond_ref.at[at], precond_sem.at[part])
        )
    for copy in copies + [diag_copy] + precond_copies:
        copy.start()
    for copy in copies:
        copy.wait()
    stacked = lift_ref[...].reshape(FACES * 16, NODES)
    lift = jnp.concatenate([stacked, jnp.zeros((count - FACES * 16, NODES), F32)], 0).T
    pack_ref[LIFT : LIFT + NODES] = lift
    pack_ref[EDGE : EDGE + 32, 0:NODES] = stacked[32:64]
    table = small_table()
    pack_ref[TABLE : TABLE + 32, 0:NODES] = table
    high_side = jnp.concatenate([stacked[48:64], jnp.zeros((count - 16, NODES), F32)], 0)
    pack_ref[SIDE : SIDE + 32] = dot_split(table, halves(high_side.T))
    pack_ref[NEIGHBOUR : NEIGHBOUR + FACES] = neighbour_ref[...].astype(F32)
    pack_ref[ORIENT : ORIENT + FACES] = orient_ref[...].astype(F32)
    owner = owner_ref[...]
    rank = rank_row(owner, staying, owner_count)
    pack_ref[OWNER : OWNER + 1] = owner.astype(F32)
    pack_ref[RANK : RANK + 1] = rank.astype(F32)
    pack_ref[SLOT : SLOT + 1] = slot_ref[...].astype(F32)
    traces = face_traces(start_ref)
    shape = traces[2].shape
    none = jnp.zeros(shape, F32)
    coupled = coupling(traces, none, none, neighbour_ref[...], orient_ref[...], lift)
    orient = both_halves((1, count), orient_ref[2:3], orient_ref[3:4])
    even = lax.rem(lax.axis_index("face"), 2) == 0

    def write(at, values):
        low, high = fold_lanes(values)
        first_ref[at : at + 16] = jnp.where(even, high, low).astype(BF16)
        second_ref[at : at + 16] = jnp.where(even, low, high).astype(BF16)

    write(16, [jnp.broadcast_to(orient.astype(F32), shape)] * GROUP)
    diag_copy.wait()
    resid = pack_ref[RHS : RHS + NODES] - (apply_blocks(diag_ref, start_ref[...]) - coupled)
    pack_ref[RESID : RESID + NODES] = resid
    pack_copy = pltpu.make_async_copy(pack_ref, pack_out, out_sem.at[0])
    pack_copy.start()
    for copy in precond_copies:
        copy.wait()
    reply = response(precond_ref, stacked[32:64])
    for q in range(4):
        write(32 + 16 * q, reply[GROUP * q : GROUP * q + GROUP])
    change = rim_change(precond_ref, resid)
    parts = []
    for values in (pack_rim(traces), pack_rim(traces) + change):
        high, low = halves(values)
        parts.extend([high.astype(F32), low.astype(F32)])
    write(0, parts)
    message_copies = [
        pltpu.make_async_copy(first_ref, first_out, out_sem.at[1]),
        pltpu.make_async_copy(second_ref, second_out, out_sem.at[2]),
    ]
    for copy in message_copies:
        copy.start()
    for copy in [pack_copy] + message_copies:
        copy.wait()


def sides(first, second):
    pos, slabs = lax.axis_index("face"), lax.axis_size("face")
    even = lax.rem(pos, 2) == 0
    above = jnp.where(even, first, second)
    below = jnp.where(even, second, first)
    return jnp.where(pos < slabs - 1, above, 0.0), jnp.where(pos > 0, below, 0.0)


def fold_lanes(values):
    shape = values[0].shape
    edge = shape[1] // GROUP
    rolled = [values[0]] + [pltpu.roll(values[g], g * edge, 1) for g in range(1, GROUP)]
    group = lanes(shape) // edge
    low, high = rolled[0], rolled[1]
    for g in range(1, GROUP):
        low = jnp.where(group == g, rolled[g], low)
        high = jnp.where(group == g, rolled[(g + 1) % GROUP], high)
    return low, high


def unfold_lanes(above, below):
    shape = above.shape
    edge = shape[1] // GROUP
    out = []
    for g in range(GROUP):
        if g:
            up = pltpu.roll(above, shape[1] - g * edge, 1)
            down = pltpu.roll(below, shape[1] - g * edge, 1)
        else:
            up, down = above, below
        out.append(both_halves(shape, up, down))
    return out


def aside(values):
    count = values.shape[1]
    return pltpu.roll(values, count // 4, 1), pltpu.roll(values, count - count // 4, 1)


def middle_kernel(
    first_ref, second_ref, diag_ref, precond_ref, pack_ref, partial_ref, answer_ref,
    sol_ref, resid_ref, rim_ref,
):
    count = diag_ref.shape[2]
    shape = (16, count)
    packed = Packed(pack_ref)
    rhs_ref = packed.rhs
    lift, neighbour_ref, orient_ref = packed.lift, packed.neighbour, packed.orient
    above, below = sides(first_ref[...].astype(F32), second_ref[...].astype(F32))
    head_high, head_low, later_high, later_low = unfold_lanes(above[0:16], below[0:16])
    head, later = head_high + head_low, later_high + later_low
    orient = both_halves((16, count), above[16:32], below[16:32])[0:1].astype(jnp.int32)
    from_high, from_low = aside(pack_rim(face_traces(packed.start)))
    sent = turn(both_halves(shape, from_high, from_low), orient)
    reply = []
    for q in range(4):
        at = slice(32 + 16 * q, 48 + 16 * q)
        reply.extend(unfold_lanes(above[at], below[at]))
    below, above = aside(head)
    edge = count // 4
    low = jnp.where(lanes(shape) < edge, turn(below, orient_ref[2:3]), 0.0)
    high = jnp.where(lanes(shape) >= count - edge, turn(above, orient_ref[3:4]), 0.0)
    arrived = low + high
    for group in range(NODES // 8):
        parts = [answer_ref[node] * arrived for node in range(8 * group, 8 * group + 8)]
        at = slice(8 * group, 8 * group + 8)
        sol_ref[at] = partial_ref[at] + fold([part[:8] + part[8:] for part in parts])
    change = [block * sent for block in reply]
    change = [block[:8] + block[8:] for block in change]
    change = jnp.concatenate([fold(change[:8]), fold(change[8:])], 0)
    below, above = aside(later + change)
    traces = face_traces(sol_ref)
    coupled = coupling(traces, below, above, neighbour_ref, orient_ref, lift)
    resid = rhs_ref[...] - (apply_blocks(diag_ref, sol_ref[...]) - coupled)
    rim_ref[...] = pack_rim(traces) + rim_change(precond_ref, resid)
    resid_ref[...] = resid


def stay_hits(packed, staying, aggregates):
    shape = (aggregates, packed.slot.shape[1])
    return one_hot((rows(shape) == packed.slot) & (lanes(shape) < staying))


def rest_kernel(
    staying, diag_ref, precond_ref, pack_ref, before_ref, resid_ref, local_ref, made_ref, hits_ref,
    sol_ref, rest_ref, kept_ref, send_ref,
):
    packed = Packed(pack_ref)
    sol_ref[...] = before_ref[...] + apply_blocks(precond_ref, resid_ref[...])
    kept_ref[...] = dot(stay_hits(packed, staying, kept_ref.shape[0]), local_ref[...], NT)
    traces = face_traces(sol_ref)
    none = jnp.zeros(traces[2].shape, F32)
    coupled = coupling(traces, none, none, packed.neighbour, packed.orient, packed.lift)
    rest = packed.rhs[...] - (apply_blocks(diag_ref, sol_ref[...]) - coupled)
    rest_ref[...] = rest
    owners, size, count = made_ref.shape
    both = size // 3
    high, low = halves(rest)
    low = jnp.where(lanes(low.shape) >= count - count // 4, low.astype(F32), 0.0).astype(BF16)
    made = dot_split(packed.table, (high, low)).astype(BF16)
    extra = dot(hits_ref[...], spread(made), NT).reshape(owners, both, count)
    send_ref[:, 0 : 2 * both] = made_ref[:, 0 : 2 * both]
    send_ref[:, 2 * both :] = (made_ref[:, 2 * both :].astype(F32) + extra).astype(BF16)


def spread(made):
    none = jnp.zeros((made.shape[1] - 16, made.shape[1]), made.dtype)
    return jnp.concatenate(
        [jnp.concatenate([none, made[:16]], 0), jnp.concatenate([none, made[16:]], 0)], 1
    )


def send_kernel(first_ref, second_ref, rest_ref, pack_ref, hits_ref, made_ref, low_ref, send_ref):
    packed = Packed(pack_ref)
    owners, size, count = made_ref.shape
    both = size // 3
    edge = count // 4
    above, below = sides(first_ref[...], second_ref[...])
    below, above = aside(below)[0], aside(above)[1]
    high = jnp.where(lanes(above.shape) >= count - edge, turn(above, packed.orient[3:4]), 0.0)
    high = jnp.concatenate([high, jnp.zeros((count - 16, count), F32)], 0)
    lifted = dot_split(packed.side, halves(high)).astype(BF16)
    extra = dot(hits_ref[...], spread(lifted), NT).reshape(owners, both, count)
    send_ref[:, 2 * both :] = (made_ref[:, 2 * both :].astype(F32) + extra).astype(BF16)
    low_ref[...] = (rest_ref[...] + halo_lift(below, above, packed.orient, packed.lift)).astype(BF16)


def rank_row(owner_row, staying, owner_count):
    count = owner_row.shape[1]
    shape = (owner_count, count)
    hits = (rows(shape) == owner_row) & (lanes(shape) >= staying)
    hits = jnp.where(hits, 1.0, 0.0)
    before = jnp.where(rows((count, count)) < lanes((count, count)), 1.0, 0.0)
    earlier = dot(hits.astype(BF16), before.astype(BF16), NN)
    return jnp.sum(hits * earlier, axis=0, keepdims=True).astype(jnp.int32)


def one_hot(condition):
    return jnp.where(condition, 1.0, 0.0).astype(BF16)


def contract(four, line):
    first, second = float(line[0, 1]), float(line[0, 2])
    middle = float(line[1, 1])
    return [
        four[0] + first * four[1] + second * four[2],
        middle * (four[1] + four[2]),
        four[3] + second * four[1] + first * four[2],
    ]


def galerkin_kernel(
    staying, capacity, diag_ref, precond_ref, pack_ref, table_ref,
    send_ref, local_ref, hits_ref, partial_ref, answer_ref, full_ref,
):
    line = restrict_line()
    count = diag_ref.shape[2]
    owner_count = send_ref.shape[0]
    packed = Packed(pack_ref)
    partial_ref[...] = packed.start[...] + apply_blocks(precond_ref, packed.resid[...])
    edge = packed.edge
    stack = jnp.concatenate([part for lift in (edge[0:16], edge[16:32]) for part in halves(lift)], 0)
    none = jnp.zeros(stack.shape, BF16)
    stack = jnp.concatenate(
        [jnp.concatenate([stack if i == j else none for j in range(GROUP)], 1) for i in range(GROUP)], 0
    )
    for first in range(0, NODES, 2 * GROUP):
        wide = [
            precond_ref[first + GROUP * j : first + GROUP * j + GROUP].reshape(GROUP * NODES, count)
            for j in range(2)
        ]
        made = dot(stack, jnp.concatenate(wide, 1), NN)
        for j in range(2):
            for k in range(GROUP):
                block = made[64 * k : 64 * k + 64, count * j : count * j + count]
                answer_ref[first + GROUP * j + k] = both_halves(
                    (16, count), block[0:16] + block[16:32], block[32:48] + block[48:64]
                )
    target = packed.target(staying, capacity)
    twice = jnp.concatenate([target, target], 1)
    shape = (2 * capacity, 2 * count)
    upper = (rows(shape) >= capacity).astype(jnp.int32)
    place = rows(shape) - capacity * upper
    place = jnp.where(upper == (lanes(shape) >= count).astype(jnp.int32), place, -2 * owner_count * capacity)
    hits = jnp.concatenate([one_hot(place + capacity * o == twice) for o in range(owner_count)], 0)
    hits_ref[...] = hits
    table = table_ref[...]
    padded = table.shape[0] // 2
    tall = padded // GROUP
    planes = []
    for i in range(4):
        bars = []
        for half in range(2):
            first = 2 * GROUP * (2 * i + half)
            wide = [
                diag_ref[first + GROUP * j : first + GROUP * j + GROUP].reshape(GROUP * NODES, count)
                for j in range(2)
            ]
            both = dot(table, jnp.concatenate(wide, 1), NN)
            made = both[:padded] + both[padded:]
            for j in range(2):
                four = [made[tall * k : tall * k + tall, count * j : count * j + count] for k in range(4)]
                bars.append(contract(four, line))
        sheet = [contract([bars[j][k] for j in range(4)], line) for k in range(3)]
        planes.append([sheet[k][j] for j in range(3) for k in range(3)])
    made = [contract([planes[i][rest] for i in range(4)], line) for rest in range(9)]
    full_ref[5 * 128 - 16 : 5 * 128] = jnp.zeros((16, count), F32)
    for c in range(COARSE):
        at = COARSE * c if c < SPLIT else 5 * 128 + COARSE * (c - SPLIT)
        full_ref[at : at + tall] = made[c % 9][c // 9]
    full_ref[5 * 128 + COARSE * (COARSE - SPLIT) :] = jnp.zeros((128 - COARSE * (COARSE - SPLIT), count), F32)
    slot = (packed.slot + 1).astype(F32)
    full_ref[5 * 128 - 1 : 5 * 128] = slot
    full_ref[6 * 128 - 1 : 6 * 128] = slot
    local = full_ref[...].astype(BF16)
    local_ref[...] = local
    for pair in range(3):
        wide = jnp.concatenate([local[256 * pair : 256 * pair + 128], local[256 * pair + 128 : 256 * pair + 256]], 1)
        made = dot(hits, wide, NT).reshape(owner_count, 2 * capacity, 128).astype(BF16)
        send_ref[:, 2 * capacity * pair : 2 * capacity * pair + 2 * capacity] = made


def last_kernel(
    staying, got_ref, kept_ref, low_ref, pack_ref, sol_ref,
    sol_out, op_out, rhs_out,
    op_ref, out_ref, sem, op_sem,
):
    sol_copy = pltpu.make_async_copy(sol_ref, sol_out, sem.at[0])
    sol_copy.start()
    packed = Packed(pack_ref)
    aggregates = op_ref.shape[0]
    owners, size, count = got_ref.shape
    both = size // 3
    capacity = both // 2
    stay = stay_hits(packed, staying, aggregates)
    ids = got_ref[:, 2 * both : size].astype(F32).reshape(owners * both, count)[:, count - 1 : count]
    shape = (owners * both, 2 * aggregates)
    column = lanes(shape)
    column = jnp.where(column >= aggregates, column - aggregates, column)
    hits = jnp.where(ids == (column + 1).astype(F32), 1.0, 0.0).reshape(owners, both, 2 * aggregates)
    shape = (owners, both, 2 * aggregates)
    upper = lax.broadcasted_iota(jnp.int32, shape, 1) >= capacity
    right = lax.broadcasted_iota(jnp.int32, shape, 2) >= aggregates
    paired = jnp.where(upper == right, hits, 0.0).reshape(owners * both, 2 * aggregates).astype(BF16)
    cut = SPLIT * COARSE
    copies = []
    for pair in (2, 0, 1):
        block = got_ref[:, both * pair : both * pair + both].astype(F32).reshape(owners * both, count).astype(BF16)
        total = dot(paired, block, TN)
        out = []
        for side in range(2):
            at = 128 * (2 * pair + side)
            out.append(total[aggregates * side : aggregates * side + aggregates] + kept_ref[:, at : at + 128])
        first, last = 256 * pair, min(256 * pair + 256, COARSE * COARSE)
        middle = cut if pair == 2 else first + 128
        op_ref[:, first:middle] = out[0][:, : middle - first]
        op_ref[:, middle:last] = out[1][:, : last - middle]
        some = pl.ds(first, last - first)
        copies.append(pltpu.make_async_copy(op_ref.at[:, some], op_out.at[:, some], op_sem.at[pair]))
        copies[-1].start()
        if pair == 2:
            nodes = dot(low_ref[...], stay, NT)
            made = dot_split(packed.table, halves(nodes))
            sums = [made[16 * side : 16 * side + 16] + out[side].T[count - 16 :] for side in range(2)]
            out_ref[0:CUT] = sums[0][0:CUT]
            out_ref[CUT:COARSE] = sums[1][0 : COARSE - CUT]
            copies.append(pltpu.make_async_copy(out_ref, rhs_out, sem.at[1]))
            copies[-1].start()
    for copy in [sol_copy] + copies:
        copy.wait()


def call(kernel, outs, args, spaces, out_spaces=None, scratch=(), flops=0, limit=VMEM_LIMIT, aliases=None):
    bytes_in = sum(a.size * a.dtype.itemsize for a in args)
    bytes_out = sum(o.size * o.dtype.itemsize for o in outs)
    out_spaces = out_spaces or [pltpu.VMEM] * len(outs)
    return pl.pallas_call(
        kernel,
        out_shape=tuple(outs),
        in_specs=[pl.BlockSpec(memory_space=space) for space in spaces],
        out_specs=tuple(pl.BlockSpec(memory_space=space) for space in out_spaces),
        scratch_shapes=list(scratch),
        input_output_aliases=aliases or {},
        compiler_params=pltpu.CompilerParams(vmem_limit_bytes=limit),
        cost_estimate=pl.CostEstimate(
            flops=flops, bytes_accessed=bytes_in + bytes_out, transcendentals=0
        ),
    )(*args)


def struct(shape, dtype):
    return jax.ShapeDtypeStruct(shape, dtype)


def block_table(table, copies, tall):
    out = []
    for part in split_table(table):
        full = np.zeros((copies * tall, copies * table.shape[1]), BF16)
        for copy in range(copies):
            full[
                copy * tall : copy * tall + table.shape[0],
                copy * table.shape[1] : (copy + 1) * table.shape[1],
            ] = part
        out.append(full)
    return np.concatenate(out, 0)


def per_device(start, rhs, diag_block, precond, lift, neighbour, orient, owner, slot):
    count = start.shape[1]
    staying = count // 4
    aggregates = count // 2
    owner_count = lax.axis_size("dom")
    slabs = lax.axis_size("face")
    movers = count - staying
    capacity = 2 * ((movers + owner_count - 2) // (owner_count - 1))
    capacity = ceil_to(capacity, 4)
    chunk = 6 * capacity
    entries = 6 * 128
    owner = owner.reshape(1, count)
    slot = slot.reshape(1, count)
    table = jnp.asarray(block_table(restrict_table(), GROUP, 32))
    pairs = [(i, i ^ 1) for i in range(slabs)]
    others = [(i, (i + 1 if i % 2 else i - 1) % slabs) for i in range(slabs)]

    def exchange(one, other):
        return lax.ppermute(one, "face", pairs), lax.ppermute(other, "face", others)

    args = [diag_block, precond, start, rhs, lift, neighbour, orient, owner, slot, table]
    outs = [struct((96, count), BF16), struct((96, count), BF16), struct((PACKED, count), F32)]
    held = [each for each in args if each is not rhs and each is not start and each is not table]
    to_first, to_second, pack = call(
        lambda *refs: smooth_kernel(staying, owner_count, *refs),
        outs,
        args,
        [pl.ANY] * len(args),
        [pl.ANY] * len(outs),
        scratch=[pltpu.VMEM(each.shape, each.dtype) for each in held + outs]
        + [
            pltpu.SemaphoreType.DMA((7,)),
            pltpu.SemaphoreType.DMA(()),
            pltpu.SemaphoreType.DMA((len(RIM_ROWS),)),
            pltpu.SemaphoreType.DMA((3,)),
        ],
        flops=100_000_000,
        limit=FIRST_LIMIT,
    )
    first, second = exchange(to_first, to_second)
    made, local_op, hits, partial, answer = call(
        lambda *refs: galerkin_kernel(staying, capacity, *refs),
        [
            struct((owner_count, chunk, 128), BF16),
            struct((entries, count), BF16),
            struct((2 * capacity * owner_count, 2 * count), BF16),
            struct((NODES, count), F32),
            struct((NODES, 16, count), F32),
        ],
        [diag_block, precond, pack, table],
        [pltpu.VMEM] * 4,
        scratch=[pltpu.VMEM((entries, count), F32)],
        flops=1_000_000_000,
    )
    sol, resid, rim = call(
        middle_kernel,
        [struct((NODES, count), F32), struct((NODES, count), F32), struct((16, count), F32)],
        [first, second, diag_block, precond, pack, partial, answer],
        [pltpu.VMEM] * 7,
        flops=200_000_000,
    )
    first, second = exchange(rim, rim)
    sol, rest, kept, made = call(
        lambda *refs: rest_kernel(staying, *refs),
        [struct((NODES, count), F32), struct((NODES, count), F32), struct((aggregates, entries), F32), struct(made.shape, BF16)],
        [diag_block, precond, pack, sol, resid, local_op, made, hits],
        [pltpu.VMEM] * 8,
        flops=1_000_000_000,
    )
    low, send = call(
        send_kernel,
        [struct((NODES, count), BF16), struct((owner_count, chunk, 128), BF16)],
        [first, second, rest, pack, hits, made],
        [pltpu.VMEM] * 6,
        flops=50_000_000,
        aliases={5: 1},
    )
    got = lax.all_to_all(send, "dom", split_axis=0, concat_axis=0, tiled=True)
    outs = [
        struct((NODES, count), F32),
        struct((aggregates, COARSE * COARSE), F32),
        struct((COARSE, aggregates), F32),
    ]
    sol, coarse_op, coarse_rhs = call(
        lambda *refs: last_kernel(staying, *refs),
        outs,
        [got, kept, low, pack, sol],
        [pltpu.VMEM] * 5,
        [pl.ANY] * 3,
        scratch=[pltpu.VMEM(each.shape, each.dtype) for each in outs[1:]]
        + [pltpu.SemaphoreType.DMA((2,)), pltpu.SemaphoreType.DMA((3,))],
        flops=100_000_000,
    )
    return (sol, coarse_op.T, coarse_rhs)


def solution(mesh):
    return jax.shard_map(
        per_device,
        mesh=mesh,
        in_specs=(
            P(None, ("dom", "face")),
            P(None, ("dom", "face")),
            P(None, None, ("dom", "face")),
            P(None, None, ("dom", "face")),
            P(),
            P(None, ("dom", "face")),
            P(None, ("dom", "face")),
            P(("dom", "face")),
            P(("dom", "face")),
        ),
        out_specs=(P(None, ("dom", "face")), P(None, ("dom", "face")), P(None, ("dom", "face"))),
        check_vma=False,
    )
```
